32 devices in a mesh: dp: 8 (over z, y), mp: 4 (over x, core).
Axes of the slice: x: 2, y: 2, z: 4, core: 2. Of those that a mesh axis runs over, the one named last changes fastest.
Arguments:
- layer_input: bfloat16 [24, 512, 768], P('dp', 'mp'), may hold values from -6 to 6
- targets: bfloat16 [24, 512, 768], P('dp', 'mp'), may hold values from -6 to 6
- attn_gain: bfloat16 [768], replicated, may hold values from 0.5 to 1.5
- ffn_gain: bfloat16 [768], replicated, may hold values from 0.5 to 1.5
- query_matrix: bfloat16 [768, 768], replicated, may hold values from -0.09375 to 0.09375
- key_matrix: bfloat16 [768, 768], replicated, may hold values from -0.09375 to 0.09375
- value_matrix: bfloat16 [768, 768], replicated, may hold values from -0.21875 to 0.21875
- attention_output_weight: bfloat16 [768, 768], replicated, may hold values from -1.25 to 1.25
- feedforward_input_weight: bfloat16 [768, 3072], replicated, may hold values from -0.21875 to 0.21875
- feedforward_output_weight: bfloat16 [3072, 768], replicated, may hold values from -0.15625 to 0.15625
- bias_table: float32 [32, 12], replicated, may hold values from -4 to 4
- factors: float32 [4, 4, 4], replicated, may hold values from -6 to 6
- down_left: float32 [4, 192], replicated, may hold values from -0.875 to 0.875
- down_right: float32 [4, 12], replicated, may hold values from -0.875 to 0.875
- up_left: float32 [4, 12], replicated, may hold values from -2 to 2
- up_right: float32 [4, 192], replicated, may hold values from -2 to 2
- lengths: int32 [24], P('dp'), may hold values from 48 to 512, as said below
- relative_bucket: int32 [512, 512], replicated, may hold values from 0 to 31, as said below
Outputs:
- loss: float32 [], replicated
- block_out: bfloat16 [24, 512, 768], P('dp', 'mp')
- grad_input: float32 [24, 512, 768], P('dp', 'mp')
- grad_attn_gain: float32 [768], replicated
- grad_ffn_gain: float32 [768], replicated
- grad_bias_table: float32 [32, 12], replicated
- grad_factors: float32 [4, 4, 4], replicated
- grad_down_left: float32 [4, 192], replicated
- grad_down_right: float32 [4, 12], replicated
- grad_up_left: float32 [4, 12], replicated
- grad_up_right: float32 [4, 192], replicated
The draws below stay inside these ranges and needn't reach their ends.
Inputs may be any that keep to these rules, and one draw needn't show every extreme that they name: lengths[b] counts the real tokens of sequence b, which stand at its first positions; some sequence has exactly 512 of them and some exactly 48. relative_bucket[l, m] = label[t5(m - l)], where label is one permutation of 0 to 31 and t5 is T5's bidirectional bucket with max distance 128: with half = 16, exact = 8 and n = |m - l|, t5 = n for n < exact, else exact plus the number of j in 1 to half - exact - 1 with n^(half - exact) >= exact^(half - exact) * (128 / exact)^j; plus half where m > l.
All inputs are finite; a program needn't handle non-finite values.
Results may differ from the reference program's by a relative error of at most 0.02.
The reference program's roundings to bfloat16 on the way count: a program that leaves them out, or rounds other values in their place, can miss the bound.
Values may be sent and summed in bfloat16 or wider, within the bound.
No kernel may reach another device: no remote copies, remote signals or barrier semaphores. Data moves between devices by JAX's collectives and lax.ppermute only.
A program may use at most 128 MiB of HBM per device.

```python
import math
import jax
import jax.numpy as jnp
from jax import lax

D = 768
H = 12
FF = 3072
NB = 32
BOT = 48
KRON = 4
L = 512
SEQ_GRP = 3
BATCH = 24
TOKENS = 12288


def draw_lengths(key, part):
    group_count = BATCH // SEQ_GRP
    order = jnp.arange(BATCH, dtype=jnp.int32)
    group_of = order // SEQ_GRP
    base_class = 3 * (group_count - 1 - group_of) // group_count
    key_class, key_span, key_long, key_short = jax.random.split(key, 4)
    jitter = jax.random.randint(key_class, (BATCH,), -1, 2)
    length_class = jnp.clip(base_class + jitter, 0, 3)
    capacity = jnp.right_shift(jnp.full((BATCH,), L, jnp.int32), length_class)
    lowest = capacity - capacity // 4
    spread = jax.random.randint(key_span, (BATCH,), 0, 1 << 20)
    result = lowest + spread % (capacity - lowest + 1)
    long_at = BATCH - SEQ_GRP + jax.random.randint(key_long, (), 0, SEQ_GRP)
    short_at = jax.random.randint(key_short, (), 0, SEQ_GRP)
    result = jnp.where(order == long_at, L, result)
    result = jnp.where(order == short_at, L // 8 - L // 32, result)
    return result.astype(jnp.int32)


def bucket_edges(half_count, exact_count):
    power = half_count - exact_count
    ratio = 128 // exact_count
    edges = []
    for step in range(1, power):
        needed = exact_count ** power * ratio ** step
        distance = exact_count
        while distance ** power < needed:
            distance = distance + 1
        edges.append(distance)
    return edges


def draw_relative_bucket(key, part):
    half_count = NB // 2
    exact_count = NB // 4
    positions = jnp.arange(L, dtype=jnp.int32)
    relative = positions[None, :] - positions[:, None]
    distance = jnp.abs(relative)
    far_bucket = jnp.full((L, L), exact_count, jnp.int32)
    for edge in bucket_edges(half_count, exact_count):
        far_bucket = far_bucket + (distance >= edge).astype(jnp.int32)
    bucket = jnp.where(distance < exact_count, distance, far_bucket)
    bucket = bucket + jnp.where(relative > 0, half_count, 0).astype(jnp.int32)
    label = jax.random.permutation(jax.random.fold_in(key, 7), NB).astype(jnp.int32)
    onehot = (bucket[:, :, None] == jnp.arange(NB, dtype=jnp.int32)).astype(jnp.int32)
    return jnp.sum(onehot * label[None, None, :], axis=-1).astype(jnp.int32)


def shard_levels(stream_key, extent, pieces, low, top_value):
    def one(dim, shards_of):
        draws = jax.random.uniform(jax.random.fold_in(jax.random.fold_in(stream_key, 6), dim), (shards_of,), jnp.float32, low / len(pieces), top_value / len(pieces))
        return jnp.repeat(jnp.exp(draws), extent[dim] // shards_of).reshape((-1,) + (1,) * (len(extent) - dim - 1))

    gain = one(*pieces[0])
    for cut in pieces[1:]:
        gain = gain * one(*cut)
    return gain


def noise(key, shape, scale, bound, cuts=(), held_as=jnp.bfloat16):
    gain = shard_levels(key, shape, cuts, -0.22, 0.18) if cuts else 1.0
    drawn = jax.random.normal(key, shape, jnp.float32) * scale * gain
    return jnp.minimum(jnp.maximum(drawn, -bound), bound).astype(held_as)


def setup_inputs(seed: int = 0) -> dict:
    seeds = jax.random.split(jax.random.key(seed), 19)
    layer_input = noise(seeds[0], (BATCH, L, D), 1.0, 6.0, ((0, 8), (1, 4)))
    targets = noise(seeds[1], (BATCH, L, D), 1.0, 6.0, ((0, 8), (1, 4)))
    attn_gain = jnp.clip(1.0 + 0.1 * jax.random.normal(seeds[2], (D,), jnp.float32), 0.5, 1.5).astype(jnp.bfloat16)
    ffn_gain = jnp.clip(1.0 + 0.1 * jax.random.normal(seeds[3], (D,), jnp.float32), 0.5, 1.5).astype(jnp.bfloat16)
    query_matrix = noise(seeds[4], (D, D), (5 * D) ** -0.5, 0.09375)
    key_matrix = noise(seeds[5], (D, D), (5 * D) ** -0.5, 0.09375)
    value_matrix = noise(seeds[6], (D, D), D ** -0.5, 0.21875)
    attention_output_weight = noise(seeds[7], (D, D), (D // 32) ** -0.5, 1.25)
    feedforward_input_weight = noise(seeds[8], (D, FF), D ** -0.5, 0.21875)
    feedforward_output_weight = noise(seeds[9], (FF, D), (FF // 2) ** -0.5, 0.15625)
    bias_table = noise(seeds[10], (NB, H), 1.0, 4.0, (), jnp.float32)
    factors = noise(seeds[11], (KRON, KRON, KRON), 1.0, 6.0, (), jnp.float32)
    down_left = noise(seeds[12], (KRON, D // KRON), 0.15, 0.875, (), jnp.float32)
    down_right = noise(seeds[13], (KRON, BOT // KRON), 0.15, 0.875, (), jnp.float32)
    up_left = noise(seeds[14], (KRON, BOT // KRON), 0.35, 2.0, (), jnp.float32)
    up_right = noise(seeds[15], (KRON, D // KRON), 0.35, 2.0, (), jnp.float32)
    lengths = draw_lengths(jax.random.fold_in(seeds[18], 71), 0)
    relative_bucket = draw_relative_bucket(jax.random.fold_in(seeds[18], 71), 0)
    return dict(layer_input=layer_input, targets=targets, attn_gain=attn_gain, ffn_gain=ffn_gain, query_matrix=query_matrix, key_matrix=key_matrix, value_matrix=value_matrix, attention_output_weight=attention_output_weight, feedforward_input_weight=feedforward_input_weight, feedforward_output_weight=feedforward_output_weight, bias_table=bias_table, factors=factors, down_left=down_left, down_right=down_right, up_left=up_left, up_right=up_right, lengths=lengths, relative_bucket=relative_bucket)


EPSILON = 1e-06
MATMUL_ACCURACY = lax.Precision.HIGHEST

@jax.custom_vjp
def low(v):
    return lax.optimization_barrier(v.astype(jnp.bfloat16)).astype(jnp.float32)

@jax.custom_vjp
def low_back(v):
    return v

def low_keep(v):
    return (low(v), None)

def low_pass(kept, grad):
    return (grad,)

def back_keep(v):
    return (v, None)

def back_low(kept, grad):
    return (low(grad),)
low.defvjp(low_keep, low_pass)
low_back.defvjp(back_keep, back_low)

def rms_scale(values):
    return lax.rsqrt(lax.optimization_barrier(jnp.mean(values * values, axis=-1, keepdims=True)) + EPSILON)

def build_mats(factors, down_left, down_right, up_left, up_right):
    kron_size = factors.shape[0]
    model_width = kron_size * down_left.shape[1]
    bottleneck = kron_size * down_right.shape[1]
    down_mat = jnp.einsum('iac,ib,id->abcd', factors, down_left, down_right, precision=MATMUL_ACCURACY).reshape(model_width, bottleneck)
    up_mat = jnp.einsum('ica,id,ib->cdab', factors, up_left, up_right, precision=MATMUL_ACCURACY).reshape(bottleneck, model_width)
    return (down_mat, up_mat)

def layer_block(seq_in, seq_len, gain_one, gain_two, bias_heads, down_lowered, up_lowered, frozen):
    w_query, w_key, w_value, w_out, w_in, w_back = frozen
    group_size, seq_length, model_width = seq_in.shape
    head_count = bias_heads.shape[0]
    head_dim = model_width // head_count
    first_normed_input = low(seq_in * rms_scale(seq_in) * gain_one)

    def project(weight):
        return low(low_back(jnp.einsum('gld,de->gle', first_normed_input, weight, precision=MATMUL_ACCURACY)))
    query_all = project(w_query).reshape(group_size, seq_length, head_count, head_dim)
    key_all = project(w_key).reshape(group_size, seq_length, head_count, head_dim)
    value_all = project(w_value).reshape(group_size, seq_length, head_count, head_dim)
    scores = low_back(jnp.einsum('glhe,gmhe->ghlm', query_all, key_all, precision=MATMUL_ACCURACY) + bias_heads[None])
    positions = jnp.arange(seq_length, dtype=jnp.int32)
    key_valid = (positions[None, :] < seq_len[:, None])[:, None, None, :]
    top_score = lax.optimization_barrier(jnp.max(jnp.where(key_valid, scores, -jnp.inf), axis=-1, keepdims=True))
    exp_total = lax.optimization_barrier(jnp.sum(jnp.where(key_valid, jnp.exp(scores - top_score), 0.0), axis=-1, keepdims=True))
    log_norm = top_score + jnp.log(exp_total)
    probs = low(jnp.where(key_valid, jnp.exp(scores - log_norm), 0.0))
    context = jnp.einsum('ghlm,gmhe->glhe', probs, value_all, precision=MATMUL_ACCURACY).reshape(group_size, seq_length, model_width)
    context = low(low_back(context))
    residual = seq_in + low_back(jnp.einsum('gle,ed->gld', context, w_out, precision=MATMUL_ACCURACY))
    second_normed_input = low(residual * rms_scale(residual) * gain_two)
    hidden_state = low(jax.nn.gelu(low_back(jnp.einsum('gld,df->glf', second_normed_input, w_in, precision=MATMUL_ACCURACY)), approximate=True))
    feedforward_output = low(low_back(jnp.einsum('glf,fd->gld', hidden_state, w_back, precision=MATMUL_ACCURACY)))
    compressed_hidden = low_back(jnp.einsum('ebj,jm->ebm', feedforward_output, down_lowered, precision=MATMUL_ACCURACY))
    activated_hidden = low(jax.nn.gelu(compressed_hidden, approximate=True))
    adapter_result = low_back(jnp.einsum('afm,mj->afj', activated_hidden, up_lowered, precision=MATMUL_ACCURACY))
    return residual + feedforward_output + adapter_result

def reference(layer_input, targets, attn_gain, ffn_gain, query_matrix, key_matrix, value_matrix, attention_output_weight, feedforward_input_weight, feedforward_output_weight, bias_table, factors, down_left, down_right, up_left, up_right, lengths, relative_bucket):
    frozen = tuple((weight.astype(jnp.float32) for weight in (query_matrix, key_matrix, value_matrix, attention_output_weight, feedforward_input_weight, feedforward_output_weight)))
    group_size = math.gcd(BATCH, max(1, 2048 // L))
    length_blocks = lengths.reshape(BATCH // group_size, group_size)

    def forward(inputs, gain_one, gain_two, table, fac, dleft, dright, uleft, uright):
        down_mat, up_mat = build_mats(fac, dleft, dright, uleft, uright)
        down_lowered = low(down_mat)
        up_lowered = low(up_mat)
        bias_heads = jnp.transpose(table[relative_bucket], (2, 0, 1))

        def per_group(inputs_pair):
            seq_in, seq_len = inputs_pair
            return layer_block(seq_in, seq_len, gain_one, gain_two, bias_heads, down_lowered, up_lowered, frozen)
        blocks = (inputs.reshape(BATCH // group_size, group_size, L, D), length_blocks)
        return lax.map(jax.checkpoint(per_group), blocks).reshape(BATCH, L, D)
    final, pullback = jax.vjp(forward, layer_input.astype(jnp.float32), attn_gain.astype(jnp.float32), ffn_gain.astype(jnp.float32), bias_table, factors, down_left, down_right, up_left, up_right)
    positions = jnp.arange(L, dtype=jnp.int32)
    tok_valid = positions[None, :] < lengths[:, None]
    error_signal = jnp.where(tok_valid[:, :, None], final - targets.astype(jnp.float32), 0.0)
    grads = pullback(error_signal)
    count = jnp.sum(lengths.astype(jnp.float32))
    scale = TOKENS / count
    params = (factors, down_left, down_right, up_left, up_right)
    penalty = 0.5 * BATCH * sum((jnp.sum(param * param) for param in params))
    loss = (scale * 0.5 * jnp.sum(error_signal * error_signal) + penalty) / (TOKENS * D)
    return (loss, final.astype(jnp.bfloat16), scale * grads[0], scale * grads[1], scale * grads[2], scale * grads[3], scale * grads[4] + BATCH * factors, scale * grads[5] + BATCH * down_left, scale * grads[6] + BATCH * down_right, scale * grads[7] + BATCH * up_left, scale * grads[8] + BATCH * up_right)
```

```python
import functools

import jax
import jax.numpy as jnp
from jax import lax
from jax.experimental import pallas as pl
from jax.experimental.pallas import tpu as pltpu
from jax.sharding import PartitionSpec as P

EPSILON = 1e-06
F32 = jnp.float32
BF16 = jnp.bfloat16
EXACT = lax.Precision.HIGHEST
GELU_A = 0.7978845608028654
GELU_B = 0.044715
LANES = 128


def dot(a, b, ca=1, cb=0, precision=None):
    return lax.dot_general(
        a, b, (((ca,), (cb,)), ((), ())), preferred_element_type=F32, precision=precision
    )


def iota(shape, dim):
    return lax.broadcasted_iota(jnp.int32, shape, dim)


def rms(values):
    return lax.rsqrt(jnp.mean(values * values, axis=-1, keepdims=True) + EPSILON)


def gelu_pair(v):
    square = v * v
    t = jnp.tanh(v * (GELU_A + (GELU_A * GELU_B) * square))
    half = 0.5 * v
    value = half * (1.0 + t)
    slope = 0.5 * (1.0 + t) + half * (1.0 - t * t) * (
        GELU_A + (3.0 * GELU_A * GELU_B) * square
    )
    return value, slope


def hot(left, right):
    return (left == right).astype(F32)


def factor_rows(fac_ref, transposed):
    kron = fac_ref.shape[0]
    pieces = [fac_ref[i].T if transposed else fac_ref[i] for i in range(kron)]
    return jnp.concatenate(pieces, axis=0)


class Kron:
    def __init__(self, fac_ref, transposed, left_ref, right_ref):
        kron = left_ref.shape[0]
        self.block = left_ref.shape[1]
        self.inner = right_ref.shape[1]
        self.kron = kron
        width = kron * self.block
        rows = kron * kron
        inner = self.inner
        self.expand = hot(iota((rows, kron), 0) // kron, iota((rows, kron), 1))
        take_c = hot(iota((kron, LANES), 0), iota((kron, LANES), 1) // inner)
        lane_d = iota((inner, LANES), 1)
        take_d = jnp.where(
            lane_d < kron * inner, hot(iota((inner, LANES), 0), lane_d % inner), 0.0
        )
        self.same_a = hot(iota((rows, width), 0) % kron, iota((rows, width), 1) // self.block)
        wide_left = jnp.concatenate([left_ref[...]] * kron, axis=1)
        self.left = dot(self.expand, wide_left, precision=EXACT) * self.same_a
        self.fac = dot(factor_rows(fac_ref, transposed), take_c, precision=EXACT)
        self.right = dot(
            self.expand, dot(right_ref[...], take_d, precision=EXACT), precision=EXACT
        )

    def matrix(self):
        return dot(self.left, self.fac * self.right, 0, 0, precision=EXACT)


class KronBack:
    def __init__(self, kron, block, inner, left, fac, right):
        self.kron, self.block, self.inner = kron, block, inner
        self.left, self.fac, self.right = left, fac, right

    def place(self, of_lane, start):
        lane_in = iota((LANES, LANES), 0)
        keep = (lane_in < self.kron * self.inner) & (iota((LANES, LANES), 1) - start == of_lane(lane_in))
        return keep.astype(BF16)

    def back(self, grad, fac_at, right_at):
        grad = grad.astype(BF16)
        rows = self.kron * self.kron
        width = self.kron * self.block
        inner = dot(self.left.astype(BF16), grad)
        g_fac = dot((inner * self.right).astype(BF16), self.place(lambda n: n // self.inner, fac_at))
        expand = (iota((rows, self.kron), 0) // self.kron == iota((rows, self.kron), 1)).astype(BF16)
        same_i = dot(expand, (inner * self.fac).astype(BF16), 0, 0)
        g_right = dot(same_i.astype(BF16), self.place(lambda n: n % self.inner, right_at))
        outer = dot((self.fac * self.right).astype(BF16), grad, 1, 1)
        outer = outer * hot(iota((rows, width), 0) % self.kron, iota((rows, width), 1) // self.block)
        outer = dot(expand, outer.astype(BF16), 0, 0)
        g_left = sum(outer[:, n * self.block : (n + 1) * self.block] for n in range(self.kron))
        return g_fac, g_right, g_left


def prep_kernel(fac_ref, dl_ref, dr_ref, ul_ref, ur_ref, low_ref, left_ref, fac_out, right_out):
    down = Kron(fac_ref, False, dl_ref, dr_ref)
    up = Kron(fac_ref, True, ur_ref, ul_ref)
    for n, one in enumerate((down, up)):
        low_ref[n] = one.matrix().astype(BF16)
        left_ref[n] = one.left
        fac_out[n] = one.fac
        right_out[n] = one.right


def main_kernel(
    lengths_ref,
    x_ref,
    wf_ref,
    cx_ref,
    m1_ref,
    mf_ref,
    mc_ref,
    t_ref,
    tf_ref,
    gain1_ref,
    gain2_ref,
    table_ref,
    low_ref,
    left_ref,
    fac_ref,
    right_ref,
    bucket_hbm,
    wq_hbm,
    wk_hbm,
    wv_hbm,
    wo_hbm,
    win_hbm,
    wout_hbm,
    blk_ref,
    gres_ref,
    gw_own_ref,
    gc_own_ref,
    send_ref,
    small_ref,
    wq,
    wk,
    wv,
    wo,
    win,
    wout,
    edge_s,
    rows_s,
    xn_s,
    q_s,
    k_s,
    v_s,
    bias_s,
    pack_s,
    pw_s,
    pc_s,
    ctx_s,
    inv_s,
    res_s,
    hid_s,
    slope_s,
    ffn_s,
    err_s,
    do_s,
    dq_s,
    dkt_s,
    dvt_s,
    sems,
):
    mp = lax.axis_index("mp")
    w_idx = jnp.where(mp < 2, 0, 2)
    blk = x_ref.shape[1]
    width = x_ref.shape[2]
    heads = table_ref.shape[0]
    pairs = heads // 2
    seq = 4 * blk
    ffw = win.shape[1]

    edges = []
    for n, row in enumerate((0, seq - 8)):
        edge = pltpu.make_async_copy(bucket_hbm.at[row : row + 8], edge_s.at[n], sems.at[6 + n])
        edge.start()
        edges.append(edge)
    copies = []
    for n, (src, dst) in enumerate(
        ((wk_hbm, wk), (wv_hbm, wv), (wq_hbm, wq), (wo_hbm, wo), (win_hbm, win), (wout_hbm, wout))
    ):
        copy = pltpu.make_async_copy(src, dst, sems.at[n])
        copy.start()
        copies.append(copy)

    slot_pos = (mp, mp ^ 2, mp ^ 1, mp ^ 3)

    rows_s[0:blk] = x_ref[w_idx]
    rows_s[blk : 2 * blk] = wf_ref[...]
    rows_s[2 * blk : 3 * blk] = m1_ref[w_idx]
    rows_s[3 * blk : 4 * blk] = mf_ref[...]
    rows_s[4 * blk : 5 * blk] = x_ref[1]
    rows_s[5 * blk : 6 * blk] = cx_ref[...]
    rows_s[6 * blk : 7 * blk] = m1_ref[1]
    rows_s[7 * blk : 8 * blk] = mc_ref[...]

    gain1 = gain1_ref[...].astype(F32).reshape(1, width)
    gain2 = gain2_ref[...].astype(F32).reshape(1, width)

    for n in range(8):
        values = rows_s[n * blk : (n + 1) * blk].astype(F32)
        xn_s[n * blk : (n + 1) * blk] = (values * rms(values) * gain1).astype(BF16)

    span = 2 * seq
    for edge in edges:
        edge.wait()
    by_lane = jnp.concatenate(
        [pltpu.roll(edge_s[1, 7:8, :], 1, 1), edge_s[0, 0:1, :]], axis=1
    )
    buckets = hot(iota((table_ref.shape[1], span), 0), by_lane)
    by_distance = dot(table_ref[...], buckets, precision=EXACT)
    for h in range(heads):
        bias_s[h] = pltpu.roll(
            jnp.broadcast_to(by_distance[h : h + 1], (blk, span)),
            span - blk,
            1,
            stride=1,
            stride_axis=0,
        )
    for c in copies[:3]:
        c.wait()
    for n in range(4):
        piece = xn_s[2 * n * blk : 2 * (n + 1) * blk]
        k_s[2 * n * blk : 2 * (n + 1) * blk] = dot(piece, wk[...]).astype(BF16)
        v_s[2 * n * blk : 2 * (n + 1) * blk] = dot(piece, wv[...]).astype(BF16)
    q_s[0 : 2 * blk] = dot(xn_s[0 : 2 * blk], wq[...]).astype(BF16)
    q_s[2 * blk : 3 * blk] = dot(xn_s[4 * blk : 5 * blk], wq[...]).astype(BF16)

    low_half = iota((blk, LANES), 1) < LANES // 2
    len_w = lengths_ref[w_idx]
    len_c = lengths_ref[1]
    key_lane = iota((1, blk), 1)

    def masks(length):
        return [
            jnp.where(slot_pos[s] * blk + key_lane < length, 0.0, -jnp.inf).astype(F32)
            for s in range(4)
        ]

    def offset(s, q_pos):
        return pl.multiple_of((slot_pos[s] - q_pos + 3) * blk, blk)

    groups = (
        (0, (mp, mp ^ 2), 0, masks(len_w), pw_s),
        (2 * blk, (mp,), seq, masks(len_c), pc_s),
    )

    def by_head(rows):
        half = iota(rows.shape, 1) < LANES // 2
        zero = jnp.zeros_like(rows)
        return jnp.concatenate([jnp.where(half, rows, zero), jnp.where(half, zero, rows)], axis=0)

    def forward(hp, group):
        q_row, q_poss, k_row, mask, p_ref = group
        count = len(q_poss)
        cols = slice(hp * LANES, (hp + 1) * LANES)
        all_rows = slice(q_row, q_row + count * blk)
        scores = dot(by_head(q_s[all_rows, cols]), k_s[k_row : k_row + seq, cols], 1, 1)
        invs = []
        for u in range(2 * count):
            h, b = divmod(u, count)
            rows = slice(u * blk, (u + 1) * blk)
            parts = [
                scores[rows, n * blk : (n + 1) * blk]
                + (bias_s[2 * hp + h, :, pl.ds(offset(n, q_poss[b]), blk)] + mask[n])
                for n in range(4)
            ]
            top = jnp.max(
                jnp.maximum(jnp.maximum(parts[0], parts[1]), jnp.maximum(parts[2], parts[3])),
                axis=-1,
                keepdims=True,
            )
            parts = [jnp.exp(part - top) for part in parts]
            total = jnp.sum(
                (parts[0] + parts[1]) + (parts[2] + parts[3]), axis=-1, keepdims=True
            )
            invs.append(1.0 / total)
            for n in range(4):
                p_ref[hp, rows, n * blk : (n + 1) * blk] = parts[n].astype(BF16)
        out = dot(p_ref[hp], v_s[k_row : k_row + seq, cols])
        for b in range(count):
            rows = slice(q_row + b * blk, q_row + (b + 1) * blk)
            inv = jnp.where(low_half, invs[b], invs[count + b])
            inv_s[rows, cols] = inv
            mixed = jnp.where(
                low_half,
                out[b * blk : (b + 1) * blk],
                out[(count + b) * blk : (count + b + 1) * blk],
            )
            ctx_s[rows, cols] = (mixed * inv).astype(BF16)

    for hp in range(pairs):
        for group in groups:
            forward(hp, group)

    acc_s = bias_s
    acc_s[...] = jnp.zeros_like(acc_s)

    tokens = 3 * blk
    own = jnp.concatenate([rows_s[0 : 2 * blk], rows_s[4 * blk : 5 * blk]], axis=0).astype(F32)
    copies[3].wait()
    residual = own + dot(ctx_s[...], wo[...])
    res_s[...] = residual
    inv2 = rms(residual)
    yn = (residual * inv2 * gain2).astype(BF16)
    xn_s[0:tokens] = yn
    copies[4].wait()
    chunk = 512

    @pl.loop(0, ffw // chunk)
    def _(n):
        cols = pl.ds(pl.multiple_of(n * chunk, chunk), chunk)
        value, slope = gelu_pair(dot(xn_s[0:tokens], win[:, cols]))
        hid_s[:, cols] = value.astype(BF16)
        slope_s[:, cols] = slope.astype(BF16)

    copies[5].wait()
    for n in range(width // 256):
        cols = slice(n * 256, (n + 1) * 256)
        ffn_s[:, cols] = dot(hid_s[...], wout[:, cols]).astype(BF16)

    down_low = low_ref[0]
    up_low = low_ref[1]
    ffn = ffn_s[...]
    activated, act_slope = gelu_pair(dot(ffn, down_low))
    activated = activated.astype(BF16)
    final = res_s[...] + ffn.astype(F32) + dot(activated, up_low, 1, 1)
    blk_ref[...] = final.astype(BF16)

    row = iota((blk, 1), 0)
    valid = jnp.concatenate(
        [mp * blk + row < len_w, (mp ^ 2) * blk + row < len_w, mp * blk + row < len_c], axis=0
    )
    goal = jnp.concatenate([t_ref[w_idx], tf_ref[...], t_ref[1]], axis=0).astype(F32)
    err = jnp.where(valid, final - goal, 0.0)
    err_s[...] = err
    loss = 0.5 * jnp.sum(jnp.sum(err * err, axis=0, keepdims=True), axis=1, keepdims=True)
    g_adapter = err.astype(BF16)
    grad_up = dot(g_adapter, activated, 0, 0)
    g_squeezed = (dot(g_adapter, up_low) * act_slope).astype(BF16)
    grad_down = dot(ffn, g_squeezed, 0, 0)
    block = width // 4
    inner = 12
    backs = [
        KronBack(4, block, inner, left_ref[n], fac_ref[n], right_ref[n]).back(
            grad, *PACK_KRON[n]
        )
        for n, grad in enumerate((grad_down, grad_up))
    ]
    g_ffn = (err + dot(g_squeezed, down_low, 1, 1)).astype(BF16)
    ffn_s[...] = g_ffn

    @pl.loop(0, ffw // chunk)
    def _(n):
        cols = pl.ds(pl.multiple_of(n * chunk, chunk), chunk)
        hid_s[:, cols] = (dot(ffn_s[...], wout[cols, :], 1, 1) * slope_s[:, cols].astype(F32)).astype(
            BF16
        )

    parts = []
    for n in range(width // 256):
        parts.append(dot(hid_s[...], win[n * 256 : (n + 1) * 256, :], 1, 1))
    g_normed = jnp.concatenate(parts, axis=1)
    residual = res_s[...]
    inv2 = rms(residual)
    g2 = jnp.sum(g_normed * residual * inv2, axis=0, keepdims=True)
    weighted = g_normed * gain2
    inner = jnp.mean(weighted * residual, axis=-1, keepdims=True)
    g_res = err_s[...] + inv2 * weighted - residual * (inv2 * inv2 * inv2 * inner)
    gres_ref[...] = g_res
    g_ctx = dot(g_res.astype(BF16), wo[...], 1, 1).astype(BF16)
    do_s[...] = g_ctx

    def backward(hp, group):
        q_row, q_poss, k_row, mask, p_ref = group
        count = len(q_poss)
        cols = slice(hp * LANES, (hp + 1) * LANES)
        all_rows = slice(q_row, q_row + count * blk)
        kp = k_s[k_row : k_row + seq, cols]
        do = by_head(do_s[all_rows, cols].astype(F32) * inv_s[all_rows, cols])
        ctx = ctx_s[all_rows, cols].astype(F32)
        delta = jnp.sum(do * jnp.concatenate([ctx, ctx], axis=0), axis=-1, keepdims=True)
        do = do.astype(BF16)
        dp = dot(do, v_s[k_row : k_row + seq, cols], 1, 1)
        ds = p_ref[hp].astype(F32) * (dp - delta)
        low = ds.astype(BF16)
        dq = dot(low, kp)
        for b in range(count):
            rows = slice(q_row + b * blk, q_row + (b + 1) * blk)
            dq_s[rows, cols] = jnp.where(
                low_half,
                dq[b * blk : (b + 1) * blk],
                dq[(count + b) * blk : (count + b + 1) * blk],
            ).astype(BF16)
        dkt_s[cols, k_row : k_row + seq] = dot(by_head(q_s[all_rows, cols]), low, 0, 0).astype(BF16)
        dvt_s[cols, k_row : k_row + seq] = dot(do, p_ref[hp], 0, 0).astype(BF16)
        return ds

    for hp in range(pairs):
        ds_w = backward(hp, groups[0])
        ds_c = backward(hp, groups[1])
        for h in range(2):
            near = ds_w[2 * h * blk : (2 * h + 1) * blk] + ds_c[h * blk : (h + 1) * blk]
            far = ds_w[(2 * h + 1) * blk : (2 * h + 2) * blk]
            for piece, q_pos in ((near, mp), (far, mp ^ 2)):
                for n in range(4):
                    place = pl.ds(offset(n, q_pos), blk)
                    acc_s[2 * hp + h, :, place] += piece[:, n * blk : (n + 1) * blk]

    def back_rows(start):
        part = dot(dkt_s[:, start : start + 2 * blk], wk[...], 0, 1)
        return part + dot(dvt_s[:, start : start + 2 * blk], wv[...], 0, 1)

    def gain_part(part, start):
        values = rows_s[start : start + part.shape[0]].astype(F32)
        return jnp.sum(part * values * rms(values), axis=0, keepdims=True)

    part = back_rows(0) + dot(dq_s[0 : 2 * blk], wq[...], 1, 1)
    g1 = gain_part(part, 0)
    gw_own_ref[...] = part
    part = back_rows(2 * blk)
    g1 = g1 + gain_part(part, 2 * blk)
    send_ref[0 : 2 * blk] = part.astype(BF16)
    part = back_rows(4 * blk)
    extra = dot(dq_s[2 * blk : 3 * blk], wq[...], 1, 1)
    part = jnp.concatenate([part[0:blk] + extra, part[blk : 2 * blk]], axis=0)
    g1 = g1 + gain_part(part, 4 * blk)
    gc_own_ref[...] = part
    part = back_rows(6 * blk)
    g1 = g1 + gain_part(part, 6 * blk)
    send_ref[2 * blk : 4 * blk] = part.astype(BF16)

    sub = iota((8, span), 0)
    sums = []
    for h in range(heads):
        total = jnp.zeros((8, span), F32)
        for g in range(blk // 8):
            total = total + pltpu.roll(acc_s[h, 8 * g : 8 * g + 8, :], (blk - 8 * g) % span, 1)
        for bit in (1, 2, 4):
            total = jnp.where((sub & bit) > 0, pltpu.roll(total, span - bit, 1), total)
        sums.append(jnp.sum(total, axis=0, keepdims=True))
    g_table = dot(jnp.concatenate(sums, axis=0), buckets, 1, 1, precision=EXACT)

    (gf_d, g_dr, g_dl), (gf_u, g_ul, g_ur) = backs
    half = LANES // 2
    row16 = iota((16, LANES), 0)
    lane16 = iota((16, LANES), 1)
    top = gf_d + gf_u
    pack_s[0:16] = top
    pack_s[0:4] += g_dr + g_ul
    pack_s[0:heads, 0 : table_ref.shape[1]] = g_table
    pack_s[0:4, half:LANES] = g_dl[:, 0:half]
    pack_s[4:8, half:LANES] = g_dl[:, half : 2 * half]
    pack_s[8:12, half:LANES] = g_dl[:, 2 * half : 3 * half]
    pack_s[12:16, half:LANES] = g_ur[:, 0:half]
    pack_s[16:20] = g_ur[:, half : 3 * half]
    for n in range(width // LANES):
        pack_s[20 + n : 21 + n] = g1[:, n * LANES : (n + 1) * LANES]
        pack_s[26 + n : 27 + n] = g2[:, n * LANES : (n + 1) * LANES]
    real = (lengths_ref[0] + lengths_ref[1] + lengths_ref[2]).astype(F32)
    sums = jnp.where(lane16 < 2, loss, real)
    high = sums.astype(BF16).astype(F32)
    sums = jnp.where(lane16 % 2 == 0, high, sums - high)
    packed = jnp.where((row16 == 15) & (lane16 < 4), sums, pack_s[0:16]).astype(BF16)
    rest = pack_s[16:32].astype(BF16)
    for n in range(small_ref.shape[0]):
        small_ref[n, 0:16] = packed
        small_ref[n, 16:32] = rest


PACK_KRON = ((32, 40), (36, 52))


def norm_back_rows(grad, values, gain):
    inv = rms(values)
    weighted = grad * gain
    inner = jnp.mean(weighted * values, axis=-1, keepdims=True)
    return inv * weighted - values * (inv * inv * inv * inner)


def mid_kernel(x_ref, wf_ref, gain1_ref, gw_ref, gc_ref, recv_ref, gres_ref, w_out, away_ref):
    blk = x_ref.shape[1]
    w_idx = jnp.where(lax.axis_index("mp") < 2, 0, 2)
    gain1 = gain1_ref[...].astype(F32).reshape(1, x_ref.shape[2])
    away_ref[1] = (gc_ref[blk : 2 * blk] + recv_ref[3 * blk : 4 * blk].astype(F32)).astype(BF16)
    grad = gw_ref[blk : 2 * blk] + recv_ref[blk : 2 * blk].astype(F32)
    back = norm_back_rows(grad, wf_ref[...].astype(F32), gain1)
    away_ref[0] = (gres_ref[blk : 2 * blk] + back).astype(BF16)
    grad = gw_ref[0:blk] + recv_ref[0:blk].astype(F32)
    back = norm_back_rows(grad, x_ref[w_idx].astype(F32), gain1)
    w_out[...] = gres_ref[0:blk] + back


def last_kernel(
    token_total,
    seq_total,
    x_ref,
    gain1_ref,
    gc_ref,
    recv_ref,
    gres_ref,
    back_ref,
    w_grad_ref,
    blk_ref,
    blk_f_ref,
    gathered_ref,
    fac_ref,
    dl_ref,
    dr_ref,
    ul_ref,
    ur_ref,
    loss_ref,
    out_ref,
    grad_ref,
    g1_ref,
    g2_ref,
    gt_ref,
    gfac_ref,
    gdl_ref,
    gdr_ref,
    gul_ref,
    gur_ref,
):
    blk = x_ref.shape[1]
    width = x_ref.shape[2]
    w_idx = jnp.where(lax.axis_index("mp") < 2, 0, 2)
    f_idx = 2 - w_idx
    total = gathered_ref[0].astype(F32)
    for n in range(1, gathered_ref.shape[0]):
        total = total + gathered_ref[n].astype(F32)
    half = LANES // 2
    tail = total[15:16, 0:4]
    count = (tail[:, 2:3] + tail[:, 3:4]) * 0.25
    scale = token_total / count
    params = [dl_ref, dr_ref, ul_ref, ur_ref]
    squares = [jnp.sum(fac_ref[n] * fac_ref[n], keepdims=True) for n in range(fac_ref.shape[0])]
    squares += [jnp.sum(p[...] * p[...], keepdims=True) for p in params]
    penalty = 0.5 * seq_total * sum(squares)
    loss_ref[...] = (scale * (tail[:, 0:1] + tail[:, 1:2]) + penalty) / (token_total * width)

    grad_ref[f_idx] = scale * back_ref[0].astype(F32)
    grad_ref[w_idx] = scale * w_grad_ref[...]
    grad = gc_ref[0:blk] + recv_ref[2 * blk : 3 * blk].astype(F32) + back_ref[1].astype(F32)
    gain1 = gain1_ref[...].astype(F32).reshape(1, width)
    back = norm_back_rows(grad, x_ref[1].astype(F32), gain1)
    grad_ref[1] = scale * (gres_ref[2 * blk : 3 * blk] + back)
    out_ref[w_idx] = blk_ref[0:blk]
    out_ref[f_idx] = blk_f_ref[...]
    out_ref[1] = blk_ref[2 * blk : 3 * blk]

    heads, buckets = gt_ref.shape
    gt_ref[...] = scale * total[0:heads, 0:buckets]
    kron = fac_ref.shape[0]
    for i in range(kron):
        rows = slice(i * kron, (i + 1) * kron)
        gfac_ref[i] = (
            scale * (total[rows, 32 : 32 + kron] + total[rows, 36 : 36 + kron].T)
            + seq_total * fac_ref[i]
        )
    gdr_ref[...] = scale * total[0:4, 40:52] + seq_total * dr_ref[...]
    gul_ref[...] = scale * total[0:4, 52:64] + seq_total * ul_ref[...]
    g_dl = jnp.concatenate([total[4 * n : 4 * n + 4, half:LANES] for n in range(3)], axis=1)
    gdl_ref[...] = scale * g_dl + seq_total * dl_ref[...]
    g_ur = jnp.concatenate([total[12:16, half:LANES], total[16:20]], axis=1)
    gur_ref[...] = scale * g_ur + seq_total * ur_ref[...]
    for n in range(width // LANES):
        g1_ref[n : n + 1] = scale * total[20 + n : 21 + n]
        g2_ref[n : n + 1] = scale * total[26 + n : 27 + n]


VMEM = pl.BlockSpec(memory_space=pltpu.VMEM)
SMEM = pl.BlockSpec(memory_space=pltpu.SMEM)
ANY = pl.BlockSpec(memory_space=pl.ANY)


def local(
    layer_input,
    targets,
    attn_gain,
    ffn_gain,
    query_matrix,
    key_matrix,
    value_matrix,
    attention_output_weight,
    feedforward_input_weight,
    feedforward_output_weight,
    bias_table,
    factors,
    down_left,
    down_right,
    up_left,
    up_right,
    lengths,
    relative_bucket,
):
    seqs, blk, width = layer_input.shape
    mp_size = lax.axis_size("mp")
    mp = lax.axis_index("mp")
    axes = ("dp", "mp")
    devices = lax.axis_size("dp") * mp_size
    heads = bias_table.shape[1]
    ffw = feedforward_input_weight.shape[1]
    kron = factors.shape[0]
    seq_total = lax.axis_size("dp") * seqs
    token_total = seq_total * blk * mp_size
    assert seqs == 3 and mp_size == 4
    core = [(i, i ^ 1) for i in range(mp_size)]
    chip = [(i, i ^ 2) for i in range(mp_size)]

    f_idx = jnp.where(mp < 2, 2, 0).astype(jnp.int32)
    wf = lax.ppermute(lax.dynamic_index_in_dim(layer_input, f_idx, 0, False), "mp", chip)
    cx = lax.ppermute(layer_input[1], "mp", chip)
    tf = lax.ppermute(lax.dynamic_index_in_dim(targets, f_idx, 0, False), "mp", chip)
    m1 = lax.ppermute(layer_input, "mp", core)
    mf = lax.ppermute(wf, "mp", core)
    mc = lax.ppermute(cx, "mp", core)
    span = 2 * blk * mp_size
    table_t = bias_table.T

    sds = jax.ShapeDtypeStruct
    rows3 = 3 * blk
    small_params = pltpu.CompilerParams(vmem_limit_bytes=24 * 2**20)
    low, lefts, facs, rights = pl.pallas_call(
        prep_kernel,
        out_shape=[
            sds((2, width, LANES), BF16),
            sds((2, kron * kron, width), F32),
            sds((2, kron * kron, LANES), F32),
            sds((2, kron * kron, LANES), F32),
        ],
        in_specs=[VMEM] * 5,
        out_specs=[VMEM] * 4,
        compiler_params=small_params,
        name="prep",
    )(factors, down_left, down_right, up_left, up_right)

    outs = pl.pallas_call(
        main_kernel,
        out_shape=[
            sds((rows3, width), BF16),
            sds((rows3, width), F32),
            sds((2 * blk, width), F32),
            sds((2 * blk, width), F32),
            sds((4 * blk, width), BF16),
            sds((devices, 32, LANES), BF16),
        ],
        in_specs=[SMEM] + [VMEM] * 15 + [ANY] * 7,
        out_specs=[VMEM] * 6,
        scratch_shapes=[
            pltpu.VMEM((width, width), BF16),
            pltpu.VMEM((width, width), BF16),
            pltpu.VMEM((width, width), BF16),
            pltpu.VMEM((width, width), BF16),
            pltpu.VMEM((width, ffw), BF16),
            pltpu.VMEM((ffw, width), BF16),
            pltpu.VMEM((2, 8, blk * mp_size), jnp.int32),
            pltpu.VMEM((8 * blk, width), BF16),
            pltpu.VMEM((8 * blk, width), BF16),
            pltpu.VMEM((rows3, width), BF16),
            pltpu.VMEM((8 * blk, width), BF16),
            pltpu.VMEM((8 * blk, width), BF16),
            pltpu.VMEM((heads, blk, span), F32),
            pltpu.VMEM((32, LANES), F32),
            pltpu.VMEM((heads // 2, 4 * blk, 4 * blk), BF16),
            pltpu.VMEM((heads // 2, 2 * blk, 4 * blk), BF16),
            pltpu.VMEM((rows3, width), BF16),
            pltpu.VMEM((rows3, width), F32),
            pltpu.VMEM((rows3, width), F32),
            pltpu.VMEM((rows3, ffw), BF16),
            pltpu.VMEM((rows3, ffw), BF16),
            pltpu.VMEM((rows3, width), BF16),
            pltpu.VMEM((rows3, width), F32),
            pltpu.VMEM((rows3, width), BF16),
            pltpu.VMEM((rows3, width), BF16),
            pltpu.VMEM((width, 8 * blk), BF16),
            pltpu.VMEM((width, 8 * blk), BF16),
            pltpu.SemaphoreType.DMA((8,)),
        ],
        compiler_params=pltpu.CompilerParams(vmem_limit_bytes=62 * 2**20),
        name="layer",
    )(
        lengths,
        layer_input,
        wf,
        cx,
        m1,
        mf,
        mc,
        targets,
        tf,
        attn_gain,
        ffn_gain,
        table_t,
        low,
        lefts,
        facs,
        rights,
        relative_bucket,
        query_matrix,
        key_matrix,
        value_matrix,
        attention_output_weight,
        feedforward_input_weight,
        feedforward_output_weight,
    )
    blk3, g_res, gw, gc, send, small = outs
    recv = lax.ppermute(send, "mp", core)
    blk_f = lax.ppermute(blk3[blk : 2 * blk], "mp", chip)
    w_grad, away = pl.pallas_call(
        mid_kernel,
        out_shape=[sds((blk, width), F32), sds((2, blk, width), BF16)],
        in_specs=[VMEM] * 7,
        out_specs=[VMEM] * 2,
        compiler_params=small_params,
        name="middle",
    )(layer_input, wf, attn_gain, gw, gc, recv, g_res)
    back = lax.ppermute(away, "mp", chip)
    gathered = lax.all_to_all(small, axes, split_axis=0, concat_axis=0, tiled=True)

    loss, block_out, grad_input, g1, g2, g_table, *g_params = pl.pallas_call(
        functools.partial(last_kernel, float(token_total), float(seq_total)),
        out_shape=[
            sds((1, 1), F32),
            sds((seqs, blk, width), BF16),
            sds((seqs, blk, width), F32),
            sds((width // LANES, LANES), F32),
            sds((width // LANES, LANES), F32),
            sds(table_t.shape, F32),
        ]
        + [sds(p.shape, F32) for p in (factors, down_left, down_right, up_left, up_right)],
        in_specs=[VMEM] * 15,
        out_specs=[VMEM] * 11,
        compiler_params=small_params,
        name="finish",
    )(
        layer_input,
        attn_gain,
        gc,
        recv,
        g_res,
        back,
        w_grad,
        blk3,
        blk_f,
        gathered,
        factors,
        down_left,
        down_right,
        up_left,
        up_right,
    )
    return (
        loss.reshape(()),
        block_out,
        grad_input,
        g1.reshape(width),
        g2.reshape(width),
        g_table.T,
        *g_params,
    )


def solution(mesh):
    rows = P("dp", "mp", None)
    return jax.shard_map(
        local,
        mesh=mesh,
        in_specs=(rows, rows) + (P(),) * 14 + (P("dp"), P()),
        out_specs=(P(), rows, rows) + (P(),) * 8,
        check_vma=False,
    )
```

```python
import functools
from types import SimpleNamespace

import jax
import jax.numpy as jnp
from jax import lax
from jax.experimental import pallas as pl
from jax.experimental.pallas import tpu as pltpu
from jax.sharding import PartitionSpec as P

EPSILON = 1e-06
F32 = jnp.float32
BF16 = jnp.bfloat16
EXACT = lax.Precision.HIGHEST
GELU_A = 0.7978845608028654
GELU_B = 0.044715
LANES = 128
HALF = LANES // 2
VMEM_BYTES = 62 * 2**20
HBM = pltpu.HBM
VMEM = pltpu.VMEM
SMEM = pltpu.SMEM


def dot(a, b, ca=1, cb=0, precision=None):
    return lax.dot_general(
        a, b, (((ca,), (cb,)), ((), ())), preferred_element_type=F32, precision=precision
    )


def iota(shape, dim):
    return lax.broadcasted_iota(jnp.int32, shape, dim)


def rms(values):
    return lax.rsqrt(jnp.mean(values * values, axis=-1, keepdims=True) + EPSILON)


def gelu_pair(v):
    square = v * v
    w = 1.0 + jnp.tanh(v * (GELU_A + (GELU_A * GELU_B) * square))
    half = 0.5 * v
    slope = w * (0.5 + half * (2.0 - w) * (GELU_A + (3.0 * GELU_A * GELU_B) * square))
    return half * w, slope


def hot(left, right):
    return (left == right).astype(F32)


class Mover:
    def __init__(self, sems):
        self.sems = sems
        self.used = 0

    def start(self, src, dst):
        copy = pltpu.make_async_copy(src, dst, self.sems.at[self.used])
        self.used += 1
        copy.start()
        return copy


def call(name, body, ins, outs, scratch, sems, cost_us=None):
    names = [n for n, _, _ in ins] + [n for n, _, _, _ in outs] + list(scratch) + ["sems"]

    def kernel(*refs):
        body(SimpleNamespace(**dict(zip(names, refs))))

    results = pl.pallas_call(
        kernel,
        out_shape=[jax.ShapeDtypeStruct(shape, dtype) for _, shape, dtype, _ in outs],
        in_specs=[pl.BlockSpec(memory_space=space) for _, _, space in ins],
        out_specs=[pl.BlockSpec(memory_space=space) for _, _, _, space in outs],
        scratch_shapes=[pltpu.VMEM(shape, dtype) for shape, dtype in scratch.values()]
        + [pltpu.SemaphoreType.DMA((max(sems, 1),))],
        compiler_params=pltpu.CompilerParams(vmem_limit_bytes=VMEM_BYTES),
        cost_estimate=None
        if cost_us is None
        else pl.CostEstimate(flops=int(cost_us * 1e9), bytes_accessed=0, transcendentals=0),
        name=name,
    )(*[array for _, array, _ in ins])
    return SimpleNamespace(**dict(zip([o[0] for o in outs], results)))


def factor_rows(fac_ref, transposed):
    kron = fac_ref.shape[0]
    pieces = [fac_ref[i].T if transposed else fac_ref[i] for i in range(kron)]
    return jnp.concatenate(pieces, axis=0)


class Kron:
    def __init__(self, fac_ref, transposed, left_ref, right_ref):
        kron = left_ref.shape[0]
        self.block = left_ref.shape[1]
        self.inner = right_ref.shape[1]
        self.kron = kron
        width = kron * self.block
        rows = kron * kron
        inner = self.inner
        self.expand = hot(iota((rows, kron), 0) // kron, iota((rows, kron), 1))
        take_c = hot(iota((kron, LANES), 0), iota((kron, LANES), 1) // inner)
        lane_d = iota((inner, LANES), 1)
        take_d = jnp.where(
            lane_d < kron * inner, hot(iota((inner, LANES), 0), lane_d % inner), 0.0
        )
        self.same_a = hot(iota((rows, width), 0) % kron, iota((rows, width), 1) // self.block)
        wide_left = jnp.concatenate([left_ref[...]] * kron, axis=1)
        self.left = dot(self.expand, wide_left, precision=EXACT) * self.same_a
        self.fac = dot(factor_rows(fac_ref, transposed), take_c, precision=EXACT)
        self.right = dot(
            self.expand, dot(right_ref[...], take_d, precision=EXACT), precision=EXACT
        )

    def matrix(self):
        return dot(self.left, self.fac * self.right, 0, 0, precision=EXACT)


class KronBack:
    def __init__(self, kron, block, inner, left, fac, right):
        self.kron, self.block, self.inner = kron, block, inner
        self.left, self.fac, self.right = left, fac, right

    def place(self, of_lane, start):
        lane_in = iota((LANES, LANES), 0)
        keep = (lane_in < self.kron * self.inner) & (iota((LANES, LANES), 1) - start == of_lane(lane_in))
        return keep.astype(BF16)

    def back(self, grad, fac_at, right_at):
        grad = grad.astype(BF16)
        rows = self.kron * self.kron
        width = self.kron * self.block
        inner = dot(self.left.astype(BF16), grad)
        g_fac = dot((inner * self.right).astype(BF16), self.place(lambda n: n // self.inner, fac_at))
        expand = (iota((rows, self.kron), 0) // self.kron == iota((rows, self.kron), 1)).astype(BF16)
        same_i = dot(expand, (inner * self.fac).astype(BF16), 0, 0)
        g_right = dot(same_i.astype(BF16), self.place(lambda n: n % self.inner, right_at))
        outer = dot((self.fac * self.right).astype(BF16), grad, 1, 1)
        outer = outer * hot(iota((rows, width), 0) % self.kron, iota((rows, width), 1) // self.block)
        outer = dot(expand, outer.astype(BF16), 0, 0)
        g_left = sum(outer[:, n * self.block : (n + 1) * self.block] for n in range(self.kron))
        return g_fac, g_right, g_left


def my_mp():
    return lax.axis_index("mp")


def worked(mp):
    return jnp.where(mp < 2, 0, 2)


def gain_row(ref):
    return ref[...].astype(F32).reshape(1, ref.shape[0])


def slot_positions(mp):
    return (mp, mp ^ 2, mp ^ 1, mp ^ 3)


def pick_body(r):
    w = worked(my_mp())
    mover = Mover(r.sems)
    copies = [
        mover.start(r.x.at[2 - w], r.xf),
        mover.start(r.x.at[1], r.xc),
        mover.start(r.t.at[2 - w], r.tf),
    ]
    for copy in copies:
        copy.wait()


def normed(rows, gain):
    values = rows.astype(F32)
    return (values * rms(values) * gain).astype(BF16)


def prep_body(r):
    w = worked(my_mp())
    blk = r.x.shape[1]
    mover = Mover(r.sems)
    copies = [
        mover.start(src, dst)
        for src, dst in (
            (r.x.at[w], r.rows.at[0:blk]),
            (r.x.at[1], r.rows.at[2 * blk : 3 * blk]),
            (r.m1.at[w], r.rows.at[blk : 2 * blk]),
            (r.m1.at[1], r.rows.at[3 * blk : 4 * blk]),
            (r.wk_hbm, r.wk),
            (r.wv_hbm, r.wv),
            (r.wq_hbm, r.wq),
        )
    ]
    down = Kron(r.fac_in, False, r.dl, r.dr)
    up = Kron(r.fac_in, True, r.ur, r.ul)
    for n, one in enumerate((down, up)):
        r.low[n] = one.matrix().astype(BF16)
        r.left[n] = one.left
        r.fac[n] = one.fac
        r.right[n] = one.right
    gain = gain_row(r.gain1)
    for copy in copies[:4]:
        copy.wait()
    for n in range(4):
        rows = slice(n * blk, (n + 1) * blk)
        r.xn[rows] = normed(r.rows[rows], gain)
    copies[4].wait()
    r.k[...] = dot(r.xn[...], r.wk[...]).astype(BF16)
    copies[5].wait()
    r.v[...] = dot(r.xn[...], r.wv[...]).astype(BF16)
    copies[6].wait()
    r.q[0:blk] = dot(r.xn[0:blk], r.wq[...]).astype(BF16)
    r.q[blk : 2 * blk] = dot(r.xn[2 * blk : 3 * blk], r.wq[...]).astype(BF16)


def start_edges(r, mover, seq):
    return [
        mover.start(r.bucket.at[row : row + 8], r.edge.at[n]) for n, row in enumerate((0, seq - 8))
    ]


def bucket_hots(r, seq):
    by_lane = jnp.concatenate([pltpu.roll(r.edge[1, 7:8, :], 1, 1), r.edge[0, 0:1, :]], axis=1)
    return hot(iota((r.table.shape[1], 2 * seq), 0), by_lane)


def fill_bias(r, buckets, blk):
    span = buckets.shape[1]
    by_distance = dot(r.table[...], buckets, precision=EXACT)
    for h in range(by_distance.shape[0]):
        row = by_distance[h : h + 1]
        near = pltpu.roll(
            jnp.broadcast_to(row[:, 2 * blk : 6 * blk], (blk, span // 2)),
            3 * blk,
            1,
            stride=1,
            stride_axis=0,
        )
        r.bias[h, :, 0 : 2 * blk] = jnp.broadcast_to(row[:, 1:2], (blk, 2 * blk))
        r.bias[h, :, 2 * blk : 5 * blk] = near[:, 0 : 3 * blk]
        r.bias[h, :, 5 * blk : 7 * blk] = jnp.broadcast_to(row[:, span - 1 : span], (blk, 2 * blk))


def key_masks(slots, length, blk):
    lane = iota((1, blk), 1)
    return [jnp.where(s * blk + lane < length, 0.0, -jnp.inf).astype(F32) for s in slots]


def by_head(rows):
    half = iota(rows.shape, 1) < HALF
    zero = jnp.zeros_like(rows)
    return jnp.concatenate([jnp.where(half, rows, zero), jnp.where(half, zero, rows)], axis=0)


def attend(hp, q, k, v, bias, mask, slots, q_poss, p, inv_out, ctx_out):
    count = len(q_poss)
    blk = q.shape[0] // count
    low_half = iota((blk, LANES), 1) < HALF
    scores = dot(by_head(q[...]), k[...], 1, 1)
    for u in range(2 * count):
        h, b = divmod(u, count)
        rows = slice(u * blk, (u + 1) * blk)
        parts = []
        for n in range(4):
            place = pl.ds(pl.multiple_of((slots[n] - q_poss[b] + 3) * blk, blk), blk)
            parts.append(
                scores[rows, n * blk : (n + 1) * blk] + (bias[2 * hp + h, :, place] + mask[n])
            )
        top = jnp.max(
            jnp.maximum(jnp.maximum(parts[0], parts[1]), jnp.maximum(parts[2], parts[3])),
            axis=-1,
            keepdims=True,
        )
        parts = [jnp.exp(part - top) for part in parts]
        for n in range(4):
            p[rows, n * blk : (n + 1) * blk] = parts[n].astype(BF16)
    values = v[...]
    out = dot(p[...], jnp.concatenate([values, jnp.ones_like(values)], axis=1))
    inv_all = 1.0 / out[:, LANES:]
    out = out[:, 0:LANES]
    for b in range(count):
        rows = slice(b * blk, (b + 1) * blk)
        inv = jnp.where(
            low_half, inv_all[rows], inv_all[(count + b) * blk : (count + b + 1) * blk]
        )
        inv_out[rows] = inv
        mixed = jnp.where(
            low_half, out[rows], out[(count + b) * blk : (count + b + 1) * blk]
        )
        ctx_out[rows] = (mixed * inv).astype(BF16)


def attend_back(q, k, v, p, do, inv, ctx, count, dq_out, dkt_out, dvt_out):
    blk = q.shape[0] // count
    low_half = iota((blk, LANES), 1) < HALF
    do = by_head(do[...].astype(F32) * inv[...])
    ctx = ctx[...].astype(F32)
    delta = jnp.sum(do * jnp.concatenate([ctx, ctx], axis=0), axis=-1, keepdims=True)
    do = do.astype(BF16)
    dp = dot(do, v[...], 1, 1)
    ds = p[...].astype(F32) * (dp - delta)
    low = ds.astype(BF16)
    dq = dot(low, k[...])
    for b in range(count):
        rows = slice(b * blk, (b + 1) * blk)
        dq_out[rows] = jnp.where(
            low_half, dq[rows], dq[(count + b) * blk : (count + b + 1) * blk]
        ).astype(BF16)
    dkt_out[...] = dot(by_head(q[...]), low, 0, 0).astype(BF16)
    dvt_out[...] = dot(do, p[...], 0, 0).astype(BF16)
    return ds


def main_body(r):
    mp = my_mp()
    w = worked(mp)
    slots = slot_positions(mp)
    blk, width = r.wf.shape
    seq = 4 * blk
    heads = r.table.shape[0]
    pairs = width // LANES
    ffw = r.win.shape[1]
    at = lambda n: slice(n * blk, (n + 1) * blk)
    mover = Mover(r.sems)
    go = lambda pairs_of: [mover.start(src, dst) for src, dst in pairs_of]
    edges = start_edges(r, mover, seq)
    far_rows = go(
        (
            (r.wf, r.rows.at[at(1)]),
            (r.mf, r.rows.at[at(3)]),
            (r.cx, r.rows.at[at(5)]),
            (r.mc, r.rows.at[at(7)]),
        )
    )
    weights_kv = go(((r.wk_hbm, r.wk), (r.wv_hbm, r.wv), (r.wq_hbm, r.wq)))
    shared = go(
        (
            (r.q0.at[at(0)], r.q_s.at[at(0)]),
            (r.k0.at[at(0)], r.k_s.at[at(0)]),
            (r.v0.at[at(0)], r.v_s.at[at(0)]),
            (r.k0.at[at(1)], r.k_s.at[at(2)]),
            (r.v0.at[at(1)], r.v_s.at[at(2)]),
            (r.q0.at[at(1)], r.q_s.at[at(2)]),
            (r.k0.at[at(2)], r.k_s.at[at(4)]),
            (r.v0.at[at(2)], r.v_s.at[at(4)]),
            (r.k0.at[at(3)], r.k_s.at[at(6)]),
            (r.v0.at[at(3)], r.v_s.at[at(6)]),
        )
    )
    gain1 = gain_row(r.gain1)
    gain2 = gain_row(r.gain2)

    for copy in edges:
        copy.wait()
    buckets = bucket_hots(r, seq)
    fill_bias(r, buckets, blk)
    for n in range(4):
        far_rows[n].wait()
        r.far[at(n)] = normed(r.rows[at(2 * n + 1)], gain1)
    for copy, weight, dst in ((weights_kv[0], r.wk, r.k_s), (weights_kv[1], r.wv, r.v_s)):
        copy.wait()
        every = dot(r.far[...], weight[...]).astype(BF16)
        for n in range(4):
            dst[at(2 * n + 1)] = every[at(n)]
    own_rows = go(((r.x.at[w], r.rows.at[at(0)]), (r.x.at[1], r.rows.at[at(4)])))
    weight_o = mover.start(r.wo_hbm, r.wo)
    weight_in = mover.start(r.win_hbm, r.win)
    weight_out = mover.start(r.wout_hbm, r.wout)
    goals = go(
        (
            (r.t.at[w], r.goal.at[at(0)]),
            (r.tf, r.goal.at[at(1)]),
            (r.t.at[1], r.goal.at[at(2)]),
        )
    )
    late = go(
        (
            (r.m1.at[w], r.rows.at[at(2)]),
            (r.m1.at[1], r.rows.at[at(6)]),
        )
    )
    weights_kv[2].wait()
    r.q_s[at(1)] = dot(r.far[at(0)], r.wq[...]).astype(BF16)
    for copy in shared:
        copy.wait()
    masks = [key_masks(slots, r.lengths[n], blk) for n in (w, 1)]
    groups = (
        (slice(0, 2 * blk), (mp, mp ^ 2), slice(0, seq), r.pw_s),
        (at(2), (mp,), slice(seq, 2 * seq), r.pc_s),
    )
    for hp in range(pairs):
        cols = slice(hp * LANES, (hp + 1) * LANES)
        for (q_rows, q_poss, k_rows, p), mask in zip(groups, masks):
            attend(
                hp,
                r.q_s.at[q_rows, cols],
                r.k_s.at[k_rows, cols],
                r.v_s.at[k_rows, cols],
                r.bias,
                mask,
                slots,
                q_poss,
                p.at[hp],
                r.inv_s.at[q_rows, cols],
                r.ctx_s.at[q_rows, cols],
            )

    acc = r.bias
    acc[...] = jnp.zeros_like(acc)

    tokens = 3 * blk
    for copy in own_rows:
        copy.wait()
    own = jnp.concatenate([r.rows[0 : 2 * blk], r.rows[at(4)]], axis=0).astype(F32)
    weight_o.wait()
    residual = own + dot(r.ctx_s[...], r.wo[...])
    r.res[...] = residual
    inv2 = rms(residual)
    r.xn[...] = (residual * inv2 * gain2).astype(BF16)
    weight_in.wait()
    weight_out.wait()
    chunk = 512
    chunks = [slice(n * chunk, (n + 1) * chunk) for n in range(ffw // chunk)]
    pre = dot(r.xn[...], r.win[:, chunks[0]])
    total = None
    for n, cols in enumerate(chunks):
        ahead = dot(r.xn[...], r.win[:, chunks[n + 1]]) if n + 1 < len(chunks) else None
        value, slope = gelu_pair(pre)
        value = value.astype(BF16)
        r.slope[:, cols] = slope.astype(BF16)
        part = dot(value, r.wout[cols, :])
        total = part if total is None else total + part
        pre = ahead
    r.ffn[...] = total.astype(BF16)

    down_low = r.low[0]
    up_low = r.low[1]
    ffn = r.ffn[...]
    activated, act_slope = gelu_pair(dot(ffn, down_low))
    activated = activated.astype(BF16)
    final = r.res[...] + ffn.astype(F32) + dot(activated, up_low, 1, 1)
    r.blk_s[...] = final.astype(BF16)
    out = go(
        (
            (r.blk_s.at[at(1)], r.blk_f),
            (r.blk_s.at[at(0)], r.blk_own.at[0]),
            (r.blk_s.at[at(2)], r.blk_own.at[1]),
        )
    )
    row = iota((blk, 1), 0)
    valid = jnp.concatenate(
        [
            pos * blk + row < length
            for pos, length in ((mp, r.lengths[w]), (mp ^ 2, r.lengths[w]), (mp, r.lengths[1]))
        ],
        axis=0,
    )
    for copy in goals:
        copy.wait()
    err = jnp.where(valid, final - r.goal[...].astype(F32), 0.0)
    r.err[...] = err
    loss = 0.5 * jnp.sum(jnp.sum(err * err, axis=0, keepdims=True), axis=1, keepdims=True)
    g_adapter = err.astype(BF16)
    grad_up = dot(g_adapter, activated, 0, 0)
    g_squeezed = (dot(g_adapter, up_low) * act_slope).astype(BF16)
    grad_down = dot(ffn, g_squeezed, 0, 0)
    kron, block, inner = r.shape_kron
    backs = [
        KronBack(kron, block, inner, r.left[n], r.fac[n], r.right[n]).back(grad, *PACK_KRON[n])
        for n, grad in enumerate((grad_down, grad_up))
    ]
    r.ffn[...] = (err + dot(g_squeezed, down_low, 1, 1)).astype(BF16)

    for n in range(ffw // chunk):
        cols = slice(n * chunk, (n + 1) * chunk)
        r.hid[:, cols] = (dot(r.ffn[...], r.wout[cols, :], 1, 1) * r.slope[:, cols].astype(F32)).astype(
            BF16
        )
    g_normed = jnp.concatenate(
        [dot(r.hid[...], r.win[n * 256 : (n + 1) * 256, :], 1, 1) for n in range(width // 256)],
        axis=1,
    )
    residual = r.res[...]
    inv2 = rms(residual)
    g2 = jnp.sum(g_normed * residual * inv2, axis=0, keepdims=True)
    weighted = g_normed * gain2
    mean = jnp.mean(weighted * residual, axis=-1, keepdims=True)
    g_res = r.err[...] + inv2 * weighted - residual * (inv2 * inv2 * inv2 * mean)
    r.err[...] = g_res
    r.do[...] = dot(g_res.astype(BF16), r.wo[...], 1, 1).astype(BF16)

    for hp in range(pairs):
        cols = slice(hp * LANES, (hp + 1) * LANES)
        scores = []
        for q_rows, q_poss, k_rows, p in groups:
            scores.append(
                attend_back(
                    r.q_s.at[q_rows, cols],
                    r.k_s.at[k_rows, cols],
                    r.v_s.at[k_rows, cols],
                    p.at[hp],
                    r.do.at[q_rows, cols],
                    r.inv_s.at[q_rows, cols],
                    r.ctx_s.at[q_rows, cols],
                    len(q_poss),
                    r.dq.at[q_rows, cols],
                    r.dkt.at[cols, k_rows],
                    r.dvt.at[cols, k_rows],
                )
            )
        for h in range(2):
            near = scores[0][2 * h * blk : (2 * h + 1) * blk] + scores[1][h * blk : (h + 1) * blk]
            far = scores[0][(2 * h + 1) * blk : (2 * h + 2) * blk]
            for piece, q_pos in ((near, mp), (far, mp ^ 2)):
                for n in range(4):
                    place = pl.ds(pl.multiple_of((slots[n] - q_pos + 3) * blk, blk), blk)
                    acc[2 * hp + h, :, place] += piece[:, n * blk : (n + 1) * blk]

    sub = iota((8, seq), 0)

    def along_diagonals(h):
        total = jnp.zeros((8, seq), F32)
        for g in range(blk // 8):
            near = jnp.concatenate(
                [acc[h, 8 * g : 8 * g + 8, 2 * blk : 5 * blk], jnp.zeros((8, blk), F32)], axis=1
            )
            total = total + pltpu.roll(near, blk - 8 * g, 1)
        for bit in (1, 2, 4):
            total = jnp.where((sub & bit) > 0, pltpu.roll(total, seq - bit, 1), total)
        near = jnp.sum(total, axis=0, keepdims=True)
        below = jnp.sum(acc[h, :, 0 : 2 * blk], axis=0, keepdims=True)
        above = jnp.sum(acc[h, :, 5 * blk : 7 * blk], axis=0, keepdims=True)
        return jnp.concatenate(
            [
                jnp.zeros((1, blk), F32),
                below[:, 0:blk],
                below[:, blk : 2 * blk] + near[:, 0:blk],
                near[:, blk:seq],
                above,
            ],
            axis=1,
        )

    for copy in late:
        copy.wait()
    sums = []
    g1 = jnp.zeros((1, width), F32)
    side = 256
    for first, dq_rows in ((0, slice(0, 2 * blk)), (4, at(2))):
        cols = slice(first * blk, first * blk + seq)
        pieces = []
        for n in range(width // side):
            outs = slice(n * side, (n + 1) * side)
            piece = dot(r.dkt[:, cols], r.wk[outs, :], 0, 1)
            if len(sums) < heads:
                sums.append(along_diagonals(len(sums)))
            piece = piece + dot(r.dvt[:, cols], r.wv[outs, :], 0, 1)
            if len(sums) < heads:
                sums.append(along_diagonals(len(sums)))
            pieces.append(piece)
        parts = jnp.concatenate(pieces, axis=1)
        own = dot(r.dq[dq_rows], r.wq[...], 1, 1)
        for n in range(4):
            part = parts[at(n)]
            if n * blk < own.shape[0]:
                part = part + own[at(n)]
            values = r.rows[at(first + n)].astype(F32)
            inv1 = rms(values)
            scaled = part * values
            g1 = g1 + jnp.sum(scaled * inv1, axis=0, keepdims=True)
            mean = jnp.mean(scaled * gain1, axis=-1, keepdims=True)
            back = inv1 * (part * gain1) - values * (inv1 * inv1 * inv1 * mean)
            if n < 2:
                m = n if first == 0 else 2 + n
                if m < 3:
                    back = back + r.err[at(m)]
                r.base_s[at(m)] = back
                out += go(((r.base_s.at[at(m)], r.base.at[m]),))
            else:
                m = n - 2 if first == 0 else n
                r.send_s[at(m)] = back.astype(BF16)
                out += go(((r.send_s.at[at(m)], r.send.at[m]),))
    for h in range(len(sums), heads):
        sums.append(along_diagonals(h))
    g_table = dot(jnp.concatenate(sums, axis=0), buckets, 1, 1, precision=EXACT)

    (gf_d, g_dr, g_dl), (gf_u, g_ul, g_ur) = backs
    row16 = iota((16, LANES), 0)
    lane16 = iota((16, LANES), 1)
    pack = r.pack
    pack[0:16] = gf_d + gf_u
    pack[0:4] += g_dr + g_ul
    pack[0:heads, 0 : r.table.shape[1]] = g_table
    pack[0:4, HALF:LANES] = g_dl[:, 0:HALF]
    pack[4:8, HALF:LANES] = g_dl[:, HALF : 2 * HALF]
    pack[8:12, HALF:LANES] = g_dl[:, 2 * HALF : 3 * HALF]
    pack[12:16, HALF:LANES] = g_ur[:, 0:HALF]
    pack[16:20] = g_ur[:, HALF : 3 * HALF]
    for n in range(width // LANES):
        pack[20 + n : 21 + n] = g1[:, n * LANES : (n + 1) * LANES]
        pack[26 + n : 27 + n] = g2[:, n * LANES : (n + 1) * LANES]
    real = (r.lengths[0] + r.lengths[1] + r.lengths[2]).astype(F32)
    both = jnp.where(lane16 < 2, loss, real)
    high = both.astype(BF16).astype(F32)
    both = jnp.where(lane16 % 2 == 0, high, both - high)
    r.small[0:16] = jnp.where((row16 == 15) & (lane16 < 4), both, pack[0:16]).astype(BF16)
    r.small[16:32] = pack[16:32].astype(BF16)
    for copy in out:
        copy.wait()


PACK_KRON = ((32, 40), (36, 52))


def middle_body(r):
    mover = Mover(r.sems)
    copies = [
        mover.start(src, dst)
        for src, dst in (
            (r.base.at[1], r.base_s.at[0]),
            (r.recv.at[1], r.recv_s.at[0]),
            (r.base.at[3], r.base_s.at[1]),
            (r.recv.at[3], r.recv_s.at[1]),
            (r.blk_f, r.away.at[2]),
        )
    ]
    spread = r.small.shape[0] // 2
    first = pl.multiple_of((my_mp() % 2) * spread, spread)
    half = r.small[pl.ds(first, spread)].astype(F32) + r.others[pl.ds(first, spread)].astype(F32)
    row = iota(half.shape, 0)
    lane = iota(half.shape, 1)
    even = lane % 2 == 0
    whole = half + jnp.where(even, pltpu.roll(half, LANES - 1, 1), pltpu.roll(half, 1, 1))
    high = whole.astype(BF16).astype(F32)
    parted = (row == 15) & (lane < 4) & (my_mp() % 2 == 0)
    half = jnp.where(parted, jnp.where(even, high, whole - high), half).astype(BF16)
    for n in range(r.spread.shape[0]):
        r.spread[n] = half
    for n in range(2):
        copies[2 * n].wait()
        copies[2 * n + 1].wait()
        r.away[n] = (r.base_s[n] + r.recv_s[n].astype(F32)).astype(BF16)
    copies[4].wait()


def finish_body(token_total, seq_total, r):
    w = worked(my_mp())
    width = r.grad.shape[2]
    mover = Mover(r.sems)
    copies = [
        mover.start(src, dst)
        for src, dst in (
            (r.gathered, r.gathered_s),
            (r.back.at[0], r.back_s.at[0]),
            (r.back.at[1], r.back_s.at[1]),
            (r.base.at[0], r.base_s.at[0]),
            (r.recv.at[0], r.recv_s.at[0]),
            (r.base.at[2], r.base_s.at[1]),
            (r.recv.at[2], r.recv_s.at[1]),
            (r.back.at[2], r.block.at[2 - w]),
            (r.blk_own.at[0], r.block.at[w]),
            (r.blk_own.at[1], r.block.at[1]),
        )
    ]
    copies[0].wait()
    halves = [r.gathered_s[n].astype(F32) for n in range(2)]
    for n in range(2, r.gathered_s.shape[0]):
        halves[n % 2] = halves[n % 2] + r.gathered_s[n].astype(F32)
    total = jnp.concatenate(halves, axis=0)
    tail = total[15:16, 0:4]
    count = (tail[:, 2:3] + tail[:, 3:4]) * 0.25
    scale = token_total / count
    params = [r.dl, r.dr, r.ul, r.ur]
    squares = [jnp.sum(r.fac[n] * r.fac[n], keepdims=True) for n in range(r.fac.shape[0])]
    squares += [jnp.sum(p[...] * p[...], keepdims=True) for p in params]
    penalty = 0.5 * seq_total * sum(squares)
    r.loss[...] = (scale * (tail[:, 0:1] + tail[:, 1:2]) + penalty) / (token_total * width)

    heads, buckets = r.g_table.shape
    r.g_table[...] = scale * total[0:heads, 0:buckets]
    kron = r.fac.shape[0]
    for i in range(kron):
        rows = slice(i * kron, (i + 1) * kron)
        r.g_fac[i] = (
            scale * (total[rows, 32 : 32 + kron] + total[rows, 36 : 36 + kron].T)
            + seq_total * r.fac[i]
        )
    r.g_dr[...] = scale * total[0:4, 40:52] + seq_total * r.dr[...]
    r.g_ul[...] = scale * total[0:4, 52:64] + seq_total * r.ul[...]
    g_dl = jnp.concatenate([total[4 * n : 4 * n + 4, HALF:LANES] for n in range(3)], axis=1)
    r.g_dl[...] = scale * g_dl + seq_total * r.dl[...]
    g_ur = jnp.concatenate([total[12:16, HALF:LANES], total[16:20]], axis=1)
    r.g_ur[...] = scale * g_ur + seq_total * r.ur[...]
    for n in range(width // LANES):
        r.g1[n : n + 1] = scale * total[20 + n : 21 + n]
        r.g2[n : n + 1] = scale * total[26 + n : 27 + n]

    for copy in copies[1:]:
        copy.wait()
    r.grad[2 - w] = scale * r.back_s[0].astype(F32)
    r.grad[w] = scale * (r.base_s[0] + r.recv_s[0].astype(F32))
    r.grad[1] = scale * (r.base_s[1] + r.recv_s[1].astype(F32) + r.back_s[1].astype(F32))


def local(
    layer_input,
    targets,
    attn_gain,
    ffn_gain,
    query_matrix,
    key_matrix,
    value_matrix,
    attention_output_weight,
    feedforward_input_weight,
    feedforward_output_weight,
    bias_table,
    factors,
    down_left,
    down_right,
    up_left,
    up_right,
    lengths,
    relative_bucket,
):
    seqs, blk, width = layer_input.shape
    mp_size = lax.axis_size("mp")
    axes = ("dp", "mp")
    devices = lax.axis_size("dp") * mp_size
    heads = bias_table.shape[1]
    ffw = feedforward_input_weight.shape[1]
    kron = factors.shape[0]
    seq_total = lax.axis_size("dp") * seqs
    token_total = seq_total * blk * mp_size
    assert seqs == 3 and mp_size == 4
    core = [(i, i ^ 1) for i in range(mp_size)]
    chip = [(i, i ^ 2) for i in range(mp_size)]
    pairs = heads // 2
    seq = blk * mp_size
    table = bias_table.T
    square = ((width, width), BF16)
    rows = lambda n, dtype=BF16: ((n * blk, width), dtype)

    picked = call(
        "pick",
        pick_body,
        [("x", layer_input, HBM), ("t", targets, HBM)],
        [(n, (blk, width), BF16, VMEM) for n in ("xf", "xc", "tf")],
        {},
        3,
    )
    wf = lax.ppermute(picked.xf, "mp", chip)
    cx = lax.ppermute(picked.xc, "mp", chip)
    tf = lax.ppermute(picked.tf, "mp", chip)
    m1 = lax.ppermute(layer_input, "mp", core)
    prep = call(
        "prep",
        prep_body,
        [
            ("x", layer_input, HBM),
            ("m1", m1, HBM),
            ("gain1", attn_gain, VMEM),
            ("fac_in", factors, VMEM),
            ("dl", down_left, VMEM),
            ("dr", down_right, VMEM),
            ("ul", up_left, VMEM),
            ("ur", up_right, VMEM),
            ("wq_hbm", query_matrix, HBM),
            ("wk_hbm", key_matrix, HBM),
            ("wv_hbm", value_matrix, HBM),
        ],
        [
            ("q",) + rows(2) + (VMEM,),
            ("k",) + rows(4) + (VMEM,),
            ("v",) + rows(4) + (VMEM,),
            ("low", (2, width, LANES), BF16, VMEM),
            ("left", (2, kron * kron, width), F32, VMEM),
            ("fac", (2, kron * kron, LANES), F32, VMEM),
            ("right", (2, kron * kron, LANES), F32, VMEM),
        ],
        {"rows": rows(4), "xn": rows(4), "wq": square, "wk": square, "wv": square},
        7,
        4.0,
    )

    wf, cx, prep.k = lax.optimization_barrier((wf, cx, prep.k))
    mf = lax.ppermute(wf, "mp", core)
    mc = lax.ppermute(cx, "mp", core)

    def main_with_shape(r):
        r.shape_kron = (kron, down_left.shape[1], down_right.shape[1])
        main_body(r)

    main = call(
        "main",
        main_with_shape,
        [
            ("lengths", lengths, SMEM),
            ("x", layer_input, HBM),
            ("t", targets, HBM),
            ("wf", wf, HBM),
            ("cx", cx, HBM),
            ("tf", tf, HBM),
            ("m1", m1, HBM),
            ("mf", mf, HBM),
            ("mc", mc, HBM),
            ("gain1", attn_gain, VMEM),
            ("gain2", ffn_gain, VMEM),
            ("table", table, VMEM),
            ("bucket", relative_bucket, HBM),
            ("low", prep.low, VMEM),
            ("left", prep.left, VMEM),
            ("fac", prep.fac, VMEM),
            ("right", prep.right, VMEM),
            ("q0", prep.q, HBM),
            ("k0", prep.k, HBM),
            ("v0", prep.v, HBM),
            ("wq_hbm", query_matrix, HBM),
            ("wk_hbm", key_matrix, HBM),
            ("wv_hbm", value_matrix, HBM),
            ("wo_hbm", attention_output_weight, HBM),
            ("win_hbm", feedforward_input_weight, HBM),
            ("wout_hbm", feedforward_output_weight, HBM),
        ],
        [
            ("blk_own", (2, blk, width), BF16, HBM),
            ("blk_f", (blk, width), BF16, HBM),
            ("base", (4, blk, width), F32, HBM),
            ("send", (4, blk, width), BF16, HBM),
            ("small", (32, LANES), BF16, VMEM),
        ],
        {
            "wq": square,
            "wk": square,
            "wv": square,
            "wo": square,
            "win": ((width, ffw), BF16),
            "wout": ((ffw, width), BF16),
            "edge": ((2, 8, seq), jnp.int32),
            "rows": rows(8),
            "goal": rows(3),
            "xn": rows(3),
            "q_s": rows(3),
            "k_s": rows(8),
            "v_s": rows(8),
            "far": rows(4),
            "bias": ((heads, blk, 7 * blk), F32),
            "pack": ((32, LANES), F32),
            "pw_s": ((pairs, seq, seq), BF16),
            "pc_s": ((pairs, 2 * blk, seq), BF16),
            "ctx_s": rows(3),
            "inv_s": rows(3, F32),
            "res": rows(3, F32),
            "hid": ((3 * blk, ffw), BF16),
            "slope": ((3 * blk, ffw), BF16),
            "ffn": rows(3),
            "err": rows(3, F32),
            "do": rows(3),
            "dq": rows(3),
            "dkt": ((width, 2 * seq), BF16),
            "dvt": ((width, 2 * seq), BF16),
            "blk_s": rows(3),
            "base_s": rows(4, F32),
            "send_s": rows(4),
        },
        44,
        28.0,
    )
    recv = lax.ppermute(main.send, "mp", core)
    others = lax.ppermute(main.small, "mp", core)
    pair = lambda dtype: ((2, blk, width), dtype)
    middle = call(
        "middle",
        middle_body,
        [("base", main.base, HBM), ("recv", recv, HBM), ("blk_f", main.blk_f, HBM), ("small", main.small, VMEM), ("others", others, VMEM)],
        [("away", (3, blk, width), BF16, VMEM), ("spread", (devices, 16, LANES), BF16, VMEM)],
        {"base_s": pair(F32), "recv_s": pair(BF16)},
        5,
    )
    spread, away = lax.optimization_barrier((middle.spread, middle.away))
    back = lax.ppermute(away, "mp", chip)
    gathered = lax.all_to_all(spread, axes, split_axis=0, concat_axis=0, tiled=True)

    done = call(
        "finish",
        functools.partial(finish_body, float(token_total), float(seq_total)),
        [
            ("gathered", gathered, HBM),
            ("base", main.base, HBM),
            ("recv", recv, HBM),
            ("back", back, HBM),
            ("blk_own", main.blk_own, HBM),
            ("fac", factors, VMEM),
            ("dl", down_left, VMEM),
            ("dr", down_right, VMEM),
            ("ul", up_left, VMEM),
            ("ur", up_right, VMEM),
        ],
        [
            ("loss", (1, 1), F32, VMEM),
            ("block", (seqs, blk, width), BF16, VMEM),
            ("grad", (seqs, blk, width), F32, VMEM),
            ("g1", (width // LANES, LANES), F32, VMEM),
            ("g2", (width // LANES, LANES), F32, VMEM),
            ("g_table", table.shape, F32, VMEM),
            ("g_fac", factors.shape, F32, VMEM),
            ("g_dl", down_left.shape, F32, VMEM),
            ("g_dr", down_right.shape, F32, VMEM),
            ("g_ul", up_left.shape, F32, VMEM),
            ("g_ur", up_right.shape, F32, VMEM),
        ],
        {
            "gathered_s": ((devices, 16, LANES), BF16),
            "back_s": pair(BF16),
            "base_s": pair(F32),
            "recv_s": pair(BF16),
        },
        10,
    )
    return (
        done.loss.reshape(()),
        done.block,
        done.grad,
        done.g1.reshape(width),
        done.g2.reshape(width),
        done.g_table.T,
        done.g_fac,
        done.g_dl,
        done.g_dr,
        done.g_ul,
        done.g_ur,
    )


def solution(mesh):
    rows = P("dp", "mp", None)
    return jax.shard_map(
        local,
        mesh=mesh,
        in_specs=(rows, rows) + (P(),) * 14 + (P("dp"), P()),
        out_specs=(P(), rows, rows) + (P(),) * 8,
        check_vma=False,
    )
```

```python
import functools
from types import SimpleNamespace

import jax
import jax.numpy as jnp
from jax import lax
from jax.experimental import pallas as pl
from jax.experimental.pallas import tpu as pltpu
from jax.sharding import PartitionSpec as P

EPSILON = 1e-06
F32 = jnp.float32
BF16 = jnp.bfloat16
EXACT = lax.Precision.HIGHEST
GELU_A = 0.7978845608028654
GELU_B = 0.044715
LANES = 128
HALF = LANES // 2
VMEM_BYTES = 62 * 2**20
HBM = pltpu.HBM
VMEM = pltpu.VMEM
SMEM = pltpu.SMEM


def dot(a, b, ca=1, cb=0, precision=None):
    return lax.dot_general(
        a, b, (((ca,), (cb,)), ((), ())), preferred_element_type=F32, precision=precision
    )


def iota(shape, dim):
    return lax.broadcasted_iota(jnp.int32, shape, dim)


def rms(values):
    return lax.rsqrt(jnp.mean(values * values, axis=-1, keepdims=True) + EPSILON)


def gelu_pair(v):
    square = v * v
    w = 1.0 + jnp.tanh(v * (GELU_A + (GELU_A * GELU_B) * square))
    half = 0.5 * v
    slope = w * (0.5 + half * (2.0 - w) * (GELU_A + (3.0 * GELU_A * GELU_B) * square))
    return half * w, slope


def hot(left, right):
    return (left == right).astype(F32)


class Mover:
    def __init__(self, sems):
        self.sems = sems
        self.used = 0

    def start(self, src, dst):
        copy = pltpu.make_async_copy(src, dst, self.sems.at[self.used])
        self.used += 1
        copy.start()
        return copy


def call(name, body, ins, outs, scratch, sems, cost_us=None):
    names = [n for n, _, _ in ins] + [n for n, _, _, _ in outs] + list(scratch) + ["sems"]

    def kernel(*refs):
        body(SimpleNamespace(**dict(zip(names, refs))))

    results = pl.pallas_call(
        kernel,
        out_shape=[jax.ShapeDtypeStruct(shape, dtype) for _, shape, dtype, _ in outs],
        in_specs=[pl.BlockSpec(memory_space=space) for _, _, space in ins],
        out_specs=[pl.BlockSpec(memory_space=space) for _, _, _, space in outs],
        scratch_shapes=[pltpu.VMEM(shape, dtype) for shape, dtype in scratch.values()]
        + [pltpu.SemaphoreType.DMA((max(sems, 1),))],
        compiler_params=pltpu.CompilerParams(vmem_limit_bytes=VMEM_BYTES),
        cost_estimate=None
        if cost_us is None
        else pl.CostEstimate(flops=int(cost_us * 1e9), bytes_accessed=0, transcendentals=0),
        name=name,
    )(*[array for _, array, _ in ins])
    return SimpleNamespace(**dict(zip([o[0] for o in outs], results)))


def factor_rows(fac_ref, transposed):
    kron = fac_ref.shape[0]
    pieces = [fac_ref[i].T if transposed else fac_ref[i] for i in range(kron)]
    return jnp.concatenate(pieces, axis=0)


class Kron:
    def __init__(self, fac_ref, transposed, left_ref, right_ref):
        kron = left_ref.shape[0]
        self.block = left_ref.shape[1]
        self.inner = right_ref.shape[1]
        self.kron = kron
        width = kron * self.block
        rows = kron * kron
        inner = self.inner
        self.expand = hot(iota((rows, kron), 0) // kron, iota((rows, kron), 1))
        take_c = hot(iota((kron, LANES), 0), iota((kron, LANES), 1) // inner)
        lane_d = iota((inner, LANES), 1)
        take_d = jnp.where(
            lane_d < kron * inner, hot(iota((inner, LANES), 0), lane_d % inner), 0.0
        )
        self.same_a = hot(iota((rows, width), 0) % kron, iota((rows, width), 1) // self.block)
        wide_left = jnp.concatenate([left_ref[...]] * kron, axis=1)
        self.left = dot(self.expand, wide_left, precision=EXACT) * self.same_a
        self.fac = dot(factor_rows(fac_ref, transposed), take_c, precision=EXACT)
        self.right = dot(
            self.expand, dot(right_ref[...], take_d, precision=EXACT), precision=EXACT
        )

    def matrix(self):
        return dot(self.left, self.fac * self.right, 0, 0, precision=EXACT)


class KronBack:
    def __init__(self, kron, block, inner, left, fac, right):
        self.kron, self.block, self.inner = kron, block, inner
        self.left, self.fac, self.right = left, fac, right

    def place(self, of_lane, start):
        lane_in = iota((LANES, LANES), 0)
        keep = (lane_in < self.kron * self.inner) & (iota((LANES, LANES), 1) - start == of_lane(lane_in))
        return keep.astype(BF16)

    def back(self, grad, fac_at, right_at):
        grad = grad.astype(BF16)
        rows = self.kron * self.kron
        width = self.kron * self.block
        inner = dot(self.left.astype(BF16), grad)
        g_fac = dot((inner * self.right).astype(BF16), self.place(lambda n: n // self.inner, fac_at))
        expand = (iota((rows, self.kron), 0) // self.kron == iota((rows, self.kron), 1)).astype(BF16)
        same_i = dot(expand, (inner * self.fac).astype(BF16), 0, 0)
        g_right = dot(same_i.astype(BF16), self.place(lambda n: n % self.inner, right_at))
        outer = dot((self.fac * self.right).astype(BF16), grad, 1, 1)
        outer = outer * hot(iota((rows, width), 0) % self.kron, iota((rows, width), 1) // self.block)
        outer = dot(expand, outer.astype(BF16), 0, 0)
        g_left = sum(outer[:, n * self.block : (n + 1) * self.block] for n in range(self.kron))
        return g_fac, g_right, g_left


def my_mp():
    return lax.axis_index("mp")


def worked(mp):
    return jnp.where(mp < 2, 0, 2)


def gain_row(ref):
    return ref[...].astype(F32).reshape(1, ref.shape[0])


def slot_positions(mp):
    return (mp, mp ^ 2, mp ^ 1, mp ^ 3)


def pick_body(r):
    w = worked(my_mp())
    mover = Mover(r.sems)
    copies = [
        mover.start(r.x.at[2 - w], r.xf),
        mover.start(r.x.at[1], r.xc),
        mover.start(r.t.at[2 - w], r.tf),
    ]
    for copy in copies:
        copy.wait()


def normed(rows, gain):
    values = rows.astype(F32)
    return (values * rms(values) * gain).astype(BF16)


def prep_body(r):
    w = worked(my_mp())
    blk = r.x.shape[1]
    mover = Mover(r.sems)
    seq = 4 * blk
    edges = start_edges(r, mover, seq)
    copies = [
        mover.start(src, dst)
        for src, dst in (
            (r.x.at[w], r.rows.at[0:blk]),
            (r.x.at[1], r.rows.at[2 * blk : 3 * blk]),
            (r.m1.at[w], r.rows.at[blk : 2 * blk]),
            (r.m1.at[1], r.rows.at[3 * blk : 4 * blk]),
            (r.wk_hbm, r.wk),
            (r.wv_hbm, r.wv),
            (r.wq_hbm, r.wq),
        )
    ]
    down = Kron(r.fac_in, False, r.dl, r.dr)
    up = Kron(r.fac_in, True, r.ur, r.ul)
    for n, one in enumerate((down, up)):
        r.low[n] = one.matrix().astype(BF16)
        r.left[n] = one.left
        r.fac[n] = one.fac
        r.right[n] = one.right
    for copy in edges:
        copy.wait()
    fill_bias(r, bucket_hots(r, seq), blk)
    gain = gain_row(r.gain1)
    for copy in copies[:4]:
        copy.wait()
    for n in range(4):
        rows = slice(n * blk, (n + 1) * blk)
        r.xn[rows] = normed(r.rows[rows], gain)
    copies[4].wait()
    r.k[...] = dot(r.xn[...], r.wk[...]).astype(BF16)
    copies[5].wait()
    r.v[...] = dot(r.xn[...], r.wv[...]).astype(BF16)
    copies[6].wait()
    r.q[0:blk] = dot(r.xn[0:blk], r.wq[...]).astype(BF16)
    r.q[blk : 2 * blk] = dot(r.xn[2 * blk : 3 * blk], r.wq[...]).astype(BF16)


def start_edges(r, mover, seq):
    return [
        mover.start(r.bucket.at[row : row + 8], r.edge.at[n]) for n, row in enumerate((0, seq - 8))
    ]


def bucket_hots(r, seq):
    by_lane = jnp.concatenate([pltpu.roll(r.edge[1, 7:8, :], 1, 1), r.edge[0, 0:1, :]], axis=1)
    return hot(iota((r.table.shape[1], 2 * seq), 0), by_lane)


def fill_bias(r, buckets, blk):
    span = buckets.shape[1]
    by_distance = dot(r.table[...], buckets, precision=EXACT)
    for h in range(by_distance.shape[0]):
        row = by_distance[h : h + 1]
        near = pltpu.roll(
            jnp.broadcast_to(row[:, 2 * blk : 6 * blk], (blk, span // 2)),
            3 * blk,
            1,
            stride=1,
            stride_axis=0,
        )
        r.bias[h, :, 0 : 2 * blk] = jnp.broadcast_to(row[:, 1:2], (blk, 2 * blk))
        r.bias[h, :, 2 * blk : 5 * blk] = near[:, 0 : 3 * blk]
        r.bias[h, :, 5 * blk : 7 * blk] = jnp.broadcast_to(row[:, span - 1 : span], (blk, 2 * blk))


def key_masks(slots, length, blk):
    lane = iota((1, blk), 1)
    return [jnp.where(s * blk + lane < length, 0.0, -jnp.inf).astype(F32) for s in slots]


def by_head(rows):
    half = iota(rows.shape, 1) < HALF
    zero = jnp.zeros_like(rows)
    return jnp.concatenate([jnp.where(half, rows, zero), jnp.where(half, zero, rows)], axis=0)


def attend(hp, q, k, v, bias, mask, slots, q_poss, p, inv_out, ctx_out):
    count = len(q_poss)
    blk = q.shape[0] // count
    low_half = iota((blk, LANES), 1) < HALF
    scores = dot(by_head(q[...]), k[...], 1, 1)
    step = blk // 2
    for u in range(4 * count):
        h, b = divmod(u // 2, count)
        rows = slice(u * step, (u + 1) * step)
        q_rows = slice((u % 2) * step, (u % 2 + 1) * step)
        parts = []
        for n in range(4):
            place = pl.ds(pl.multiple_of((slots[n] - q_poss[b] + 3) * blk, blk), blk)
            parts.append(
                scores[rows, n * blk : (n + 1) * blk] + (bias[2 * hp + h, q_rows, place] + mask[n])
            )
        top = jnp.max(
            jnp.maximum(jnp.maximum(parts[0], parts[1]), jnp.maximum(parts[2], parts[3])),
            axis=-1,
            keepdims=True,
        )
        for n in range(4):
            p[rows, n * blk : (n + 1) * blk] = jnp.exp(parts[n] - top).astype(BF16)
    values = v[...]
    out = dot(p[...], jnp.concatenate([values, jnp.ones_like(values)], axis=1))
    inv_all = 1.0 / out[:, LANES:]
    out = out[:, 0:LANES]
    for b in range(count):
        rows = slice(b * blk, (b + 1) * blk)
        inv = jnp.where(
            low_half, inv_all[rows], inv_all[(count + b) * blk : (count + b + 1) * blk]
        )
        inv_out[rows] = inv
        mixed = jnp.where(
            low_half, out[rows], out[(count + b) * blk : (count + b + 1) * blk]
        )
        ctx_out[rows] = (mixed * inv).astype(BF16)


def attend_back(q, k, v, p, do, inv, ctx, count, dq_out, dkt_out, dvt_out):
    blk = q.shape[0] // count
    low_half = iota((blk, LANES), 1) < HALF
    do = by_head(do[...].astype(F32) * inv[...])
    ctx = ctx[...].astype(F32)
    delta = jnp.sum(do * jnp.concatenate([ctx, ctx], axis=0), axis=-1, keepdims=True)
    do = do.astype(BF16)
    dp = dot(do, v[...], 1, 1)
    ds = p[...].astype(F32) * (dp - delta)
    low = ds.astype(BF16)
    dq = dot(low, k[...])
    for b in range(count):
        rows = slice(b * blk, (b + 1) * blk)
        dq_out[rows] = jnp.where(
            low_half, dq[rows], dq[(count + b) * blk : (count + b + 1) * blk]
        ).astype(BF16)
    dkt_out[...] = dot(by_head(q[...]), low, 0, 0).astype(BF16)
    dvt_out[...] = dot(do, p[...], 0, 0).astype(BF16)
    return ds


def main_body(r):
    mp = my_mp()
    w = worked(mp)
    slots = slot_positions(mp)
    blk, width = r.wf.shape
    seq = 4 * blk
    heads = r.table.shape[0]
    pairs = width // LANES
    ffw = r.win.shape[1]
    at = lambda n: slice(n * blk, (n + 1) * blk)
    mover = Mover(r.sems)
    go = lambda pairs_of: [mover.start(src, dst) for src, dst in pairs_of]
    edges = start_edges(r, mover, seq)
    far_rows = go(
        (
            (r.wf, r.rows.at[at(1)]),
            (r.mf, r.rows.at[at(3)]),
            (r.cx, r.rows.at[at(5)]),
            (r.mc, r.rows.at[at(7)]),
        )
    )
    weights_kv = go(((r.wk_hbm, r.wk), (r.wv_hbm, r.wv), (r.wq_hbm, r.wq)))
    toeplitz = mover.start(r.bias_hbm, r.bias)
    shared = go(
        (
            (r.q0.at[at(0)], r.q_s.at[at(0)]),
            (r.k0.at[at(0)], r.k_s.at[at(0)]),
            (r.v0.at[at(0)], r.v_s.at[at(0)]),
            (r.k0.at[at(1)], r.k_s.at[at(2)]),
            (r.v0.at[at(1)], r.v_s.at[at(2)]),
            (r.q0.at[at(1)], r.q_s.at[at(2)]),
            (r.k0.at[at(2)], r.k_s.at[at(4)]),
            (r.v0.at[at(2)], r.v_s.at[at(4)]),
            (r.k0.at[at(3)], r.k_s.at[at(6)]),
            (r.v0.at[at(3)], r.v_s.at[at(6)]),
        )
    )
    gain1 = gain_row(r.gain1)
    gain2 = gain_row(r.gain2)

    for copy in edges:
        copy.wait()
    buckets = bucket_hots(r, seq)
    for n in range(4):
        far_rows[n].wait()
        r.far[at(n)] = normed(r.rows[at(2 * n + 1)], gain1)
    for copy, weight, dst in ((weights_kv[0], r.wk, r.k_s), (weights_kv[1], r.wv, r.v_s)):
        copy.wait()
        every = dot(r.far[...], weight[...]).astype(BF16)
        for n in range(4):
            dst[at(2 * n + 1)] = every[at(n)]
    own_rows = go(((r.x.at[w], r.rows.at[at(0)]), (r.x.at[1], r.rows.at[at(4)])))
    weight_o = mover.start(r.wo_hbm, r.wo)
    weight_in = mover.start(r.win_hbm, r.win)
    weight_out = mover.start(r.wout_hbm, r.wout)
    goals = go(
        (
            (r.t.at[w], r.goal.at[at(0)]),
            (r.tf, r.goal.at[at(1)]),
            (r.t.at[1], r.goal.at[at(2)]),
        )
    )
    late = go(
        (
            (r.m1.at[w], r.rows.at[at(2)]),
            (r.m1.at[1], r.rows.at[at(6)]),
        )
    )
    weights_kv[2].wait()
    r.q_s[at(1)] = dot(r.far[at(0)], r.wq[...]).astype(BF16)
    for copy in shared:
        copy.wait()
    toeplitz.wait()
    masks = [key_masks(slots, r.lengths[n], blk) for n in (w, 1)]
    groups = (
        (slice(0, 2 * blk), (mp, mp ^ 2), slice(0, seq), r.pw_s),
        (at(2), (mp,), slice(seq, 2 * seq), r.pc_s),
    )
    for hp in range(pairs):
        cols = slice(hp * LANES, (hp + 1) * LANES)
        for (q_rows, q_poss, k_rows, p), mask in zip(groups, masks):
            attend(
                hp,
                r.q_s.at[q_rows, cols],
                r.k_s.at[k_rows, cols],
                r.v_s.at[k_rows, cols],
                r.bias,
                mask,
                slots,
                q_poss,
                p.at[hp],
                r.inv_s.at[q_rows, cols],
                r.ctx_s.at[q_rows, cols],
            )

    acc = r.bias
    acc[...] = jnp.zeros_like(acc)

    tokens = 3 * blk
    for copy in own_rows:
        copy.wait()
    own = jnp.concatenate([r.rows[0 : 2 * blk], r.rows[at(4)]], axis=0).astype(F32)
    weight_o.wait()
    residual = own + dot(r.ctx_s[...], r.wo[...])
    r.res[...] = residual
    inv2 = rms(residual)
    r.xn[...] = (residual * inv2 * gain2).astype(BF16)
    weight_in.wait()
    weight_out.wait()
    chunk = 512
    chunks = [slice(n * chunk, (n + 1) * chunk) for n in range(ffw // chunk)]
    pre = dot(r.xn[...], r.win[:, chunks[0]])
    total = None
    for n, cols in enumerate(chunks):
        ahead = dot(r.xn[...], r.win[:, chunks[n + 1]]) if n + 1 < len(chunks) else None
        value, slope = gelu_pair(pre)
        value = value.astype(BF16)
        r.slope[:, cols] = slope.astype(BF16)
        part = dot(value, r.wout[cols, :])
        total = part if total is None else total + part
        pre = ahead
    r.ffn[...] = total.astype(BF16)

    down_low = r.low[0]
    up_low = r.low[1]
    ffn = r.ffn[...]
    activated, act_slope = gelu_pair(dot(ffn, down_low))
    activated = activated.astype(BF16)
    final = r.res[...] + ffn.astype(F32) + dot(activated, up_low, 1, 1)
    r.blk_s[...] = final.astype(BF16)
    out = go(
        (
            (r.blk_s.at[at(1)], r.blk_f),
            (r.blk_s.at[at(0)], r.blk_own.at[0]),
            (r.blk_s.at[at(2)], r.blk_own.at[1]),
        )
    )
    row = iota((blk, 1), 0)
    valid = jnp.concatenate(
        [
            pos * blk + row < length
            for pos, length in ((mp, r.lengths[w]), (mp ^ 2, r.lengths[w]), (mp, r.lengths[1]))
        ],
        axis=0,
    )
    for copy in goals:
        copy.wait()
    err = jnp.where(valid, final - r.goal[...].astype(F32), 0.0)
    r.err[...] = err
    loss = 0.5 * jnp.sum(jnp.sum(err * err, axis=0, keepdims=True), axis=1, keepdims=True)
    g_adapter = err.astype(BF16)
    grad_up = dot(g_adapter, activated, 0, 0)
    g_squeezed = (dot(g_adapter, up_low) * act_slope).astype(BF16)
    grad_down = dot(ffn, g_squeezed, 0, 0)
    kron, block, inner = r.shape_kron
    backs = [
        KronBack(kron, block, inner, r.left[n], r.fac[n], r.right[n]).back(grad, *PACK_KRON[n])
        for n, grad in enumerate((grad_down, grad_up))
    ]
    r.ffn[...] = (err + dot(g_squeezed, down_low, 1, 1)).astype(BF16)

    for n in range(ffw // chunk):
        cols = slice(n * chunk, (n + 1) * chunk)
        r.hid[:, cols] = (dot(r.ffn[...], r.wout[cols, :], 1, 1) * r.slope[:, cols].astype(F32)).astype(
            BF16
        )
    g_normed = jnp.concatenate(
        [dot(r.hid[...], r.win[n * 256 : (n + 1) * 256, :], 1, 1) for n in range(width // 256)],
        axis=1,
    )
    residual = r.res[...]
    inv2 = rms(residual)
    g2 = jnp.sum(g_normed * residual * inv2, axis=0, keepdims=True)
    weighted = g_normed * gain2
    mean = jnp.mean(weighted * residual, axis=-1, keepdims=True)
    g_res = r.err[...] + inv2 * weighted - residual * (inv2 * inv2 * inv2 * mean)
    r.err[...] = g_res
    r.do[...] = dot(g_res.astype(BF16), r.wo[...], 1, 1).astype(BF16)

    for hp in range(pairs):
        cols = slice(hp * LANES, (hp + 1) * LANES)
        scores = []
        for q_rows, q_poss, k_rows, p in groups:
            scores.append(
                attend_back(
                    r.q_s.at[q_rows, cols],
                    r.k_s.at[k_rows, cols],
                    r.v_s.at[k_rows, cols],
                    p.at[hp],
                    r.do.at[q_rows, cols],
                    r.inv_s.at[q_rows, cols],
                    r.ctx_s.at[q_rows, cols],
                    len(q_poss),
                    r.dq.at[q_rows, cols],
                    r.dkt.at[cols, k_rows],
                    r.dvt.at[cols, k_rows],
                )
            )
        for h in range(2):
            near = scores[0][2 * h * blk : (2 * h + 1) * blk] + scores[1][h * blk : (h + 1) * blk]
            far = scores[0][(2 * h + 1) * blk : (2 * h + 2) * blk]
            for piece, q_pos, away in ((near, mp, 1), (far, mp ^ 2, 0)):
                for n in range(4):
                    place = pl.ds(pl.multiple_of((slots[n] - q_pos + 3) * blk, blk), blk)
                    add = piece[:, n * blk : (n + 1) * blk]
                    if n == away:
                        acc[2 * hp + h, 0:8, place] += jnp.sum(
                            add.reshape(blk // 8, 8, blk), axis=0
                        )
                    else:
                        acc[2 * hp + h, :, place] += add

    sub = iota((8, seq), 0)

    def along_diagonals(h):
        total = jnp.zeros((8, seq), F32)
        for g in range(blk // 8):
            near = jnp.concatenate(
                [acc[h, 8 * g : 8 * g + 8, 2 * blk : 5 * blk], jnp.zeros((8, blk), F32)], axis=1
            )
            total = total + pltpu.roll(near, blk - 8 * g, 1)
        for bit in (1, 2, 4):
            total = jnp.where((sub & bit) > 0, pltpu.roll(total, seq - bit, 1), total)
        near = jnp.sum(total, axis=0, keepdims=True)
        below = jnp.sum(acc[h, :, 0 : 2 * blk], axis=0, keepdims=True)
        above = jnp.sum(acc[h, :, 5 * blk : 7 * blk], axis=0, keepdims=True)
        return jnp.concatenate(
            [
                jnp.zeros((1, blk), F32),
                below[:, 0:blk],
                below[:, blk : 2 * blk] + near[:, 0:blk],
                near[:, blk:seq],
                above,
            ],
            axis=1,
        )

    for copy in late:
        copy.wait()
    sums = []
    g1 = jnp.zeros((1, width), F32)
    side = 256
    for first, dq_rows in ((0, slice(0, 2 * blk)), (4, at(2))):
        cols = slice(first * blk, first * blk + seq)
        pieces = []
        dk = r.dkt[:, cols].T
        dv = r.dvt[:, cols].T
        for n in range(width // side):
            outs = slice(n * side, (n + 1) * side)
            piece = dot(dk, r.wk[outs, :], 1, 1)
            if len(sums) < heads:
                sums.append(along_diagonals(len(sums)))
            piece = piece + dot(dv, r.wv[outs, :], 1, 1)
            if len(sums) < heads:
                sums.append(along_diagonals(len(sums)))
            pieces.append(piece)
        parts = jnp.concatenate(pieces, axis=1)
        own = dot(r.dq[dq_rows], r.wq[...], 1, 1)
        for n in range(4):
            part = parts[at(n)]
            if n * blk < own.shape[0]:
                part = part + own[at(n)]
            values = r.rows[at(first + n)].astype(F32)
            inv1 = rms(values)
            scaled = part * values
            g1 = g1 + jnp.sum(scaled * inv1, axis=0, keepdims=True)
            mean = jnp.mean(scaled * gain1, axis=-1, keepdims=True)
            back = inv1 * (part * gain1) - values * (inv1 * inv1 * inv1 * mean)
            if n < 2:
                m = n if first == 0 else 2 + n
                if m < 3:
                    back = back + r.err[at(m)]
                r.base_s[at(m)] = back
                out += go(((r.base_s.at[at(m)], r.base.at[m]),))
            else:
                m = n - 2 if first == 0 else n
                r.send_s[at(m)] = back.astype(BF16)
                out += go(((r.send_s.at[at(m)], r.send.at[m]),))
    for h in range(len(sums), heads):
        sums.append(along_diagonals(h))
    g_table = dot(jnp.concatenate(sums, axis=0), buckets, 1, 1, precision=EXACT)

    (gf_d, g_dr, g_dl), (gf_u, g_ul, g_ur) = backs
    row16 = iota((16, LANES), 0)
    lane16 = iota((16, LANES), 1)
    pack = r.pack
    pack[0:16] = gf_d + gf_u
    pack[0:4] += g_dr + g_ul
    pack[0:heads, 0 : r.table.shape[1]] = g_table
    pack[0:4, HALF:LANES] = g_dl[:, 0:HALF]
    pack[4:8, HALF:LANES] = g_dl[:, HALF : 2 * HALF]
    pack[8:12, HALF:LANES] = g_dl[:, 2 * HALF : 3 * HALF]
    pack[12:16, HALF:LANES] = g_ur[:, 0:HALF]
    pack[16:20] = g_ur[:, HALF : 3 * HALF]
    for n in range(width // LANES):
        pack[20 + n : 21 + n] = g1[:, n * LANES : (n + 1) * LANES]
        pack[26 + n : 27 + n] = g2[:, n * LANES : (n + 1) * LANES]
    real = (r.lengths[0] + r.lengths[1] + r.lengths[2]).astype(F32)
    both = jnp.where(lane16 < 2, loss, real)
    high = both.astype(BF16).astype(F32)
    both = jnp.where(lane16 % 2 == 0, high, both - high)
    r.small[0:16] = jnp.where((row16 == 15) & (lane16 < 4), both, pack[0:16]).astype(BF16)
    r.small[16:32] = pack[16:32].astype(BF16)
    for copy in out:
        copy.wait()


PACK_KRON = ((32, 40), (36, 52))


def middle_body(r):
    mover = Mover(r.sems)
    copies = [
        mover.start(src, dst)
        for src, dst in (
            (r.base.at[1], r.base_s.at[0]),
            (r.recv.at[1], r.recv_s.at[0]),
            (r.base.at[3], r.base_s.at[1]),
            (r.recv.at[3], r.recv_s.at[1]),
        )
    ]
    spread = r.small.shape[0] // 2
    first = pl.multiple_of((my_mp() % 2) * spread, spread)
    half = r.small[pl.ds(first, spread)].astype(F32) + r.others[pl.ds(first, spread)].astype(F32)
    row = iota(half.shape, 0)
    lane = iota(half.shape, 1)
    even = lane % 2 == 0
    whole = half + jnp.where(even, pltpu.roll(half, LANES - 1, 1), pltpu.roll(half, 1, 1))
    high = whole.astype(BF16).astype(F32)
    parted = (row == 15) & (lane < 4) & (my_mp() % 2 == 0)
    half = jnp.where(parted, jnp.where(even, high, whole - high), half).astype(BF16)
    for n in range(r.spread.shape[0]):
        r.spread[n] = half
    for n in range(2):
        copies[2 * n].wait()
        copies[2 * n + 1].wait()
        r.away[n] = (r.base_s[n] + r.recv_s[n].astype(F32)).astype(BF16)


def finish_body(token_total, seq_total, r):
    w = worked(my_mp())
    width = r.grad.shape[2]
    mover = Mover(r.sems)
    copies = [
        mover.start(src, dst)
        for src, dst in (
            (r.gathered, r.gathered_s),
            (r.back.at[0], r.back_s.at[0]),
            (r.back.at[1], r.back_s.at[1]),
            (r.base.at[0], r.base_s.at[0]),
            (r.recv.at[0], r.recv_s.at[0]),
            (r.base.at[2], r.base_s.at[1]),
            (r.recv.at[2], r.recv_s.at[1]),
            (r.blk_f, r.block.at[2 - w]),
            (r.blk_own.at[0], r.block.at[w]),
            (r.blk_own.at[1], r.block.at[1]),
        )
    ]
    copies[0].wait()
    halves = [r.gathered_s[n].astype(F32) for n in range(2)]
    for n in range(2, r.gathered_s.shape[0]):
        halves[n % 2] = halves[n % 2] + r.gathered_s[n].astype(F32)
    total = jnp.concatenate(halves, axis=0)
    tail = total[15:16, 0:4]
    count = (tail[:, 2:3] + tail[:, 3:4]) * 0.25
    scale = token_total / count
    params = [r.dl, r.dr, r.ul, r.ur]
    squares = [jnp.sum(r.fac[n] * r.fac[n], keepdims=True) for n in range(r.fac.shape[0])]
    squares += [jnp.sum(p[...] * p[...], keepdims=True) for p in params]
    penalty = 0.5 * seq_total * sum(squares)
    r.loss[...] = (scale * (tail[:, 0:1] + tail[:, 1:2]) + penalty) / (token_total * width)

    heads, buckets = r.g_table.shape
    r.g_table[...] = scale * total[0:heads, 0:buckets]
    kron = r.fac.shape[0]
    for i in range(kron):
        rows = slice(i * kron, (i + 1) * kron)
        r.g_fac[i] = (
            scale * (total[rows, 32 : 32 + kron] + total[rows, 36 : 36 + kron].T)
            + seq_total * r.fac[i]
        )
    r.g_dr[...] = scale * total[0:4, 40:52] + seq_total * r.dr[...]
    r.g_ul[...] = scale * total[0:4, 52:64] + seq_total * r.ul[...]
    g_dl = jnp.concatenate([total[4 * n : 4 * n + 4, HALF:LANES] for n in range(3)], axis=1)
    r.g_dl[...] = scale * g_dl + seq_total * r.dl[...]
    g_ur = jnp.concatenate([total[12:16, HALF:LANES], total[16:20]], axis=1)
    r.g_ur[...] = scale * g_ur + seq_total * r.ur[...]
    for n in range(width // LANES):
        r.g1[n : n + 1] = scale * total[20 + n : 21 + n]
        r.g2[n : n + 1] = scale * total[26 + n : 27 + n]

    for copy in copies[1:]:
        copy.wait()
    r.grad[2 - w] = scale * r.back_s[0].astype(F32)
    r.grad[w] = scale * (r.base_s[0] + r.recv_s[0].astype(F32))
    r.grad[1] = scale * (r.base_s[1] + r.recv_s[1].astype(F32) + r.back_s[1].astype(F32))


def local(
    layer_input,
    targets,
    attn_gain,
    ffn_gain,
    query_matrix,
    key_matrix,
    value_matrix,
    attention_output_weight,
    feedforward_input_weight,
    feedforward_output_weight,
    bias_table,
    factors,
    down_left,
    down_right,
    up_left,
    up_right,
    lengths,
    relative_bucket,
):
    seqs, blk, width = layer_input.shape
    mp_size = lax.axis_size("mp")
    axes = ("dp", "mp")
    devices = lax.axis_size("dp") * mp_size
    heads = bias_table.shape[1]
    ffw = feedforward_input_weight.shape[1]
    kron = factors.shape[0]
    seq_total = lax.axis_size("dp") * seqs
    token_total = seq_total * blk * mp_size
    assert seqs == 3 and mp_size == 4
    core = [(i, i ^ 1) for i in range(mp_size)]
    chip = [(i, i ^ 2) for i in range(mp_size)]
    pairs = heads // 2
    seq = blk * mp_size
    table = bias_table.T
    square = ((width, width), BF16)
    rows = lambda n, dtype=BF16: ((n * blk, width), dtype)

    picked = call(
        "pick",
        pick_body,
        [("x", layer_input, HBM), ("t", targets, HBM)],
        [(n, (blk, width), BF16, VMEM) for n in ("xf", "xc", "tf")],
        {},
        3,
    )
    wf = lax.ppermute(picked.xf, "mp", chip)
    cx = lax.ppermute(picked.xc, "mp", chip)
    tf = lax.ppermute(picked.tf, "mp", chip)
    m1 = lax.ppermute(layer_input, "mp", core)
    prep = call(
        "prep",
        prep_body,
        [
            ("x", layer_input, HBM),
            ("m1", m1, HBM),
            ("gain1", attn_gain, VMEM),
            ("fac_in", factors, VMEM),
            ("dl", down_left, VMEM),
            ("dr", down_right, VMEM),
            ("ul", up_left, VMEM),
            ("ur", up_right, VMEM),
            ("table", table, VMEM),
            ("bucket", relative_bucket, HBM),
            ("wq_hbm", query_matrix, HBM),
            ("wk_hbm", key_matrix, HBM),
            ("wv_hbm", value_matrix, HBM),
        ],
        [
            ("q",) + rows(2) + (VMEM,),
            ("k",) + rows(4) + (VMEM,),
            ("v",) + rows(4) + (VMEM,),
            ("low", (2, width, LANES), BF16, VMEM),
            ("left", (2, kron * kron, width), F32, VMEM),
            ("fac", (2, kron * kron, LANES), F32, VMEM),
            ("right", (2, kron * kron, LANES), F32, VMEM),
            ("bias", (heads, blk, 7 * blk), F32, VMEM),
        ],
        {"edge": ((2, 8, seq), jnp.int32), "rows": rows(4), "xn": rows(4), "wq": square, "wk": square, "wv": square},
        9,
        4.0,
    )

    wf, cx, prep.k = lax.optimization_barrier((wf, cx, prep.k))
    mf = lax.ppermute(wf, "mp", core)
    mc = lax.ppermute(cx, "mp", core)

    def main_with_shape(r):
        r.shape_kron = (kron, down_left.shape[1], down_right.shape[1])
        main_body(r)

    main = call(
        "main",
        main_with_shape,
        [
            ("lengths", lengths, SMEM),
            ("x", layer_input, HBM),
            ("t", targets, HBM),
            ("wf", wf, HBM),
            ("cx", cx, HBM),
            ("tf", tf, HBM),
            ("m1", m1, HBM),
            ("mf", mf, HBM),
            ("mc", mc, HBM),
            ("gain1", attn_gain, VMEM),
            ("gain2", ffn_gain, VMEM),
            ("table", table, VMEM),
            ("bucket", relative_bucket, HBM),
            ("bias_hbm", prep.bias, HBM),
            ("low", prep.low, VMEM),
            ("left", prep.left, VMEM),
            ("fac", prep.fac, VMEM),
            ("right", prep.right, VMEM),
            ("q0", prep.q, HBM),
            ("k0", prep.k, HBM),
            ("v0", prep.v, HBM),
            ("wq_hbm", query_matrix, HBM),
            ("wk_hbm", key_matrix, HBM),
            ("wv_hbm", value_matrix, HBM),
            ("wo_hbm", attention_output_weight, HBM),
            ("win_hbm", feedforward_input_weight, HBM),
            ("wout_hbm", feedforward_output_weight, HBM),
        ],
        [
            ("blk_own", (2, blk, width), BF16, HBM),
            ("blk_f", (blk, width), BF16, HBM),
            ("base", (4, blk, width), F32, HBM),
            ("send", (4, blk, width), BF16, HBM),
            ("small", (32, LANES), BF16, VMEM),
        ],
        {
            "wq": square,
            "wk": square,
            "wv": square,
            "wo": square,
            "win": ((width, ffw), BF16),
            "wout": ((ffw, width), BF16),
            "edge": ((2, 8, seq), jnp.int32),
            "rows": rows(8),
            "goal": rows(3),
            "xn": rows(3),
            "q_s": rows(3),
            "k_s": rows(8),
            "v_s": rows(8),
            "far": rows(4),
            "bias": ((heads, blk, 7 * blk), F32),
            "pack": ((32, LANES), F32),
            "pw_s": ((pairs, seq, seq), BF16),
            "pc_s": ((pairs, 2 * blk, seq), BF16),
            "ctx_s": rows(3),
            "inv_s": rows(3, F32),
            "res": rows(3, F32),
            "hid": ((3 * blk, ffw), BF16),
            "slope": ((3 * blk, ffw), BF16),
            "ffn": rows(3),
            "err": rows(3, F32),
            "do": rows(3),
            "dq": rows(3),
            "dkt": ((width, 2 * seq), BF16),
            "dvt": ((width, 2 * seq), BF16),
            "blk_s": rows(3),
            "base_s": rows(4, F32),
            "send_s": rows(4),
        },
        45,
        28.0,
    )
    recv = lax.ppermute(main.send, "mp", core)
    others = lax.ppermute(main.small, "mp", core)
    pair = lambda dtype: ((2, blk, width), dtype)
    middle = call(
        "middle",
        middle_body,
        [("base", main.base, HBM), ("recv", recv, HBM), ("small", main.small, VMEM), ("others", others, VMEM)],
        [("away", (2, blk, width), BF16, VMEM), ("spread", (devices, 16, LANES), BF16, VMEM)],
        {"base_s": pair(F32), "recv_s": pair(BF16)},
        4,
    )
    back = lax.ppermute(middle.away, "mp", chip)
    blk_f = lax.ppermute(main.blk_f, "mp", chip)
    spread, blk_f = lax.optimization_barrier((middle.spread, blk_f))
    gathered = lax.all_to_all(spread, axes, split_axis=0, concat_axis=0, tiled=True)

    done = call(
        "finish",
        functools.partial(finish_body, float(token_total), float(seq_total)),
        [
            ("gathered", gathered, HBM),
            ("base", main.base, HBM),
            ("recv", recv, HBM),
            ("back", back, HBM),
            ("blk_own", main.blk_own, HBM),
            ("blk_f", blk_f, HBM),
            ("fac", factors, VMEM),
            ("dl", down_left, VMEM),
            ("dr", down_right, VMEM),
            ("ul", up_left, VMEM),
            ("ur", up_right, VMEM),
        ],
        [
            ("loss", (1, 1), F32, VMEM),
            ("block", (seqs, blk, width), BF16, VMEM),
            ("grad", (seqs, blk, width), F32, VMEM),
            ("g1", (width // LANES, LANES), F32, VMEM),
            ("g2", (width // LANES, LANES), F32, VMEM),
            ("g_table", table.shape, F32, VMEM),
            ("g_fac", factors.shape, F32, VMEM),
            ("g_dl", down_left.shape, F32, VMEM),
            ("g_dr", down_right.shape, F32, VMEM),
            ("g_ul", up_left.shape, F32, VMEM),
            ("g_ur", up_right.shape, F32, VMEM),
        ],
        {
            "gathered_s": ((devices, 16, LANES), BF16),
            "back_s": pair(BF16),
            "base_s": pair(F32),
            "recv_s": pair(BF16),
        },
        10,
    )
    return (
        done.loss.reshape(()),
        done.block,
        done.grad,
        done.g1.reshape(width),
        done.g2.reshape(width),
        done.g_table.T,
        done.g_fac,
        done.g_dl,
        done.g_dr,
        done.g_ul,
        done.g_ur,
    )


def solution(mesh):
    rows = P("dp", "mp", None)
    return jax.shard_map(
        local,
        mesh=mesh,
        in_specs=(rows, rows) + (P(),) * 14 + (P("dp"), P()),
        out_specs=(P(), rows, rows) + (P(),) * 8,
        check_vma=False,
    )
```

```python
import functools
from types import SimpleNamespace

import jax
import jax.numpy as jnp
from jax import lax
from jax.experimental import pallas as pl
from jax.experimental.pallas import tpu as pltpu
from jax.sharding import PartitionSpec as P

EPSILON = 1e-06
F32 = jnp.float32
BF16 = jnp.bfloat16
EXACT = lax.Precision.HIGHEST
GELU_A = 0.7978845608028654
GELU_B = 0.044715
LANES = 128
HALF = LANES // 2
VMEM_BYTES = 64 * 2**20 - 2**17
HBM = pltpu.HBM
VMEM = pltpu.VMEM
SMEM = pltpu.SMEM


def dot(a, b, ca=1, cb=0, precision=None):
    return lax.dot_general(
        a, b, (((ca,), (cb,)), ((), ())), preferred_element_type=F32, precision=precision
    )


def iota(shape, dim):
    return lax.broadcasted_iota(jnp.int32, shape, dim)


def rms(values):
    return lax.rsqrt(jnp.mean(values * values, axis=-1, keepdims=True) + EPSILON)


def gelu_pair(v):
    square = v * v
    w = 1.0 + jnp.tanh(v * (GELU_A + (GELU_A * GELU_B) * square))
    half = 0.5 * v
    slope = w * (0.5 + half * (2.0 - w) * (GELU_A + (3.0 * GELU_A * GELU_B) * square))
    return half * w, slope


def hot(left, right):
    return (left == right).astype(F32)


class Mover:
    def __init__(self, sems):
        self.sems = sems
        self.used = 0

    def start(self, src, dst):
        copy = pltpu.make_async_copy(src, dst, self.sems.at[self.used])
        self.used += 1
        copy.start()
        return copy


def call(name, body, ins, outs, scratch, sems, cost_us=None):
    names = [n for n, _, _ in ins] + [n for n, _, _, _ in outs] + list(scratch) + ["sems"]

    def kernel(*refs):
        body(SimpleNamespace(**dict(zip(names, refs))))

    results = pl.pallas_call(
        kernel,
        out_shape=[jax.ShapeDtypeStruct(shape, dtype) for _, shape, dtype, _ in outs],
        in_specs=[pl.BlockSpec(memory_space=space) for _, _, space in ins],
        out_specs=[pl.BlockSpec(memory_space=space) for _, _, _, space in outs],
        scratch_shapes=[pltpu.VMEM(shape, dtype) for shape, dtype in scratch.values()]
        + [pltpu.SemaphoreType.DMA((max(sems, 1),))],
        compiler_params=pltpu.CompilerParams(vmem_limit_bytes=VMEM_BYTES),
        cost_estimate=None
        if cost_us is None
        else pl.CostEstimate(flops=int(cost_us * 1e9), bytes_accessed=0, transcendentals=0),
        name=name,
    )(*[array for _, array, _ in ins])
    return SimpleNamespace(**dict(zip([o[0] for o in outs], results)))


def factor_rows(fac_ref, transposed):
    kron = fac_ref.shape[0]
    pieces = [fac_ref[i].T if transposed else fac_ref[i] for i in range(kron)]
    return jnp.concatenate(pieces, axis=0)


class Kron:
    def __init__(self, fac_ref, transposed, left_ref, right_ref):
        kron = left_ref.shape[0]
        self.block = left_ref.shape[1]
        self.inner = right_ref.shape[1]
        self.kron = kron
        width = kron * self.block
        rows = kron * kron
        inner = self.inner
        self.expand = hot(iota((rows, kron), 0) // kron, iota((rows, kron), 1))
        take_c = hot(iota((kron, LANES), 0), iota((kron, LANES), 1) // inner)
        lane_d = iota((inner, LANES), 1)
        take_d = jnp.where(
            lane_d < kron * inner, hot(iota((inner, LANES), 0), lane_d % inner), 0.0
        )
        self.same_a = hot(iota((rows, width), 0) % kron, iota((rows, width), 1) // self.block)
        wide_left = jnp.concatenate([left_ref[...]] * kron, axis=1)
        self.left = dot(self.expand, wide_left, precision=EXACT) * self.same_a
        self.fac = dot(factor_rows(fac_ref, transposed), take_c, precision=EXACT)
        self.right = dot(
            self.expand, dot(right_ref[...], take_d, precision=EXACT), precision=EXACT
        )

    def matrix(self):
        return dot(self.left, self.fac * self.right, 0, 0, precision=EXACT)


class KronBack:
    def __init__(self, kron, block, inner, left, fac, right):
        self.kron, self.block, self.inner = kron, block, inner
        self.left, self.fac, self.right = left, fac, right

    def place(self, of_lane, start):
        lane_in = iota((LANES, LANES), 0)
        keep = (lane_in < self.kron * self.inner) & (iota((LANES, LANES), 1) - start == of_lane(lane_in))
        return keep.astype(BF16)

    def back(self, grad, fac_at, right_at):
        grad = grad.astype(BF16)
        rows = self.kron * self.kron
        width = self.kron * self.block
        inner = dot(self.left.astype(BF16), grad)
        g_fac = dot((inner * self.right).astype(BF16), self.place(lambda n: n // self.inner, fac_at))
        expand = (iota((rows, self.kron), 0) // self.kron == iota((rows, self.kron), 1)).astype(BF16)
        same_i = dot(expand, (inner * self.fac).astype(BF16), 0, 0)
        g_right = dot(same_i.astype(BF16), self.place(lambda n: n % self.inner, right_at))
        outer = dot((self.fac * self.right).astype(BF16), grad, 1, 1)
        outer = outer * hot(iota((rows, width), 0) % self.kron, iota((rows, width), 1) // self.block)
        outer = dot(expand, outer.astype(BF16), 0, 0)
        g_left = sum(outer[:, n * self.block : (n + 1) * self.block] for n in range(self.kron))
        return g_fac, g_right, g_left


def my_mp():
    return lax.axis_index("mp")


def worked(mp):
    return jnp.where(mp < 2, 0, 2)


def gain_row(ref):
    return ref[...].astype(F32).reshape(1, ref.shape[0])


def slot_positions(mp):
    return (mp, mp ^ 2, mp ^ 1, mp ^ 3)


def pick_body(r):
    w = worked(my_mp())
    mover = Mover(r.sems)
    copies = [
        mover.start(r.x.at[2 - w], r.xf),
        mover.start(r.x.at[1], r.xc),
        mover.start(r.t.at[2 - w], r.tf),
    ]
    for copy in copies:
        copy.wait()


def normed(rows, gain):
    values = rows.astype(F32)
    return (values * rms(values) * gain).astype(BF16)


def prep_body(r):
    w = worked(my_mp())
    blk = r.x.shape[1]
    mover = Mover(r.sems)
    seq = 4 * blk
    edges = start_edges(r, mover, seq)
    copies = [
        mover.start(src, dst)
        for src, dst in (
            (r.x.at[w], r.rows.at[0:blk]),
            (r.x.at[1], r.rows.at[2 * blk : 3 * blk]),
            (r.m1.at[w], r.rows.at[blk : 2 * blk]),
            (r.m1.at[1], r.rows.at[3 * blk : 4 * blk]),
            (r.wk_hbm, r.wk),
            (r.wv_hbm, r.wv),
            (r.wq_hbm, r.wq),
        )
    ]
    down = Kron(r.fac_in, False, r.dl, r.dr)
    up = Kron(r.fac_in, True, r.ur, r.ul)
    for n, one in enumerate((down, up)):
        r.low[n] = one.matrix().astype(BF16)
        r.left[n] = one.left
        r.fac[n] = one.fac
        r.right[n] = one.right
    for copy in edges:
        copy.wait()
    fill_bias(r, bucket_hots(r, seq), blk)
    gain = gain_row(r.gain1)
    for copy in copies[:4]:
        copy.wait()
    for n in range(4):
        rows = slice(n * blk, (n + 1) * blk)
        r.xn[rows] = normed(r.rows[rows], gain)
    copies[4].wait()
    r.k[...] = dot(r.xn[...], r.wk[...]).astype(BF16)
    copies[5].wait()
    r.v[...] = dot(r.xn[...], r.wv[...]).astype(BF16)
    copies[6].wait()
    r.q[0:blk] = dot(r.xn[0:blk], r.wq[...]).astype(BF16)
    r.q[blk : 2 * blk] = dot(r.xn[2 * blk : 3 * blk], r.wq[...]).astype(BF16)


def start_edges(r, mover, seq):
    return [
        mover.start(r.bucket.at[row : row + 8], r.edge.at[n]) for n, row in enumerate((0, seq - 8))
    ]


def bucket_hots(r, seq):
    by_lane = jnp.concatenate([pltpu.roll(r.edge[1, 7:8, :], 1, 1), r.edge[0, 0:1, :]], axis=1)
    return hot(iota((r.table.shape[1], 2 * seq), 0), by_lane)


def fill_bias(r, buckets, blk):
    span = buckets.shape[1]
    by_distance = dot(r.table[...], buckets, precision=EXACT)
    for h in range(by_distance.shape[0]):
        row = by_distance[h : h + 1]
        near = pltpu.roll(
            jnp.broadcast_to(row[:, 2 * blk : 6 * blk], (blk, span // 2)),
            3 * blk,
            1,
            stride=1,
            stride_axis=0,
        )
        r.bias[h, :, 0 : 2 * blk] = jnp.broadcast_to(row[:, 1:2], (blk, 2 * blk))
        r.bias[h, :, 2 * blk : 5 * blk] = near[:, 0 : 3 * blk]
        r.bias[h, :, 5 * blk : 7 * blk] = jnp.broadcast_to(row[:, span - 1 : span], (blk, 2 * blk))


def key_masks(slots, length, blk):
    lane = iota((1, blk), 1)
    return [jnp.where(s * blk + lane < length, 0.0, -jnp.inf).astype(F32) for s in slots]


def by_head(rows):
    half = iota(rows.shape, 1) < HALF
    zero = jnp.zeros_like(rows)
    return jnp.concatenate([jnp.where(half, rows, zero), jnp.where(half, zero, rows)], axis=0)


def attend(hp, q, k, v, bias, mask, slots, q_poss, p, inv_out, ctx_out):
    count = len(q_poss)
    blk = q.shape[0] // count
    low_half = iota((blk, LANES), 1) < HALF
    scores = dot(by_head(q[...]), k[...], 1, 1)
    step = blk // 2
    for u in range(4 * count):
        h, b = divmod(u // 2, count)
        rows = slice(u * step, (u + 1) * step)
        q_rows = slice((u % 2) * step, (u % 2 + 1) * step)
        parts = []
        for n in range(4):
            place = pl.ds(pl.multiple_of((slots[n] - q_poss[b] + 3) * blk, blk), blk)
            parts.append(
                scores[rows, n * blk : (n + 1) * blk] + (bias[2 * hp + h, q_rows, place] + mask[n])
            )
        top = jnp.max(
            jnp.maximum(jnp.maximum(parts[0], parts[1]), jnp.maximum(parts[2], parts[3])),
            axis=-1,
            keepdims=True,
        )
        for n in range(4):
            p[rows, n * blk : (n + 1) * blk] = jnp.exp(parts[n] - top).astype(BF16)
    values = v[...]
    out = dot(p[...], jnp.concatenate([values, jnp.ones_like(values)], axis=1))
    inv_all = 1.0 / out[:, LANES:]
    out = out[:, 0:LANES]
    for b in range(count):
        rows = slice(b * blk, (b + 1) * blk)
        inv = jnp.where(
            low_half, inv_all[rows], inv_all[(count + b) * blk : (count + b + 1) * blk]
        )
        inv_out[rows] = inv
        mixed = jnp.where(
            low_half, out[rows], out[(count + b) * blk : (count + b + 1) * blk]
        )
        ctx_out[rows] = (mixed * inv).astype(BF16)


def attend_back(q, k, v, p, do, inv, ctx, count, dq_out, dkt_out, dvt_out):
    blk = q.shape[0] // count
    low_half = iota((blk, LANES), 1) < HALF
    do = by_head(do[...].astype(F32) * inv[...])
    ctx = ctx[...].astype(F32)
    delta = jnp.sum(do * jnp.concatenate([ctx, ctx], axis=0), axis=-1, keepdims=True)
    do = do.astype(BF16)
    dp = dot(do, v[...], 1, 1)
    ds = p[...].astype(F32) * (dp - delta)
    low = ds.astype(BF16)
    dq = dot(low, k[...])
    for b in range(count):
        rows = slice(b * blk, (b + 1) * blk)
        dq_out[rows] = jnp.where(
            low_half, dq[rows], dq[(count + b) * blk : (count + b + 1) * blk]
        ).astype(BF16)
    dkt_out[...] = dot(by_head(q[...]), low, 0, 0).astype(BF16)
    dvt_out[...] = dot(do, p[...], 0, 0).astype(BF16)
    return ds


def main_body(r):
    mp = my_mp()
    w = worked(mp)
    slots = slot_positions(mp)
    blk, width = r.wf.shape
    seq = 4 * blk
    heads = r.table.shape[0]
    pairs = width // LANES
    ffw = r.win.shape[1]
    at = lambda n: slice(n * blk, (n + 1) * blk)
    mover = Mover(r.sems)
    go = lambda pairs_of: [mover.start(src, dst) for src, dst in pairs_of]
    edges = start_edges(r, mover, seq)
    far_rows = go(
        (
            (r.wf, r.rows.at[at(1)]),
            (r.mf, r.rows.at[at(3)]),
            (r.cx, r.rows.at[at(5)]),
            (r.mc, r.rows.at[at(7)]),
        )
    )
    weights_kv = go(((r.wk_hbm, r.wk), (r.wv_hbm, r.wv), (r.wq_hbm, r.wq)))
    toeplitz = mover.start(r.bias_hbm, r.bias)
    shared = go(
        (
            (r.q0.at[at(0)], r.q_s.at[at(0)]),
            (r.k0.at[at(0)], r.k_s.at[at(0)]),
            (r.v0.at[at(0)], r.v_s.at[at(0)]),
            (r.k0.at[at(1)], r.k_s.at[at(2)]),
            (r.v0.at[at(1)], r.v_s.at[at(2)]),
            (r.q0.at[at(1)], r.q_s.at[at(2)]),
            (r.k0.at[at(2)], r.k_s.at[at(4)]),
            (r.v0.at[at(2)], r.v_s.at[at(4)]),
            (r.k0.at[at(3)], r.k_s.at[at(6)]),
            (r.v0.at[at(3)], r.v_s.at[at(6)]),
        )
    )
    gain1 = gain_row(r.gain1)
    gain2 = gain_row(r.gain2)

    for copy in edges:
        copy.wait()
    buckets = bucket_hots(r, seq)
    for n in range(4):
        far_rows[n].wait()
        r.far[at(n)] = normed(r.rows[at(2 * n + 1)], gain1)
    for copy, weight, dst in ((weights_kv[0], r.wk, r.k_s), (weights_kv[1], r.wv, r.v_s)):
        copy.wait()
        every = dot(r.far[...], weight[...]).astype(BF16)
        for n in range(4):
            dst[at(2 * n + 1)] = every[at(n)]
    own_rows = go(((r.x.at[w], r.rows.at[at(0)]), (r.x.at[1], r.rows.at[at(4)])))
    weight_o = mover.start(r.wo_hbm, r.wo)
    weight_in = mover.start(r.win_hbm, r.win)
    weight_out = mover.start(r.wout_hbm, r.wout)
    goals = go(
        (
            (r.t.at[w], r.goal.at[at(0)]),
            (r.tf, r.goal.at[at(1)]),
            (r.t.at[1], r.goal.at[at(2)]),
        )
    )
    late = go(
        (
            (r.m1.at[w], r.rows.at[at(2)]),
            (r.m1.at[1], r.rows.at[at(6)]),
        )
    )
    weights_kv[2].wait()
    r.q_s[at(1)] = dot(r.far[at(0)], r.wq[...]).astype(BF16)
    for copy in shared:
        copy.wait()
    toeplitz.wait()
    masks = [key_masks(slots, r.lengths[n], blk) for n in (w, 1)]
    groups = (
        (slice(0, 2 * blk), (mp, mp ^ 2), slice(0, seq), r.pw_s),
        (at(2), (mp,), slice(seq, 2 * seq), r.pc_s),
    )
    for hp in range(pairs):
        cols = slice(hp * LANES, (hp + 1) * LANES)
        for (q_rows, q_poss, k_rows, p), mask in zip(groups, masks):
            attend(
                hp,
                r.q_s.at[q_rows, cols],
                r.k_s.at[k_rows, cols],
                r.v_s.at[k_rows, cols],
                r.bias,
                mask,
                slots,
                q_poss,
                p.at[hp],
                r.inv_s.at[q_rows, cols],
                r.ctx_s.at[q_rows, cols],
            )

    acc = r.bias
    acc[...] = jnp.zeros_like(acc)

    tokens = 3 * blk
    for copy in own_rows:
        copy.wait()
    own = jnp.concatenate([r.rows[0 : 2 * blk], r.rows[at(4)]], axis=0).astype(F32)
    weight_o.wait()
    residual = own + dot(r.ctx_s[...], r.wo[...])
    r.res[...] = residual
    inv2 = rms(residual)
    r.xn[...] = (residual * inv2 * gain2).astype(BF16)
    weight_in.wait()
    weight_out.wait()
    chunk = 512
    chunks = [slice(n * chunk, (n + 1) * chunk) for n in range(ffw // chunk)]
    pre = dot(r.xn[...], r.win[:, chunks[0]])
    total = None
    for n, cols in enumerate(chunks):
        ahead = dot(r.xn[...], r.win[:, chunks[n + 1]]) if n + 1 < len(chunks) else None
        value, slope = gelu_pair(pre)
        value = value.astype(BF16)
        r.slope[:, cols] = slope.astype(BF16)
        part = dot(value, r.wout[cols, :])
        total = part if total is None else total + part
        pre = ahead
    r.ffn[...] = total.astype(BF16)

    down_low = r.low[0]
    up_low = r.low[1]
    ffn = r.ffn[...]
    activated, act_slope = gelu_pair(dot(ffn, down_low))
    activated = activated.astype(BF16)
    final = r.res[...] + ffn.astype(F32) + dot(activated, up_low, 1, 1)
    r.blk_s[...] = final.astype(BF16)
    out = go(
        (
            (r.blk_s.at[at(1)], r.blk_f),
            (r.blk_s.at[at(0)], r.blk_own.at[0]),
            (r.blk_s.at[at(2)], r.blk_own.at[1]),
        )
    )
    row = iota((blk, 1), 0)
    valid = jnp.concatenate(
        [
            pos * blk + row < length
            for pos, length in ((mp, r.lengths[w]), (mp ^ 2, r.lengths[w]), (mp, r.lengths[1]))
        ],
        axis=0,
    )
    for copy in goals:
        copy.wait()
    err = jnp.where(valid, final - r.goal[...].astype(F32), 0.0)
    r.err[...] = err
    loss = 0.5 * jnp.sum(jnp.sum(err * err, axis=0, keepdims=True), axis=1, keepdims=True)
    g_adapter = err.astype(BF16)
    grad_up = dot(g_adapter, activated, 0, 0)
    g_squeezed = (dot(g_adapter, up_low) * act_slope).astype(BF16)
    grad_down = dot(ffn, g_squeezed, 0, 0)
    kron, block, inner = r.shape_kron
    backs = [
        KronBack(kron, block, inner, r.left[n], r.fac[n], r.right[n]).back(grad, *PACK_KRON[n])
        for n, grad in enumerate((grad_down, grad_up))
    ]
    r.ffn[...] = (err + dot(g_squeezed, down_low, 1, 1)).astype(BF16)

    for n in range(ffw // chunk):
        cols = slice(n * chunk, (n + 1) * chunk)
        r.hid[:, cols] = (dot(r.ffn[...], r.wout[cols, :], 1, 1) * r.slope[:, cols].astype(F32)).astype(
            BF16
        )
    g_normed = jnp.concatenate(
        [dot(r.hid[...], r.win[n * 256 : (n + 1) * 256, :], 1, 1) for n in range(width // 256)],
        axis=1,
    )
    residual = r.res[...]
    inv2 = rms(residual)
    g2 = jnp.sum(g_normed * residual * inv2, axis=0, keepdims=True)
    weighted = g_normed * gain2
    mean = jnp.mean(weighted * residual, axis=-1, keepdims=True)
    g_res = r.err[...] + inv2 * weighted - residual * (inv2 * inv2 * inv2 * mean)
    r.err[...] = g_res
    r.do[...] = dot(g_res.astype(BF16), r.wo[...], 1, 1).astype(BF16)

    for hp in range(pairs):
        cols = slice(hp * LANES, (hp + 1) * LANES)
        scores = []
        for q_rows, q_poss, k_rows, p in groups:
            scores.append(
                attend_back(
                    r.q_s.at[q_rows, cols],
                    r.k_s.at[k_rows, cols],
                    r.v_s.at[k_rows, cols],
                    p.at[hp],
                    r.do.at[q_rows, cols],
                    r.inv_s.at[q_rows, cols],
                    r.ctx_s.at[q_rows, cols],
                    len(q_poss),
                    r.dq.at[q_rows, cols],
                    r.dkt.at[cols, k_rows],
                    r.dvt.at[cols, k_rows],
                )
            )
        for h in range(2):
            near = scores[0][2 * h * blk : (2 * h + 1) * blk] + scores[1][h * blk : (h + 1) * blk]
            far = scores[0][(2 * h + 1) * blk : (2 * h + 2) * blk]
            for piece, q_pos, away in ((near, mp, 1), (far, mp ^ 2, 0)):
                for n in range(4):
                    place = pl.ds(pl.multiple_of((slots[n] - q_pos + 3) * blk, blk), blk)
                    add = piece[:, n * blk : (n + 1) * blk]
                    if n == away:
                        acc[2 * hp + h, 0:8, place] += jnp.sum(
                            add.reshape(blk // 8, 8, blk), axis=0
                        )
                    else:
                        acc[2 * hp + h, :, place] += add

    sub = iota((8, seq), 0)

    def along_diagonals(h):
        total = jnp.zeros((8, seq), F32)
        for g in range(blk // 8):
            near = jnp.concatenate(
                [acc[h, 8 * g : 8 * g + 8, 2 * blk : 5 * blk], jnp.zeros((8, blk), F32)], axis=1
            )
            total = total + pltpu.roll(near, blk - 8 * g, 1)
        for bit in (1, 2, 4):
            total = jnp.where((sub & bit) > 0, pltpu.roll(total, seq - bit, 1), total)
        near = jnp.sum(total, axis=0, keepdims=True)
        below = jnp.sum(acc[h, :, 0 : 2 * blk], axis=0, keepdims=True)
        above = jnp.sum(acc[h, :, 5 * blk : 7 * blk], axis=0, keepdims=True)
        return jnp.concatenate(
            [
                jnp.zeros((1, blk), F32),
                below[:, 0:blk],
                below[:, blk : 2 * blk] + near[:, 0:blk],
                near[:, blk:seq],
                above,
            ],
            axis=1,
        )

    for copy in late:
        copy.wait()
    sums = []
    g1 = jnp.zeros((1, width), F32)
    side = 256
    for first, dq_rows in ((0, slice(0, 2 * blk)), (4, at(2))):
        cols = slice(first * blk, first * blk + seq)
        pieces = []
        dk = r.dkt[:, cols].T
        dv = r.dvt[:, cols].T
        for n in range(width // side):
            outs = slice(n * side, (n + 1) * side)
            piece = dot(dk, r.wk[outs, :], 1, 1)
            if len(sums) < heads:
                sums.append(along_diagonals(len(sums)))
            piece = piece + dot(dv, r.wv[outs, :], 1, 1)
            if len(sums) < heads:
                sums.append(along_diagonals(len(sums)))
            pieces.append(piece)
        parts = jnp.concatenate(pieces, axis=1)
        own = dot(r.dq[dq_rows], r.wq[...], 1, 1)
        for n in range(4):
            part = parts[at(n)]
            if n * blk < own.shape[0]:
                part = part + own[at(n)]
            values = r.rows[at(first + n)].astype(F32)
            inv1 = rms(values)
            scaled = part * values
            g1 = g1 + jnp.sum(scaled * inv1, axis=0, keepdims=True)
            mean = jnp.mean(scaled * gain1, axis=-1, keepdims=True)
            back = inv1 * (part * gain1) - values * (inv1 * inv1 * inv1 * mean)
            if n < 2:
                m = n if first == 0 else 2 + n
                if m < 3:
                    back = back + r.err[at(m)]
                r.base_s[at(m)] = back
                out += go(((r.base_s.at[at(m)], r.base.at[m]),))
            else:
                m = n - 2 if first == 0 else n
                r.send_s[at(m)] = back.astype(BF16)
                out += go(((r.send_s.at[at(m)], r.send.at[m]),))
    for h in range(len(sums), heads):
        sums.append(along_diagonals(h))
    g_table = dot(jnp.concatenate(sums, axis=0), buckets, 1, 1, precision=EXACT)

    (gf_d, g_dr, g_dl), (gf_u, g_ul, g_ur) = backs
    row16 = iota((16, LANES), 0)
    lane16 = iota((16, LANES), 1)
    pack = r.pack
    pack[0:16] = gf_d + gf_u
    pack[0:4] += g_dr + g_ul
    pack[0:heads, 0 : r.table.shape[1]] = g_table
    pack[0:4, HALF:LANES] = g_dl[:, 0:HALF]
    pack[4:8, HALF:LANES] = g_dl[:, HALF : 2 * HALF]
    pack[8:12, HALF:LANES] = g_dl[:, 2 * HALF : 3 * HALF]
    pack[12:16, HALF:LANES] = g_ur[:, 0:HALF]
    pack[16:20] = g_ur[:, HALF : 3 * HALF]
    for n in range(width // LANES):
        pack[20 + n : 21 + n] = g1[:, n * LANES : (n + 1) * LANES]
        pack[26 + n : 27 + n] = g2[:, n * LANES : (n + 1) * LANES]
    real = (r.lengths[0] + r.lengths[1] + r.lengths[2]).astype(F32)
    both = jnp.where(lane16 < 2, loss, real)
    high = both.astype(BF16).astype(F32)
    both = jnp.where(lane16 % 2 == 0, high, both - high)
    r.small[0:16] = jnp.where((row16 == 15) & (lane16 < 4), both, pack[0:16]).astype(BF16)
    r.small[16:32] = pack[16:32].astype(BF16)
    for copy in out:
        copy.wait()


PACK_KRON = ((32, 40), (36, 52))


def middle_body(r):
    mover = Mover(r.sems)
    copies = [
        mover.start(src, dst)
        for src, dst in (
            (r.base.at[1], r.base_s.at[0]),
            (r.recv.at[1], r.recv_s.at[0]),
            (r.base.at[3], r.base_s.at[1]),
            (r.recv.at[3], r.recv_s.at[1]),
        )
    ]
    spread = r.small.shape[0] // 2
    first = pl.multiple_of((my_mp() % 2) * spread, spread)
    half = r.small[pl.ds(first, spread)].astype(F32) + r.others[pl.ds(first, spread)].astype(F32)
    row = iota(half.shape, 0)
    lane = iota(half.shape, 1)
    even = lane % 2 == 0
    whole = half + jnp.where(even, pltpu.roll(half, LANES - 1, 1), pltpu.roll(half, 1, 1))
    high = whole.astype(BF16).astype(F32)
    parted = (row == 15) & (lane < 4) & (my_mp() % 2 == 0)
    half = jnp.where(parted, jnp.where(even, high, whole - high), half).astype(BF16)
    for n in range(r.spread.shape[0]):
        r.spread[n] = half
    for n in range(2):
        copies[2 * n].wait()
        copies[2 * n + 1].wait()
        r.away[n] = (r.base_s[n] + r.recv_s[n].astype(F32)).astype(BF16)


def finish_body(token_total, seq_total, r):
    w = worked(my_mp())
    width = r.grad.shape[2]
    mover = Mover(r.sems)
    copies = [
        mover.start(src, dst)
        for src, dst in (
            (r.gathered, r.gathered_s),
            (r.back.at[0], r.back_s.at[0]),
            (r.back.at[1], r.back_s.at[1]),
            (r.base.at[0], r.base_s.at[0]),
            (r.recv.at[0], r.recv_s.at[0]),
            (r.base.at[2], r.base_s.at[1]),
            (r.recv.at[2], r.recv_s.at[1]),
            (r.blk_f, r.block.at[2 - w]),
            (r.blk_own.at[0], r.block.at[w]),
            (r.blk_own.at[1], r.block.at[1]),
        )
    ]
    copies[0].wait()
    halves = [r.gathered_s[n].astype(F32) for n in range(2)]
    for n in range(2, r.gathered_s.shape[0]):
        halves[n % 2] = halves[n % 2] + r.gathered_s[n].astype(F32)
    total = jnp.concatenate(halves, axis=0)
    tail = total[15:16, 0:4]
    count = (tail[:, 2:3] + tail[:, 3:4]) * 0.25
    scale = token_total / count
    params = [r.dl, r.dr, r.ul, r.ur]
    squares = [jnp.sum(r.fac[n] * r.fac[n], keepdims=True) for n in range(r.fac.shape[0])]
    squares += [jnp.sum(p[...] * p[...], keepdims=True) for p in params]
    penalty = 0.5 * seq_total * sum(squares)
    r.loss[...] = (scale * (tail[:, 0:1] + tail[:, 1:2]) + penalty) / (token_total * width)

    heads, buckets = r.g_table.shape
    r.g_table[...] = scale * total[0:heads, 0:buckets]
    kron = r.fac.shape[0]
    for i in range(kron):
        rows = slice(i * kron, (i + 1) * kron)
        r.g_fac[i] = (
            scale * (total[rows, 32 : 32 + kron] + total[rows, 36 : 36 + kron].T)
            + seq_total * r.fac[i]
        )
    r.g_dr[...] = scale * total[0:4, 40:52] + seq_total * r.dr[...]
    r.g_ul[...] = scale * total[0:4, 52:64] + seq_total * r.ul[...]
    g_dl = jnp.concatenate([total[4 * n : 4 * n + 4, HALF:LANES] for n in range(3)], axis=1)
    r.g_dl[...] = scale * g_dl + seq_total * r.dl[...]
    g_ur = jnp.concatenate([total[12:16, HALF:LANES], total[16:20]], axis=1)
    r.g_ur[...] = scale * g_ur + seq_total * r.ur[...]
    for n in range(width // LANES):
        r.g1[n : n + 1] = scale * total[20 + n : 21 + n]
        r.g2[n : n + 1] = scale * total[26 + n : 27 + n]

    for copy in copies[1:]:
        copy.wait()
    r.grad[2 - w] = scale * r.back_s[0].astype(F32)
    r.grad[w] = scale * (r.base_s[0] + r.recv_s[0].astype(F32))
    r.grad[1] = scale * (r.base_s[1] + r.recv_s[1].astype(F32) + r.back_s[1].astype(F32))


def local(
    layer_input,
    targets,
    attn_gain,
    ffn_gain,
    query_matrix,
    key_matrix,
    value_matrix,
    attention_output_weight,
    feedforward_input_weight,
    feedforward_output_weight,
    bias_table,
    factors,
    down_left,
    down_right,
    up_left,
    up_right,
    lengths,
    relative_bucket,
):
    seqs, blk, width = layer_input.shape
    mp_size = lax.axis_size("mp")
    axes = ("dp", "mp")
    devices = lax.axis_size("dp") * mp_size
    heads = bias_table.shape[1]
    ffw = feedforward_input_weight.shape[1]
    kron = factors.shape[0]
    seq_total = lax.axis_size("dp") * seqs
    token_total = seq_total * blk * mp_size
    assert seqs == 3 and mp_size == 4
    core = [(i, i ^ 1) for i in range(mp_size)]
    chip = [(i, i ^ 2) for i in range(mp_size)]
    pairs = heads // 2
    seq = blk * mp_size
    table = bias_table.T
    square = ((width, width), BF16)
    rows = lambda n, dtype=BF16: ((n * blk, width), dtype)

    picked = call(
        "pick",
        pick_body,
        [("x", layer_input, HBM), ("t", targets, HBM)],
        [(n, (blk, width), BF16, VMEM) for n in ("xf", "xc", "tf")],
        {},
        3,
    )
    wf = lax.ppermute(picked.xf, "mp", chip)
    cx = lax.ppermute(picked.xc, "mp", chip)
    tf = lax.ppermute(picked.tf, "mp", chip)
    m1 = lax.ppermute(layer_input, "mp", core)
    prep = call(
        "prep",
        prep_body,
        [
            ("x", layer_input, HBM),
            ("m1", m1, HBM),
            ("gain1", attn_gain, VMEM),
            ("fac_in", factors, VMEM),
            ("dl", down_left, VMEM),
            ("dr", down_right, VMEM),
            ("ul", up_left, VMEM),
            ("ur", up_right, VMEM),
            ("table", table, VMEM),
            ("bucket", relative_bucket, HBM),
            ("wq_hbm", query_matrix, HBM),
            ("wk_hbm", key_matrix, HBM),
            ("wv_hbm", value_matrix, HBM),
        ],
        [
            ("q",) + rows(2) + (VMEM,),
            ("k",) + rows(4) + (VMEM,),
            ("v",) + rows(4) + (VMEM,),
            ("low", (2, width, LANES), BF16, VMEM),
            ("left", (2, kron * kron, width), F32, VMEM),
            ("fac", (2, kron * kron, LANES), F32, VMEM),
            ("right", (2, kron * kron, LANES), F32, VMEM),
            ("bias", (heads, blk, 7 * blk), F32, VMEM),
        ],
        {"edge": ((2, 8, seq), jnp.int32), "rows": rows(4), "xn": rows(4), "wq": square, "wk": square, "wv": square},
        9,
        4.0,
    )

    wf, cx, prep.k = lax.optimization_barrier((wf, cx, prep.k))
    mf = lax.ppermute(wf, "mp", core)
    mc = lax.ppermute(cx, "mp", core)

    def main_with_shape(r):
        r.shape_kron = (kron, down_left.shape[1], down_right.shape[1])
        main_body(r)

    main = call(
        "main",
        main_with_shape,
        [
            ("lengths", lengths, SMEM),
            ("x", layer_input, HBM),
            ("t", targets, HBM),
            ("wf", wf, HBM),
            ("cx", cx, HBM),
            ("tf", tf, HBM),
            ("m1", m1, HBM),
            ("mf", mf, HBM),
            ("mc", mc, HBM),
            ("gain1", attn_gain, VMEM),
            ("gain2", ffn_gain, VMEM),
            ("table", table, VMEM),
            ("bucket", relative_bucket, HBM),
            ("bias_hbm", prep.bias, HBM),
            ("low", prep.low, VMEM),
            ("left", prep.left, VMEM),
            ("fac", prep.fac, VMEM),
            ("right", prep.right, VMEM),
            ("q0", prep.q, HBM),
            ("k0", prep.k, HBM),
            ("v0", prep.v, HBM),
            ("wq_hbm", query_matrix, HBM),
            ("wk_hbm", key_matrix, HBM),
            ("wv_hbm", value_matrix, HBM),
            ("wo_hbm", attention_output_weight, HBM),
            ("win_hbm", feedforward_input_weight, HBM),
            ("wout_hbm", feedforward_output_weight, HBM),
        ],
        [
            ("blk_own", (2, blk, width), BF16, HBM),
            ("blk_f", (blk, width), BF16, HBM),
            ("base", (4, blk, width), F32, HBM),
            ("send", (4, blk, width), BF16, HBM),
            ("small", (32, LANES), BF16, VMEM),
        ],
        {
            "wq": square,
            "wk": square,
            "wv": square,
            "wo": square,
            "win": ((width, ffw), BF16),
            "wout": ((ffw, width), BF16),
            "edge": ((2, 8, seq), jnp.int32),
            "rows": rows(8),
            "goal": rows(3),
            "xn": rows(3),
            "q_s": rows(3),
            "k_s": rows(8),
            "v_s": rows(8),
            "far": rows(4),
            "bias": ((heads, blk, 7 * blk), F32),
            "pack": ((32, LANES), F32),
            "pw_s": ((pairs, seq, seq), BF16),
            "pc_s": ((pairs, 2 * blk, seq), BF16),
            "ctx_s": rows(3),
            "inv_s": rows(3, F32),
            "res": rows(3, F32),
            "hid": ((3 * blk, ffw), BF16),
            "slope": ((3 * blk, ffw), BF16),
            "ffn": rows(3),
            "err": rows(3, F32),
            "do": rows(3),
            "dq": rows(3),
            "dkt": ((width, 2 * seq), BF16),
            "dvt": ((width, 2 * seq), BF16),
            "blk_s": rows(3),
            "base_s": rows(4, F32),
            "send_s": rows(4),
        },
        45,
        28.0,
    )
    recv = lax.ppermute(main.send, "mp", core)
    others = lax.ppermute(main.small, "mp", core)
    pair = lambda dtype: ((2, blk, width), dtype)
    middle = call(
        "middle",
        middle_body,
        [("base", main.base, HBM), ("recv", recv, HBM), ("small", main.small, VMEM), ("others", others, VMEM)],
        [("away", (2, blk, width), BF16, VMEM), ("spread", (devices, 16, LANES), BF16, VMEM)],
        {"base_s": pair(F32), "recv_s": pair(BF16)},
        4,
    )
    back = lax.ppermute(middle.away, "mp", chip)
    blk_f = lax.ppermute(main.blk_f, "mp", chip)
    spread, blk_f = lax.optimization_barrier((middle.spread, blk_f))
    gathered = lax.all_to_all(spread, axes, split_axis=0, concat_axis=0, tiled=True)

    done = call(
        "finish",
        functools.partial(finish_body, float(token_total), float(seq_total)),
        [
            ("gathered", gathered, HBM),
            ("base", main.base, HBM),
            ("recv", recv, HBM),
            ("back", back, HBM),
            ("blk_own", main.blk_own, HBM),
            ("blk_f", blk_f, HBM),
            ("fac", factors, VMEM),
            ("dl", down_left, VMEM),
            ("dr", down_right, VMEM),
            ("ul", up_left, VMEM),
            ("ur", up_right, VMEM),
        ],
        [
            ("loss", (1, 1), F32, VMEM),
            ("block", (seqs, blk, width), BF16, VMEM),
            ("grad", (seqs, blk, width), F32, VMEM),
            ("g1", (width // LANES, LANES), F32, VMEM),
            ("g2", (width // LANES, LANES), F32, VMEM),
            ("g_table", table.shape, F32, VMEM),
            ("g_fac", factors.shape, F32, VMEM),
            ("g_dl", down_left.shape, F32, VMEM),
            ("g_dr", down_right.shape, F32, VMEM),
            ("g_ul", up_left.shape, F32, VMEM),
            ("g_ur", up_right.shape, F32, VMEM),
        ],
        {
            "gathered_s": ((devices, 16, LANES), BF16),
            "back_s": pair(BF16),
            "base_s": pair(F32),
            "recv_s": pair(BF16),
        },
        10,
    )
    return (
        done.loss.reshape(()),
        done.block,
        done.grad,
        done.g1.reshape(width),
        done.g2.reshape(width),
        done.g_table.T,
        done.g_fac,
        done.g_dl,
        done.g_dr,
        done.g_ul,
        done.g_ur,
    )


def solution(mesh):
    rows = P("dp", "mp", None)
    return jax.shard_map(
        local,
        mesh=mesh,
        in_specs=(rows, rows) + (P(),) * 14 + (P("dp"), P()),
        out_specs=(P(), rows, rows) + (P(),) * 8,
        check_vma=False,
    )
```

```python
import functools
from types import SimpleNamespace

import jax
import jax.numpy as jnp
from jax import lax
from jax.experimental import pallas as pl
from jax.experimental.pallas import tpu as pltpu
from jax.sharding import PartitionSpec as P

EPSILON = 1e-06
F32 = jnp.float32
BF16 = jnp.bfloat16
EXACT = lax.Precision.HIGHEST
GELU_A = 0.7978845608028654
GELU_B = 0.044715
LANES = 128
HALF = LANES // 2
VMEM_BYTES = 64 * 2**20 - 2**12
HBM = pltpu.HBM
VMEM = pltpu.VMEM
SMEM = pltpu.SMEM


def dot(a, b, ca=1, cb=0, precision=None):
    return lax.dot_general(
        a, b, (((ca,), (cb,)), ((), ())), preferred_element_type=F32, precision=precision
    )


def iota(shape, dim):
    return lax.broadcasted_iota(jnp.int32, shape, dim)


def rms(values):
    return lax.rsqrt(jnp.mean(values * values, axis=-1, keepdims=True) + EPSILON)


def gelu_pair(v):
    square = v * v
    w = 1.0 + jnp.tanh(v * (GELU_A + (GELU_A * GELU_B) * square))
    half = 0.5 * v
    slope = w * (0.5 + half * (2.0 - w) * (GELU_A + (3.0 * GELU_A * GELU_B) * square))
    return half * w, slope


def hot(left, right):
    return (left == right).astype(F32)


class Mover:
    def __init__(self, sems):
        self.sems = sems
        self.used = 0

    def start(self, src, dst):
        copy = pltpu.make_async_copy(src, dst, self.sems.at[self.used])
        self.used += 1
        copy.start()
        return copy


def call(name, body, ins, outs, scratch, sems, cost_us=None):
    names = [n for n, _, _ in ins] + [n for n, _, _, _ in outs] + list(scratch) + ["sems"]

    def kernel(*refs):
        body(SimpleNamespace(**dict(zip(names, refs))))

    results = pl.pallas_call(
        kernel,
        out_shape=[jax.ShapeDtypeStruct(shape, dtype) for _, shape, dtype, _ in outs],
        in_specs=[pl.BlockSpec(memory_space=space) for _, _, space in ins],
        out_specs=[pl.BlockSpec(memory_space=space) for _, _, _, space in outs],
        scratch_shapes=[pltpu.VMEM(shape, dtype) for shape, dtype in scratch.values()]
        + [pltpu.SemaphoreType.DMA((max(sems, 1),))],
        compiler_params=pltpu.CompilerParams(vmem_limit_bytes=VMEM_BYTES),
        cost_estimate=None
        if cost_us is None
        else pl.CostEstimate(flops=int(cost_us * 1e9), bytes_accessed=0, transcendentals=0),
        name=name,
    )(*[array for _, array, _ in ins])
    return SimpleNamespace(**dict(zip([o[0] for o in outs], results)))


def factor_rows(fac_ref, transposed):
    kron = fac_ref.shape[0]
    pieces = [fac_ref[i].T if transposed else fac_ref[i] for i in range(kron)]
    return jnp.concatenate(pieces, axis=0)


class Kron:
    def __init__(self, fac_ref, transposed, left_ref, right_ref):
        kron = left_ref.shape[0]
        self.block = left_ref.shape[1]
        self.inner = right_ref.shape[1]
        self.kron = kron
        width = kron * self.block
        rows = kron * kron
        inner = self.inner
        self.expand = hot(iota((rows, kron), 0) // kron, iota((rows, kron), 1))
        take_c = hot(iota((kron, LANES), 0), iota((kron, LANES), 1) // inner)
        lane_d = iota((inner, LANES), 1)
        take_d = jnp.where(
            lane_d < kron * inner, hot(iota((inner, LANES), 0), lane_d % inner), 0.0
        )
        self.same_a = hot(iota((rows, width), 0) % kron, iota((rows, width), 1) // self.block)
        wide_left = jnp.concatenate([left_ref[...]] * kron, axis=1)
        self.left = dot(self.expand, wide_left, precision=EXACT) * self.same_a
        self.fac = dot(factor_rows(fac_ref, transposed), take_c, precision=EXACT)
        self.right = dot(
            self.expand, dot(right_ref[...], take_d, precision=EXACT), precision=EXACT
        )

    def matrix(self):
        return dot(self.left, self.fac * self.right, 0, 0, precision=EXACT)


class KronBack:
    def __init__(self, kron, block, inner, left, fac, right):
        self.kron, self.block, self.inner = kron, block, inner
        self.left, self.fac, self.right = left, fac, right

    def place(self, of_lane, start):
        lane_in = iota((LANES, LANES), 0)
        keep = (lane_in < self.kron * self.inner) & (iota((LANES, LANES), 1) - start == of_lane(lane_in))
        return keep.astype(BF16)

    def back(self, grad, fac_at, right_at):
        grad = grad.astype(BF16)
        rows = self.kron * self.kron
        width = self.kron * self.block
        inner = dot(self.left.astype(BF16), grad)
        g_fac = dot((inner * self.right).astype(BF16), self.place(lambda n: n // self.inner, fac_at))
        expand = (iota((rows, self.kron), 0) // self.kron == iota((rows, self.kron), 1)).astype(BF16)
        same_i = dot(expand, (inner * self.fac).astype(BF16), 0, 0)
        g_right = dot(same_i.astype(BF16), self.place(lambda n: n % self.inner, right_at))
        outer = dot((self.fac * self.right).astype(BF16), grad, 1, 1)
        outer = outer * hot(iota((rows, width), 0) % self.kron, iota((rows, width), 1) // self.block)
        outer = dot(expand, outer.astype(BF16), 0, 0)
        g_left = sum(outer[:, n * self.block : (n + 1) * self.block] for n in range(self.kron))
        return g_fac, g_right, g_left


def my_mp():
    return lax.axis_index("mp")


def worked(mp):
    return jnp.where(mp < 2, 0, 2)


def gain_row(ref):
    return ref[...].astype(F32).reshape(1, ref.shape[0])


def slot_positions(mp):
    return (mp, mp ^ 2, mp ^ 1, mp ^ 3)


def pick_body(r):
    w = worked(my_mp())
    mover = Mover(r.sems)
    copies = [
        mover.start(r.x.at[2 - w], r.xf),
        mover.start(r.x.at[1], r.xc),
        mover.start(r.t.at[2 - w], r.tf),
    ]
    for copy in copies:
        copy.wait()


def normed(rows, gain):
    values = rows.astype(F32)
    return (values * rms(values) * gain).astype(BF16)


def prep_body(r):
    w = worked(my_mp())
    blk = r.x.shape[1]
    mover = Mover(r.sems)
    seq = 4 * blk
    edges = start_edges(r, mover, seq)
    copies = [
        mover.start(src, dst)
        for src, dst in (
            (r.x.at[w], r.rows.at[0:blk]),
            (r.x.at[1], r.rows.at[2 * blk : 3 * blk]),
            (r.m1.at[w], r.rows.at[blk : 2 * blk]),
            (r.m1.at[1], r.rows.at[3 * blk : 4 * blk]),
            (r.wk_hbm, r.wk),
            (r.wv_hbm, r.wv),
            (r.wq_hbm, r.wq),
        )
    ]
    down = Kron(r.fac_in, False, r.dl, r.dr)
    up = Kron(r.fac_in, True, r.ur, r.ul)
    for n, one in enumerate((down, up)):
        r.low[n] = one.matrix().astype(BF16)
        r.left[n] = one.left
        r.fac[n] = one.fac
        r.right[n] = one.right
    for copy in edges:
        copy.wait()
    fill_bias(r, bucket_hots(r, seq), blk)
    gain = gain_row(r.gain1)
    for copy in copies[:4]:
        copy.wait()
    for n in range(4):
        rows = slice(n * blk, (n + 1) * blk)
        r.xn[rows] = normed(r.rows[rows], gain)
    copies[4].wait()
    r.k[...] = dot(r.xn[...], r.wk[...]).astype(BF16)
    copies[5].wait()
    r.v[...] = dot(r.xn[...], r.wv[...]).astype(BF16)
    copies[6].wait()
    r.q[0:blk] = dot(r.xn[0:blk], r.wq[...]).astype(BF16)
    r.q[blk : 2 * blk] = dot(r.xn[2 * blk : 3 * blk], r.wq[...]).astype(BF16)


def start_edges(r, mover, seq):
    return [
        mover.start(r.bucket.at[row : row + 8], r.edge.at[n]) for n, row in enumerate((0, seq - 8))
    ]


def bucket_hots(r, seq):
    by_lane = jnp.concatenate([pltpu.roll(r.edge[1, 7:8, :], 1, 1), r.edge[0, 0:1, :]], axis=1)
    return hot(iota((r.table.shape[1], 2 * seq), 0), by_lane)


def fill_bias(r, buckets, blk):
    span = buckets.shape[1]
    by_distance = dot(r.table[...], buckets, precision=EXACT)
    for h in range(by_distance.shape[0]):
        row = by_distance[h : h + 1]
        near = pltpu.roll(
            jnp.broadcast_to(row[:, 2 * blk : 6 * blk], (blk, span // 2)),
            3 * blk,
            1,
            stride=1,
            stride_axis=0,
        )
        r.bias[h, :, 0 : 2 * blk] = jnp.broadcast_to(row[:, 1:2], (blk, 2 * blk))
        r.bias[h, :, 2 * blk : 5 * blk] = near[:, 0 : 3 * blk]
        r.bias[h, :, 5 * blk : 7 * blk] = jnp.broadcast_to(row[:, span - 1 : span], (blk, 2 * blk))


def key_masks(slots, length, blk):
    lane = iota((1, blk), 1)
    return [jnp.where(s * blk + lane < length, 0.0, -jnp.inf).astype(F32) for s in slots]


def by_head(rows):
    half = iota(rows.shape, 1) < HALF
    zero = jnp.zeros_like(rows)
    return jnp.concatenate([jnp.where(half, rows, zero), jnp.where(half, zero, rows)], axis=0)


def attend(hp, q, k, v, bias, mask, slots, q_poss, p, inv_out, ctx_out):
    count = len(q_poss)
    blk = q.shape[0] // count
    low_half = iota((blk, LANES), 1) < HALF
    scores = dot(by_head(q[...]), k[...], 1, 1)
    step = blk // 2
    for u in range(4 * count):
        h, b = divmod(u // 2, count)
        rows = slice(u * step, (u + 1) * step)
        q_rows = slice((u % 2) * step, (u % 2 + 1) * step)
        parts = []
        for n in range(4):
            place = pl.ds(pl.multiple_of((slots[n] - q_poss[b] + 3) * blk, blk), blk)
            parts.append(
                scores[rows, n * blk : (n + 1) * blk] + (bias[2 * hp + h, q_rows, place] + mask[n])
            )
        top = jnp.max(
            jnp.maximum(jnp.maximum(parts[0], parts[1]), jnp.maximum(parts[2], parts[3])),
            axis=-1,
            keepdims=True,
        )
        for n in range(4):
            p[rows, n * blk : (n + 1) * blk] = jnp.exp(parts[n] - top).astype(BF16)
    values = v[...]
    out = dot(p[...], jnp.concatenate([values, jnp.ones_like(values)], axis=1))
    inv_all = 1.0 / out[:, LANES:]
    out = out[:, 0:LANES]
    for b in range(count):
        rows = slice(b * blk, (b + 1) * blk)
        inv = jnp.where(
            low_half, inv_all[rows], inv_all[(count + b) * blk : (count + b + 1) * blk]
        )
        inv_out[rows] = inv
        mixed = jnp.where(
            low_half, out[rows], out[(count + b) * blk : (count + b + 1) * blk]
        )
        ctx_out[rows] = (mixed * inv).astype(BF16)


def attend_back(q, k, v, p, do, inv, ctx, count, dq_out, dkt_out, dvt_out):
    blk = q.shape[0] // count
    low_half = iota((blk, LANES), 1) < HALF
    do = by_head(do[...].astype(F32) * inv[...])
    ctx = ctx[...].astype(F32)
    delta = jnp.sum(do * jnp.concatenate([ctx, ctx], axis=0), axis=-1, keepdims=True)
    do = do.astype(BF16)
    dp = dot(do, v[...], 1, 1)
    ds = p[...].astype(F32) * (dp - delta)
    low = ds.astype(BF16)
    dq = dot(low, k[...])
    for b in range(count):
        rows = slice(b * blk, (b + 1) * blk)
        dq_out[rows] = jnp.where(
            low_half, dq[rows], dq[(count + b) * blk : (count + b + 1) * blk]
        ).astype(BF16)
    dkt_out[...] = dot(by_head(q[...]), low, 0, 0).astype(BF16)
    dvt_out[...] = dot(do, p[...], 0, 0).astype(BF16)
    return ds


def main_body(r):
    mp = my_mp()
    w = worked(mp)
    slots = slot_positions(mp)
    blk, width = r.wf.shape
    seq = 4 * blk
    heads = r.table.shape[0]
    pairs = width // LANES
    ffw = r.win.shape[1]
    at = lambda n: slice(n * blk, (n + 1) * blk)
    mover = Mover(r.sems)
    go = lambda pairs_of: [mover.start(src, dst) for src, dst in pairs_of]
    edges = start_edges(r, mover, seq)
    far_rows = go(
        (
            (r.wf, r.rows.at[at(1)]),
            (r.mf, r.rows.at[at(3)]),
            (r.cx, r.rows.at[at(5)]),
            (r.mc, r.rows.at[at(7)]),
        )
    )
    weights_kv = go(((r.wk_hbm, r.wk), (r.wv_hbm, r.wv), (r.wq_hbm, r.wq)))
    toeplitz = mover.start(r.bias_hbm, r.bias)
    shared = go(
        (
            (r.q0.at[at(0)], r.q_s.at[at(0)]),
            (r.k0.at[at(0)], r.k_s.at[at(0)]),
            (r.v0.at[at(0)], r.v_s.at[at(0)]),
            (r.k0.at[at(1)], r.k_s.at[at(2)]),
            (r.v0.at[at(1)], r.v_s.at[at(2)]),
            (r.q0.at[at(1)], r.q_s.at[at(2)]),
            (r.k0.at[at(2)], r.k_s.at[at(4)]),
            (r.v0.at[at(2)], r.v_s.at[at(4)]),
            (r.k0.at[at(3)], r.k_s.at[at(6)]),
            (r.v0.at[at(3)], r.v_s.at[at(6)]),
        )
    )
    gain1 = gain_row(r.gain1)
    gain2 = gain_row(r.gain2)

    for copy in edges:
        copy.wait()
    buckets = bucket_hots(r, seq)
    for n in range(4):
        far_rows[n].wait()
        r.far[at(n)] = normed(r.rows[at(2 * n + 1)], gain1)
    for copy, weight, dst in ((weights_kv[0], r.wk, r.k_s), (weights_kv[1], r.wv, r.v_s)):
        copy.wait()
        every = dot(r.far[...], weight[...]).astype(BF16)
        for n in range(4):
            dst[at(2 * n + 1)] = every[at(n)]
    own_rows = go(((r.x.at[w], r.rows.at[at(0)]), (r.x.at[1], r.rows.at[at(4)])))
    weight_o = mover.start(r.wo_hbm, r.wo)
    weight_in = mover.start(r.win_hbm, r.win)
    weight_out = mover.start(r.wout_hbm, r.wout)
    goals = go(
        (
            (r.t.at[w], r.goal.at[at(0)]),
            (r.tf, r.goal.at[at(1)]),
            (r.t.at[1], r.goal.at[at(2)]),
        )
    )
    late = go(
        (
            (r.m1.at[w], r.rows.at[at(2)]),
            (r.m1.at[1], r.rows.at[at(6)]),
        )
    )
    weights_kv[2].wait()
    r.q_s[at(1)] = dot(r.far[at(0)], r.wq[...]).astype(BF16)
    for copy in shared:
        copy.wait()
    toeplitz.wait()
    masks = [key_masks(slots, r.lengths[n], blk) for n in (w, 1)]
    groups = (
        (slice(0, 2 * blk), (mp, mp ^ 2), slice(0, seq), r.pw_s),
        (at(2), (mp,), slice(seq, 2 * seq), r.pc_s),
    )
    for hp in range(pairs):
        cols = slice(hp * LANES, (hp + 1) * LANES)
        for (q_rows, q_poss, k_rows, p), mask in zip(groups, masks):
            attend(
                hp,
                r.q_s.at[q_rows, cols],
                r.k_s.at[k_rows, cols],
                r.v_s.at[k_rows, cols],
                r.bias,
                mask,
                slots,
                q_poss,
                p.at[hp],
                r.inv_s.at[q_rows, cols],
                r.ctx_s.at[q_rows, cols],
            )

    acc = r.bias
    acc[...] = jnp.zeros_like(acc)

    tokens = 3 * blk
    for copy in own_rows:
        copy.wait()
    own = jnp.concatenate([r.rows[0 : 2 * blk], r.rows[at(4)]], axis=0).astype(F32)
    weight_o.wait()
    residual = own + dot(r.ctx_s[...], r.wo[...])
    r.res[...] = residual
    inv2 = rms(residual)
    r.xn[...] = (residual * inv2 * gain2).astype(BF16)
    weight_in.wait()
    weight_out.wait()
    chunk = 512
    chunks = [slice(n * chunk, (n + 1) * chunk) for n in range(ffw // chunk)]
    pre = dot(r.xn[...], r.win[:, chunks[0]])
    total = None
    for n, cols in enumerate(chunks):
        ahead = dot(r.xn[...], r.win[:, chunks[n + 1]]) if n + 1 < len(chunks) else None
        value, slope = gelu_pair(pre)
        value = value.astype(BF16)
        r.slope[:, cols] = slope.astype(BF16)
        part = dot(value, r.wout[cols, :])
        total = part if total is None else total + part
        pre = ahead
    r.ffn[...] = total.astype(BF16)

    down_low = r.low[0]
    up_low = r.low[1]
    ffn = r.ffn[...]
    activated, act_slope = gelu_pair(dot(ffn, down_low))
    activated = activated.astype(BF16)
    final = r.res[...] + ffn.astype(F32) + dot(activated, up_low, 1, 1)
    r.blk_s[...] = final.astype(BF16)
    out = go(
        (
            (r.blk_s.at[at(1)], r.blk_f),
            (r.blk_s.at[at(0)], r.blk_own.at[0]),
            (r.blk_s.at[at(2)], r.blk_own.at[1]),
        )
    )
    row = iota((blk, 1), 0)
    valid = jnp.concatenate(
        [
            pos * blk + row < length
            for pos, length in ((mp, r.lengths[w]), (mp ^ 2, r.lengths[w]), (mp, r.lengths[1]))
        ],
        axis=0,
    )
    for copy in goals:
        copy.wait()
    err = jnp.where(valid, final - r.goal[...].astype(F32), 0.0)
    r.err[...] = err
    loss = 0.5 * jnp.sum(jnp.sum(err * err, axis=0, keepdims=True), axis=1, keepdims=True)
    g_adapter = err.astype(BF16)
    grad_up = dot(g_adapter, activated, 0, 0)
    g_squeezed = (dot(g_adapter, up_low) * act_slope).astype(BF16)
    grad_down = dot(ffn, g_squeezed, 0, 0)
    kron, block, inner = r.shape_kron
    backs = [
        KronBack(kron, block, inner, r.left[n], r.fac[n], r.right[n]).back(grad, *PACK_KRON[n])
        for n, grad in enumerate((grad_down, grad_up))
    ]
    r.ffn[...] = (err + dot(g_squeezed, down_low, 1, 1)).astype(BF16)

    for n in range(ffw // chunk):
        cols = slice(n * chunk, (n + 1) * chunk)
        r.hid[:, cols] = (dot(r.ffn[...], r.wout[cols, :], 1, 1) * r.slope[:, cols].astype(F32)).astype(
            BF16
        )
    g_normed = jnp.concatenate(
        [dot(r.hid[...], r.win[n * 256 : (n + 1) * 256, :], 1, 1) for n in range(width // 256)],
        axis=1,
    )
    residual = r.res[...]
    inv2 = rms(residual)
    g2 = jnp.sum(g_normed * residual * inv2, axis=0, keepdims=True)
    weighted = g_normed * gain2
    mean = jnp.mean(weighted * residual, axis=-1, keepdims=True)
    g_res = r.err[...] + inv2 * weighted - residual * (inv2 * inv2 * inv2 * mean)
    r.err[...] = g_res
    r.do[...] = dot(g_res.astype(BF16), r.wo[...], 1, 1).astype(BF16)

    for hp in range(pairs):
        cols = slice(hp * LANES, (hp + 1) * LANES)
        scores = []
        for q_rows, q_poss, k_rows, p in groups:
            scores.append(
                attend_back(
                    r.q_s.at[q_rows, cols],
                    r.k_s.at[k_rows, cols],
                    r.v_s.at[k_rows, cols],
                    p.at[hp],
                    r.do.at[q_rows, cols],
                    r.inv_s.at[q_rows, cols],
                    r.ctx_s.at[q_rows, cols],
                    len(q_poss),
                    r.dq.at[q_rows, cols],
                    r.dkt.at[cols, k_rows],
                    r.dvt.at[cols, k_rows],
                )
            )
        for h in range(2):
            near = scores[0][2 * h * blk : (2 * h + 1) * blk] + scores[1][h * blk : (h + 1) * blk]
            far = scores[0][(2 * h + 1) * blk : (2 * h + 2) * blk]
            for piece, q_pos, away in ((near, mp, 1), (far, mp ^ 2, 0)):
                for n in range(4):
                    place = pl.ds(pl.multiple_of((slots[n] - q_pos + 3) * blk, blk), blk)
                    add = piece[:, n * blk : (n + 1) * blk]
                    if n == away:
                        acc[2 * hp + h, 0:8, place] += jnp.sum(
                            add.reshape(blk // 8, 8, blk), axis=0
                        )
                    else:
                        acc[2 * hp + h, :, place] += add

    sub = iota((8, seq), 0)

    def along_diagonals(h):
        total = jnp.zeros((8, seq), F32)
        for g in range(blk // 8):
            near = jnp.concatenate(
                [acc[h, 8 * g : 8 * g + 8, 2 * blk : 5 * blk], jnp.zeros((8, blk), F32)], axis=1
            )
            total = total + pltpu.roll(near, blk - 8 * g, 1)
        for bit in (1, 2, 4):
            total = jnp.where((sub & bit) > 0, pltpu.roll(total, seq - bit, 1), total)
        near = jnp.sum(total, axis=0, keepdims=True)
        below = jnp.sum(acc[h, :, 0 : 2 * blk], axis=0, keepdims=True)
        above = jnp.sum(acc[h, :, 5 * blk : 7 * blk], axis=0, keepdims=True)
        return jnp.concatenate(
            [
                jnp.zeros((1, blk), F32),
                below[:, 0:blk],
                below[:, blk : 2 * blk] + near[:, 0:blk],
                near[:, blk:seq],
                above,
            ],
            axis=1,
        )

    for copy in late:
        copy.wait()
    sums = []
    g1 = jnp.zeros((1, width), F32)
    side = 256
    for first, dq_rows in ((0, slice(0, 2 * blk)), (4, at(2))):
        cols = slice(first * blk, first * blk + seq)
        pieces = []
        dk = r.dkt[:, cols].T
        dv = r.dvt[:, cols].T
        for n in range(width // side):
            outs = slice(n * side, (n + 1) * side)
            piece = dot(dk, r.wk[outs, :], 1, 1)
            if len(sums) < heads:
                sums.append(along_diagonals(len(sums)))
            piece = piece + dot(dv, r.wv[outs, :], 1, 1)
            if len(sums) < heads:
                sums.append(along_diagonals(len(sums)))
            pieces.append(piece)
        parts = jnp.concatenate(pieces, axis=1)
        own = dot(r.dq[dq_rows], r.wq[...], 1, 1)
        for n in range(4):
            part = parts[at(n)]
            if n * blk < own.shape[0]:
                part = part + own[at(n)]
            values = r.rows[at(first + n)].astype(F32)
            inv1 = rms(values)
            scaled = part * values
            g1 = g1 + jnp.sum(scaled * inv1, axis=0, keepdims=True)
            mean = jnp.mean(scaled * gain1, axis=-1, keepdims=True)
            back = inv1 * (part * gain1) - values * (inv1 * inv1 * inv1 * mean)
            if n < 2:
                m = n if first == 0 else 2 + n
                if m < 3:
                    back = back + r.err[at(m)]
                r.base_s[at(m)] = back
                out += go(((r.base_s.at[at(m)], r.base.at[m]),))
            else:
                m = n - 2 if first == 0 else n
                r.send_s[at(m)] = back.astype(BF16)
                out += go(((r.send_s.at[at(m)], r.send.at[m]),))
    for h in range(len(sums), heads):
        sums.append(along_diagonals(h))
    g_table = dot(jnp.concatenate(sums, axis=0), buckets, 1, 1, precision=EXACT)

    (gf_d, g_dr, g_dl), (gf_u, g_ul, g_ur) = backs
    row16 = iota((16, LANES), 0)
    lane16 = iota((16, LANES), 1)
    pack = r.pack
    pack[0:16] = gf_d + gf_u
    pack[0:4] += g_dr + g_ul
    pack[0:heads, 0 : r.table.shape[1]] = g_table
    pack[0:4, HALF:LANES] = g_dl[:, 0:HALF]
    pack[4:8, HALF:LANES] = g_dl[:, HALF : 2 * HALF]
    pack[8:12, HALF:LANES] = g_dl[:, 2 * HALF : 3 * HALF]
    pack[12:16, HALF:LANES] = g_ur[:, 0:HALF]
    pack[16:20] = g_ur[:, HALF : 3 * HALF]
    for n in range(width // LANES):
        pack[20 + n : 21 + n] = g1[:, n * LANES : (n + 1) * LANES]
        pack[26 + n : 27 + n] = g2[:, n * LANES : (n + 1) * LANES]
    real = (r.lengths[0] + r.lengths[1] + r.lengths[2]).astype(F32)
    both = jnp.where(lane16 < 2, loss, real)
    high = both.astype(BF16).astype(F32)
    both = jnp.where(lane16 % 2 == 0, high, both - high)
    r.small[0:16] = jnp.where((row16 == 15) & (lane16 < 4), both, pack[0:16]).astype(BF16)
    r.small[16:32] = pack[16:32].astype(BF16)
    for copy in out:
        copy.wait()


PACK_KRON = ((32, 40), (36, 52))


def middle_body(r):
    mover = Mover(r.sems)
    copies = [
        mover.start(src, dst)
        for src, dst in (
            (r.base.at[1], r.base_s.at[0]),
            (r.recv.at[1], r.recv_s.at[0]),
            (r.base.at[3], r.base_s.at[1]),
            (r.recv.at[3], r.recv_s.at[1]),
        )
    ]
    spread = r.small.shape[0] // 2
    first = pl.multiple_of((my_mp() % 2) * spread, spread)
    half = r.small[pl.ds(first, spread)].astype(F32) + r.others[pl.ds(first, spread)].astype(F32)
    row = iota(half.shape, 0)
    lane = iota(half.shape, 1)
    even = lane % 2 == 0
    whole = half + jnp.where(even, pltpu.roll(half, LANES - 1, 1), pltpu.roll(half, 1, 1))
    high = whole.astype(BF16).astype(F32)
    parted = (row == 15) & (lane < 4) & (my_mp() % 2 == 0)
    half = jnp.where(parted, jnp.where(even, high, whole - high), half).astype(BF16)
    for n in range(r.spread.shape[0]):
        r.spread[n] = half
    for n in range(2):
        copies[2 * n].wait()
        copies[2 * n + 1].wait()
        r.away[n] = (r.base_s[n] + r.recv_s[n].astype(F32)).astype(BF16)


def finish_body(token_total, seq_total, r):
    w = worked(my_mp())
    width = r.grad.shape[2]
    mover = Mover(r.sems)
    copies = [
        mover.start(src, dst)
        for src, dst in (
            (r.gathered, r.gathered_s),
            (r.back.at[0], r.back_s.at[0]),
            (r.back.at[1], r.back_s.at[1]),
            (r.base.at[0], r.base_s.at[0]),
            (r.recv.at[0], r.recv_s.at[0]),
            (r.base.at[2], r.base_s.at[1]),
            (r.recv.at[2], r.recv_s.at[1]),
            (r.blk_f, r.block.at[2 - w]),
            (r.blk_own.at[0], r.block.at[w]),
            (r.blk_own.at[1], r.block.at[1]),
        )
    ]
    copies[0].wait()
    halves = [r.gathered_s[n].astype(F32) for n in range(2)]
    for n in range(2, r.gathered_s.shape[0]):
        halves[n % 2] = halves[n % 2] + r.gathered_s[n].astype(F32)
    total = jnp.concatenate(halves, axis=0)
    tail = total[15:16, 0:4]
    count = (tail[:, 2:3] + tail[:, 3:4]) * 0.25
    scale = token_total / count
    params = [r.dl, r.dr, r.ul, r.ur]
    squares = [jnp.sum(r.fac[n] * r.fac[n], keepdims=True) for n in range(r.fac.shape[0])]
    squares += [jnp.sum(p[...] * p[...], keepdims=True) for p in params]
    penalty = 0.5 * seq_total * sum(squares)
    r.loss[...] = (scale * (tail[:, 0:1] + tail[:, 1:2]) + penalty) / (token_total * width)

    heads, buckets = r.g_table.shape
    r.g_table[...] = scale * total[0:heads, 0:buckets]
    kron = r.fac.shape[0]
    for i in range(kron):
        rows = slice(i * kron, (i + 1) * kron)
        r.g_fac[i] = (
            scale * (total[rows, 32 : 32 + kron] + total[rows, 36 : 36 + kron].T)
            + seq_total * r.fac[i]
        )
    r.g_dr[...] = scale * total[0:4, 40:52] + seq_total * r.dr[...]
    r.g_ul[...] = scale * total[0:4, 52:64] + seq_total * r.ul[...]
    g_dl = jnp.concatenate([total[4 * n : 4 * n + 4, HALF:LANES] for n in range(3)], axis=1)
    r.g_dl[...] = scale * g_dl + seq_total * r.dl[...]
    g_ur = jnp.concatenate([total[12:16, HALF:LANES], total[16:20]], axis=1)
    r.g_ur[...] = scale * g_ur + seq_total * r.ur[...]
    for n in range(width // LANES):
        r.g1[n : n + 1] = scale * total[20 + n : 21 + n]
        r.g2[n : n + 1] = scale * total[26 + n : 27 + n]

    for copy in copies[1:]:
        copy.wait()
    r.grad[2 - w] = scale * r.back_s[0].astype(F32)
    r.grad[w] = scale * (r.base_s[0] + r.recv_s[0].astype(F32))
    r.grad[1] = scale * (r.base_s[1] + r.recv_s[1].astype(F32) + r.back_s[1].astype(F32))


def local(
    layer_input,
    targets,
    attn_gain,
    ffn_gain,
    query_matrix,
    key_matrix,
    value_matrix,
    attention_output_weight,
    feedforward_input_weight,
    feedforward_output_weight,
    bias_table,
    factors,
    down_left,
    down_right,
    up_left,
    up_right,
    lengths,
    relative_bucket,
):
    seqs, blk, width = layer_input.shape
    mp_size = lax.axis_size("mp")
    axes = ("dp", "mp")
    devices = lax.axis_size("dp") * mp_size
    heads = bias_table.shape[1]
    ffw = feedforward_input_weight.shape[1]
    kron = factors.shape[0]
    seq_total = lax.axis_size("dp") * seqs
    token_total = seq_total * blk * mp_size
    assert seqs == 3 and mp_size == 4
    core = [(i, i ^ 1) for i in range(mp_size)]
    chip = [(i, i ^ 2) for i in range(mp_size)]
    pairs = heads // 2
    seq = blk * mp_size
    table = bias_table.T
    square = ((width, width), BF16)
    rows = lambda n, dtype=BF16: ((n * blk, width), dtype)

    picked = call(
        "pick",
        pick_body,
        [("x", layer_input, HBM), ("t", targets, HBM)],
        [(n, (blk, width), BF16, VMEM) for n in ("xf", "xc", "tf")],
        {},
        3,
    )
    wf = lax.ppermute(picked.xf, "mp", chip)
    cx = lax.ppermute(picked.xc, "mp", chip)
    tf = lax.ppermute(picked.tf, "mp", chip)
    m1 = lax.ppermute(layer_input, "mp", core)
    prep = call(
        "prep",
        prep_body,
        [
            ("x", layer_input, HBM),
            ("m1", m1, HBM),
            ("gain1", attn_gain, VMEM),
            ("fac_in", factors, VMEM),
            ("dl", down_left, VMEM),
            ("dr", down_right, VMEM),
            ("ul", up_left, VMEM),
            ("ur", up_right, VMEM),
            ("table", table, VMEM),
            ("bucket", relative_bucket, HBM),
            ("wq_hbm", query_matrix, HBM),
            ("wk_hbm", key_matrix, HBM),
            ("wv_hbm", value_matrix, HBM),
        ],
        [
            ("q",) + rows(2) + (VMEM,),
            ("k",) + rows(4) + (VMEM,),
            ("v",) + rows(4) + (VMEM,),
            ("low", (2, width, LANES), BF16, VMEM),
            ("left", (2, kron * kron, width), F32, VMEM),
            ("fac", (2, kron * kron, LANES), F32, VMEM),
            ("right", (2, kron * kron, LANES), F32, VMEM),
            ("bias", (heads, blk, 7 * blk), F32, VMEM),
        ],
        {"edge": ((2, 8, seq), jnp.int32), "rows": rows(4), "xn": rows(4), "wq": square, "wk": square, "wv": square},
        9,
        4.0,
    )

    wf, cx, prep.k = lax.optimization_barrier((wf, cx, prep.k))
    mf = lax.ppermute(wf, "mp", core)
    mc = lax.ppermute(cx, "mp", core)

    def main_with_shape(r):
        r.shape_kron = (kron, down_left.shape[1], down_right.shape[1])
        main_body(r)

    main = call(
        "main",
        main_with_shape,
        [
            ("lengths", lengths, SMEM),
            ("x", layer_input, HBM),
            ("t", targets, HBM),
            ("wf", wf, HBM),
            ("cx", cx, HBM),
            ("tf", tf, HBM),
            ("m1", m1, HBM),
            ("mf", mf, HBM),
            ("mc", mc, HBM),
            ("gain1", attn_gain, VMEM),
            ("gain2", ffn_gain, VMEM),
            ("table", table, VMEM),
            ("bucket", relative_bucket, HBM),
            ("bias_hbm", prep.bias, HBM),
            ("low", prep.low, VMEM),
            ("left", prep.left, VMEM),
            ("fac", prep.fac, VMEM),
            ("right", prep.right, VMEM),
            ("q0", prep.q, HBM),
            ("k0", prep.k, HBM),
            ("v0", prep.v, HBM),
            ("wq_hbm", query_matrix, HBM),
            ("wk_hbm", key_matrix, HBM),
            ("wv_hbm", value_matrix, HBM),
            ("wo_hbm", attention_output_weight, HBM),
            ("win_hbm", feedforward_input_weight, HBM),
            ("wout_hbm", feedforward_output_weight, HBM),
        ],
        [
            ("blk_own", (2, blk, width), BF16, HBM),
            ("blk_f", (blk, width), BF16, HBM),
            ("base", (4, blk, width), F32, HBM),
            ("send", (4, blk, width), BF16, HBM),
            ("small", (32, LANES), BF16, VMEM),
        ],
        {
            "wq": square,
            "wk": square,
            "wv": square,
            "wo": square,
            "win": ((width, ffw), BF16),
            "wout": ((ffw, width), BF16),
            "edge": ((2, 8, seq), jnp.int32),
            "rows": rows(8),
            "goal": rows(3),
            "xn": rows(3),
            "q_s": rows(3),
            "k_s": rows(8),
            "v_s": rows(8),
            "far": rows(4),
            "bias": ((heads, blk, 7 * blk), F32),
            "pack": ((32, LANES), F32),
            "pw_s": ((pairs, seq, seq), BF16),
            "pc_s": ((pairs, 2 * blk, seq), BF16),
            "ctx_s": rows(3),
            "inv_s": rows(3, F32),
            "res": rows(3, F32),
            "hid": ((3 * blk, ffw), BF16),
            "slope": ((3 * blk, ffw), BF16),
            "ffn": rows(3),
            "err": rows(3, F32),
            "do": rows(3),
            "dq": rows(3),
            "dkt": ((width, 2 * seq), BF16),
            "dvt": ((width, 2 * seq), BF16),
            "blk_s": rows(3),
            "base_s": rows(4, F32),
            "send_s": rows(4),
        },
        45,
        28.0,
    )
    recv = lax.ppermute(main.send, "mp", core)
    others = lax.ppermute(main.small, "mp", core)
    pair = lambda dtype: ((2, blk, width), dtype)
    middle = call(
        "middle",
        middle_body,
        [("base", main.base, HBM), ("recv", recv, HBM), ("small", main.small, VMEM), ("others", others, VMEM)],
        [("away", (2, blk, width), BF16, VMEM), ("spread", (devices, 16, LANES), BF16, VMEM)],
        {"base_s": pair(F32), "recv_s": pair(BF16)},
        4,
    )
    back = lax.ppermute(middle.away, "mp", chip)
    blk_f = lax.ppermute(main.blk_f, "mp", chip)
    spread, blk_f = lax.optimization_barrier((middle.spread, blk_f))
    gathered = lax.all_to_all(spread, axes, split_axis=0, concat_axis=0, tiled=True)

    done = call(
        "finish",
        functools.partial(finish_body, float(token_total), float(seq_total)),
        [
            ("gathered", gathered, HBM),
            ("base", main.base, HBM),
            ("recv", recv, HBM),
            ("back", back, HBM),
            ("blk_own", main.blk_own, HBM),
            ("blk_f", blk_f, HBM),
            ("fac", factors, VMEM),
            ("dl", down_left, VMEM),
            ("dr", down_right, VMEM),
            ("ul", up_left, VMEM),
            ("ur", up_right, VMEM),
        ],
        [
            ("loss", (1, 1), F32, VMEM),
            ("block", (seqs, blk, width), BF16, VMEM),
            ("grad", (seqs, blk, width), F32, VMEM),
            ("g1", (width // LANES, LANES), F32, VMEM),
            ("g2", (width // LANES, LANES), F32, VMEM),
            ("g_table", table.shape, F32, VMEM),
            ("g_fac", factors.shape, F32, VMEM),
            ("g_dl", down_left.shape, F32, VMEM),
            ("g_dr", down_right.shape, F32, VMEM),
            ("g_ul", up_left.shape, F32, VMEM),
            ("g_ur", up_right.shape, F32, VMEM),
        ],
        {
            "gathered_s": ((devices, 16, LANES), BF16),
            "back_s": pair(BF16),
            "base_s": pair(F32),
            "recv_s": pair(BF16),
        },
        10,
    )
    return (
        done.loss.reshape(()),
        done.block,
        done.grad,
        done.g1.reshape(width),
        done.g2.reshape(width),
        done.g_table.T,
        done.g_fac,
        done.g_dl,
        done.g_dr,
        done.g_ul,
        done.g_ur,
    )


def solution(mesh):
    rows = P("dp", "mp", None)
    return jax.shard_map(
        local,
        mesh=mesh,
        in_specs=(rows, rows) + (P(),) * 14 + (P("dp"), P()),
        out_specs=(P(), rows, rows) + (P(),) * 8,
        check_vma=False,
    )
```
